256 devices in a mesh: gx: 16 (over y, x), gy: 16 (over z, core).
Axes of the slice: x: 4, y: 4, z: 8, core: 2. Of those that a mesh axis runs over, the one named last changes fastest.
Arguments:
- field: float32 [4, 768, 768, 32], P(None, 'gx', 'gy'), may hold values from -6 to 6
- w_coarse: float32 [32, 32], replicated, may hold values from -1 to 1
- w_detail: float32 [32, 32], replicated, may hold values from -1 to 1
- w_skip: float32 [32, 32], replicated, may hold values from -1 to 1
- cotangent: float32 [4, 768, 768, 32], P(None, 'gx', 'gy'), may hold values from -6 to 6
Outputs:
- grad_field: float32 [4, 768, 768, 32], P(None, 'gx', 'gy')
- grad_coarse: float32 [32, 32], replicated
- grad_detail: float32 [32, 32], replicated
- grad_skip: float32 [32, 32], replicated
The draws below stay inside these ranges and needn't reach their ends.
All inputs are finite; a program needn't handle non-finite values.
Results may differ from the reference program's by a relative error of at most 0.00005.
Values sent between devices are 32-bit elements; how exact they have to be, the bound alone decides.
A program may use at most 128 MiB of HBM per device.

```python
import jax
import jax.numpy as jnp
from jax import lax

CH = 32
BATCH = 4
NX = 768
NY = 768
COUNT = 2359296


def shared_field(key):
    return jax.random.normal(key, (BATCH, NX, NY, CH), jnp.float32)


def own_noise(key):
    return jax.random.normal(key, (BATCH, NX, NY, CH), jnp.float32)


def draw_field(key, part):
    base = shared_field(key)
    key = jax.random.fold_in(key, 11)
    return jnp.clip(0.8 * base + 0.6 * own_noise(key), -6.0, 6.0)


def draw_cotangent(key, part):
    base = shared_field(key)
    key = jax.random.fold_in(key, 23)
    ramp = 0.5 + jnp.arange(NX, dtype=jnp.float32) / NX
    values = (0.7 * base + 0.7 * own_noise(key)) * ramp[None, :, None, None]
    return jnp.clip(values, -6.0, 6.0)


def centred(own_key, shape, scale, reach, held_as=jnp.bfloat16):
    return jnp.clip(scale * jax.random.normal(own_key, shape, jnp.float32), -reach, reach).astype(held_as)


def setup_inputs(seed: int = 0) -> dict:
    splits = jax.random.split(jax.random.key(seed), 6)
    return {
        "field": draw_field(jax.random.fold_in(splits[5], 71), 0),
        "w_coarse": centred(splits[1], (CH, CH), CH ** -0.5, 1.0, jnp.float32),
        "w_detail": centred(splits[2], (CH, CH), CH ** -0.5, 1.0, jnp.float32),
        "w_skip": centred(splits[3], (CH, CH), CH ** -0.5, 1.0, jnp.float32),
        "cotangent": draw_cotangent(jax.random.fold_in(splits[5], 71), 0),
    }


LOW_TAPS = [0.23037781330885523, 0.7148465705525415, 0.6308807679295904, -0.02798376941698385, -0.18703481171888114, 0.030841381835986965, 0.032883011666982945, -0.010597401784997278]
HIGH_TAPS = [(-1) ** offset * LOW_TAPS[7 - offset] for offset in range(8)]

def analyze(values, axis, bank):
    length = values.shape[axis]
    extended = jnp.concatenate([values, lax.slice_in_dim(values, 0, 6, axis=axis)], axis=axis)
    outputs = []
    for taps in bank:
        total = 0.0
        for offset in range(8):
            total = total + taps[offset] * lax.slice_in_dim(extended, offset, offset + length - 1, 2, axis)
        outputs.append(total)
    return jnp.concatenate(outputs, axis=0)

def pad_axis(values, axis, before, after):
    widths = [(0, 0)] * values.ndim
    widths[axis] = (before, after)
    return jnp.pad(values, widths)

def upsample(values, axis):
    stacked = jnp.stack([values, jnp.zeros_like(values)], axis=axis + 1)
    shape = list(values.shape)
    shape[axis] = shape[axis] * 2
    return stacked.reshape(shape)

def synthesize(values, axis, bank):
    groups = len(bank)
    per_group = values.shape[0] // groups
    length = values.shape[axis] * 2
    total = 0.0
    for index in range(groups):
        spread = upsample(values[index * per_group:(index + 1) * per_group], axis)
        for offset in range(8):
            total = total + bank[index][offset] * pad_axis(spread, axis, offset, 7 - offset)
    head = lax.slice_in_dim(total, 0, length, axis=axis)
    tail = lax.slice_in_dim(total, length, length + 7, axis=axis)
    return head + pad_axis(tail, axis, 0, length - 7)

def forward_transform(values):
    stack = values[None]
    for level in range(2):
        stack = analyze(analyze(stack, 2, [LOW_TAPS]), 3, [LOW_TAPS])
    return analyze(analyze(stack, 2, [LOW_TAPS, HIGH_TAPS]), 3, [LOW_TAPS, HIGH_TAPS])

def inverse_transform(bands):
    stack = synthesize(synthesize(bands, 3, [LOW_TAPS, HIGH_TAPS]), 2, [LOW_TAPS, HIGH_TAPS])
    for level in range(2):
        stack = synthesize(synthesize(stack, 3, [LOW_TAPS]), 2, [LOW_TAPS])
    return stack[0]

def mix(values, weight):
    return jnp.einsum('...c,cd->...d', values, weight, precision=lax.Precision.HIGHEST)

def layer(field, w_coarse, w_detail, w_skip):
    coeffs = forward_transform(field)
    mixed = jnp.concatenate([mix(coeffs[:1], w_coarse), mix(coeffs[1:], w_detail)], axis=0)
    pre = inverse_transform(mixed) + mix(field, w_skip)
    return jax.nn.gelu(pre)

def reference(field, w_coarse, w_detail, w_skip, cotangent):
    output, backward = jax.vjp(layer, field, w_coarse, w_detail, w_skip)
    grad_field, grad_coarse, grad_detail, grad_skip = backward(cotangent)
    scale = 1.0 / COUNT
    return (grad_field, grad_coarse * scale, grad_detail * scale, grad_skip * scale)
```

```python
import functools

import jax
import jax.numpy as jnp
import numpy as np
from jax import lax
from jax.experimental import pallas as pl
from jax.experimental.pallas import tpu as pltpu
from jax.sharding import PartitionSpec as P

LOW_TAPS = [
    0.23037781330885523,
    0.7148465705525415,
    0.6308807679295904,
    -0.02798376941698385,
    -0.18703481171888114,
    0.030841381835986965,
    0.032883011666982945,
    -0.010597401784997278,
]
HIGH_TAPS = [(-1) ** offset * LOW_TAPS[7 - offset] for offset in range(8)]

F32 = jnp.float32
BF16 = jnp.bfloat16
MESH = pl.DeviceIdType.MESH
CH = 32
BATCH = 4
CELLS = 48
COARSE = 6
ROWS = COARSE * CH
GELU_A = 0.7978845608028654
GELU_B = GELU_A * 0.044715


def bounds(low, high):
    return -((7 - low) // 2), high // 2


LEVELS = [(0, CELLS - 1)]
for _ in range(3):
    LEVELS.append(bounds(*LEVELS[-1]))


def line_matrix():
    values = np.eye(CELLS)
    low, high = LEVELS[0]
    outputs = []
    for level in range(3):
        bank = [LOW_TAPS] if level < 2 else [LOW_TAPS, HIGH_TAPS]
        first, last = LEVELS[level + 1]
        outputs = []
        for taps in bank:
            result = np.zeros((last - first + 1, CELLS))
            for k in range(first, last + 1):
                for j in range(8):
                    if low <= 2 * k + j <= high:
                        result[k - first] += taps[j] * values[2 * k + j - low]
            outputs.append(result)
        values, low, high = outputs[0], first, last
    return np.stack(outputs)


def bank_matrix():
    line = line_matrix()
    result = np.zeros((2, BATCH, 64, 2, 2, 2, 32))
    for xband in range(2):
        for b in range(BATCH):
            for part in range(2):
                for yband in range(2):
                    for k in range(COARSE):
                        result[xband, b, :CELLS, part, xband, yband, k * BATCH + b] = line[yband, part * COARSE + k]
    return result.reshape(512, 256).astype(np.float32)


def split(values):
    high = values.astype(BF16)
    return high, (values - high.astype(F32)).astype(BF16)


def dot3(left, right, dims=((1,), (0,))):
    form = (dims, ((), ()))
    total = lax.dot_general(left[0], right[0], form, preferred_element_type=F32)
    total += lax.dot_general(left[1], right[0], form, preferred_element_type=F32)
    return total + lax.dot_general(left[0], right[1], form, preferred_element_type=F32)


NT = ((1,), (1,))


class Analysis:
    def __init__(self, load):
        self.load = load
        self.memo = {}

    def get(self, level, k, taps=LOW_TAPS, band=0):
        if level == 0:
            if (0, k) not in self.memo:
                self.memo[0, k] = self.load(k)
            return self.memo[0, k]
        key = (level, k, band)
        if key not in self.memo:
            low, high = LEVELS[level - 1]
            total = None
            for j in range(8):
                if low <= 2 * k + j <= high:
                    term = self.get(level - 1, 2 * k + j) * F32(taps[j])
                    total = term if total is None else total + term
            self.memo[key] = total
        return self.memo[key]


class Synthesis:
    def __init__(self, load):
        self.load = load
        self.memo = {}

    def top(self, band, k):
        if (band, k) not in self.memo:
            self.memo[band, k] = self.load(band, k)
        return self.memo[band, k]

    def get(self, level, i):
        key = (level, i, "s")
        if key not in self.memo:
            low, high = LEVELS[level + 1]
            total = None
            for k in range(low, high + 1):
                j = i - 2 * k
                if 0 <= j < 8:
                    if level == 2:
                        term = self.top(0, k) * F32(LOW_TAPS[j]) + self.top(1, k) * F32(HIGH_TAPS[j])
                    else:
                        term = self.get(level + 1, k) * F32(LOW_TAPS[j])
                    total = term if total is None else total + term
            self.memo[key] = total
        return self.memo[key]


def kernel(
    nx, ny, field_hbm, cot_hbm, wc_ref, wd_ref, ws_ref, bh_ref, bl_ref,
    out_hbm, gc_ref, gd_ref, gs_ref,
    raw, raw_cot, field, cot, grad, mixed_skip, lines, kron, out,
    send_fwd, send_mix, recv, coeffs, wide, ar_out, ar_in, ar_part, gsum,
    in_sems, out_sems, ex_send, ex_recv, ar_send, ar_recv,
):
    gx = lax.axis_index("gx")
    gy = lax.axis_index("gy")
    right, left = lax.rem(gx + 1, nx), lax.rem(gx + nx - 1, nx)
    up, down = lax.rem(gy + 1, ny), lax.rem(gy + ny - 1, ny)

    loads = []
    for half in range(2):
        part = pl.ds(2 * half, 2)
        loads.append(pltpu.make_async_copy(field_hbm.at[part], raw.at[part], in_sems.at[half]))
    loads.append(pltpu.make_async_copy(cot_hbm, raw_cot, in_sems.at[2]))
    for load in loads:
        load.start()

    barrier = pltpu.get_barrier_semaphore()

    def greet_y(r, carry):
        pl.semaphore_signal(barrier, inc=1, device_id=(gx, lax.rem(gy + r, ny)), device_id_type=MESH)
        return carry

    def greet_x(r, carry):
        pl.semaphore_signal(barrier, inc=1, device_id=(lax.rem(gx + r, nx), gy), device_id_type=MESH)
        return carry

    lax.fori_loop(1, nx, greet_x, 0)
    lax.fori_loop(1, ny, greet_y, 0)
    pl.semaphore_signal(barrier, inc=1, device_id=(right, up), device_id_type=MESH)
    pl.semaphore_signal(barrier, inc=1, device_id=(left, down), device_id_type=MESH)

    bank = (bh_ref[...], bl_ref[...])

    def pack(source, target, half):
        columns = 128 * half
        target[:, columns : columns + 128] = jnp.zeros((CELLS * CH, 128), F32)
        for pair in range(2):
            values = source[2 * half + pair].reshape(CELLS * CH, CELLS)
            start = columns + 64 * pair
            target[:, start : start + CELLS] = values

    def column(index):
        rows = pl.multiple_of(lax.rem(index, 4) * 8, 8)
        lanes = pl.multiple_of(lax.div(index, 4) * 128, 128)
        return rows, lanes

    def analyze_column(load, rows, lanes):
        walk = Analysis(load)
        for k in range(2 * COARSE):
            for band, taps in enumerate((LOW_TAPS, HIGH_TAPS)):
                value = walk.get(3, k - COARSE, taps, band)
                lines[pl.ds(pl.multiple_of(k * CH + rows, 8), 8), pl.ds(pl.multiple_of(band * 256 + lanes, 128), 128)] = value

    def synthesis_column(rows, lanes):
        def load(band, k):
            return lines[
                pl.ds(pl.multiple_of((k + COARSE) * CH + rows, 8), 8),
                pl.ds(pl.multiple_of(band * 256 + lanes, 128), 128),
            ]

        return Synthesis(load)

    def exchange(step, sources, devices):
        copies = []
        for slot, (source, device) in enumerate(zip(sources, devices)):
            copy = pltpu.make_async_remote_copy(
                src_ref=source,
                dst_ref=recv.at[step, slot],
                send_sem=ex_send.at[step, slot],
                recv_sem=ex_recv.at[step, slot],
                device_id=device,
                device_id_type=MESH,
            )
            copy.start()
            copies.append(copy)
        return copies

    back_devices = [(left, gy), (gx, down), (left, down)]
    next_devices = [(right, gy), (gx, up), (right, up)]

    def send_partials(step):
        parts = dot3(split(lines[...]), bank)
        send_fwd[step // 2, 0] = parts[:ROWS, 128:]
        send_fwd[step // 2, 1] = parts[ROWS:, :128]
        send_fwd[step // 2, 2] = parts[:ROWS, :128]
        return parts[ROWS:, 128:], exchange(step, [send_fwd.at[step // 2, s] for s in range(3)], back_devices)

    def gather_sum(step, own, copies):
        total = own
        for slot, copy in enumerate(copies):
            copy.wait_recv()
            total = total + recv[step, slot]
        return total

    def side_by_side(values):
        return jnp.concatenate([values[k * CH : (k + 1) * CH] for k in range(COARSE)], axis=1)

    coarse_lanes = lax.broadcasted_iota(jnp.int32, (CH, 128), 1) < 32

    def mix(values, weights):
        both = dot3(weights, split(side_by_side(values)))
        chosen = [
            jnp.where(coarse_lanes, both[:CH, k * 128 : (k + 1) * 128], both[CH:, k * 128 : (k + 1) * 128])
            for k in range(COARSE)
        ]
        return jnp.concatenate(chosen, axis=0)

    def send_mixed(step, values):
        send_mix[step // 2] = values
        return exchange(step, [send_mix.at[step // 2]] * 3, next_devices)

    def synthesize_lines(step, copies):
        for copy in copies:
            copy.wait_recv()
        wide[:ROWS, :128] = recv[step, 2]
        wide[:ROWS, 128:] = recv[step, 0]
        wide[ROWS:, :128] = recv[step, 1]
        wide[ROWS:, 128:] = send_mix[step // 2]
        lines[...] = dot3(split(wide[...]), bank, NT)

    for half in range(2):
        loads[half].wait()
        pack(raw, field, half)

    def first_column(index, carry):
        rows, lanes = column(index)
        analyze_column(
            lambda x: field[pl.ds(pl.multiple_of(x * CH + rows, 8), 8), pl.ds(lanes, 128)], rows, lanes
        )
        return carry

    lax.fori_loop(0, 8, first_column, 0)
    pl.semaphore_wait(barrier, nx + ny)
    own, copies1 = send_partials(0)

    eye = (
        lax.broadcasted_iota(jnp.int32, (CH, CH), 0) == lax.broadcasted_iota(jnp.int32, (CH, CH), 1)
    ).astype(BF16)

    def transposed(weight):
        form = (NT, ((), ()))
        return lax.dot_general(eye, weight, form, preferred_element_type=F32).astype(BF16)

    coarse_parts = split(wc_ref[...])
    detail_parts = split(wd_ref[...])
    skip_parts = split(ws_ref[...])
    weights_forward = tuple(
        jnp.concatenate([transposed(c), transposed(d)], axis=0) for c, d in zip(coarse_parts, detail_parts)
    )
    weights_back = tuple(jnp.concatenate([c, d], axis=0) for c, d in zip(coarse_parts, detail_parts))

    kron[...] = jnp.zeros((4, 256, 256), F32)
    for which in range(2):
        forward = transposed(skip_parts[which]).astype(F32)
        backward = skip_parts[which].astype(F32)
        for i in range(8):
            block = slice(i * CH, (i + 1) * CH)
            kron[which, block, block] = forward
            kron[2 + which, block, block] = backward

    def skip_mix(source, first):
        weights = (kron[first].astype(BF16), kron[first + 1].astype(BF16))
        for g in range(6):
            block = slice(256 * g, 256 * g + 256)
            mixed_skip[block] = dot3(weights, split(source[block]))

    loads[2].wait()
    for half in range(2):
        pack(raw_cot, cot, half)

    coeffs[...] = gather_sum(0, own, copies1)
    copies2 = send_mixed(1, mix(coeffs[...], weights_forward))

    skip_mix(field, 0)

    synthesize_lines(1, copies2)

    def middle_column(index, carry):
        rows, lanes = column(index)
        walk = synthesis_column(rows, lanes)
        cells = pl.ds(lanes, 128)

        def load(x):
            here = pl.ds(pl.multiple_of(x * CH + rows, 8), 8)
            pre = walk.get(0, x) + mixed_skip[here, cells]
            cube = F32(GELU_B) * (pre * pre)
            tanh = jnp.tanh(pre * (F32(GELU_A) + cube))
            slope = pre * (F32(GELU_A) + F32(3.0) * cube)
            rise = (F32(0.5) + F32(0.5) * tanh) * (F32(1.0) + (slope - slope * tanh))
            value = cot[here, cells] * rise
            grad[here, cells] = value
            return value

        analyze_column(load, rows, lanes)
        return carry

    lax.fori_loop(0, 8, middle_column, 0)
    own, copies3 = send_partials(2)

    pair = jnp.zeros((256, 256), F32)
    for g in range(6):
        block = slice(256 * g, 256 * g + 256)
        pair = pair + dot3(split(field[block]), split(grad[block]), NT)
    skip_sum = pair[:CH, :CH]
    for i in range(1, 8):
        block = slice(i * CH, (i + 1) * CH)
        skip_sum = skip_sum + pair[block, block]
    skip_mix(grad, 2)

    back = gather_sum(2, own, copies3)
    copies4 = send_mixed(3, mix(back, weights_back))

    flat = side_by_side(back)
    lane = lax.rem(lax.broadcasted_iota(jnp.int32, (CH, COARSE * 128), 1), 128)
    masked = jnp.concatenate([jnp.where(lane < 32, flat, 0.0), jnp.where(lane < 32, 0.0, flat)], axis=0)
    gsum[...] = jnp.zeros((CH, 128), F32)
    gsum[:, :64] = dot3(split(side_by_side(coeffs[...])), split(masked), NT)
    gsum[:, 64:96] = skip_sum
    chunk = CH // ny
    for i in range(ny):
        ar_out[i, :chunk] = gsum[i * chunk : (i + 1) * chunk]

    def ar_copy(phase, r, source, along_x):
        size, me = (nx, gx) if along_x else (ny, gy)
        other = lax.rem(me + r, size)
        device = (other, gy) if along_x else (gx, other)
        return pltpu.make_async_remote_copy(
            src_ref=source(other),
            dst_ref=ar_in.at[phase, me],
            send_sem=ar_send.at[phase, r],
            recv_sem=ar_recv.at[phase, me],
            device_id=device,
            device_id_type=MESH,
        )

    def ar_start(phase, source, along_x):
        def step(r, carry):
            ar_copy(phase, r, source, along_x).start()
            return carry

        lax.fori_loop(1, nx if along_x else ny, step, 0)

    def ar_wait(phase, source, along_x):
        size, me = (nx, gx) if along_x else (ny, gy)

        def step(r, carry):
            other = lax.rem(me + r, size)
            arrived = ar_in.at[phase, other]
            pltpu.make_async_copy(arrived, arrived, ar_recv.at[phase, other]).wait()
            return carry

        lax.fori_loop(1, size, step, 0)

    def ar_wait_send(phase, source, along_x):
        def step(r, carry):
            ar_copy(phase, r, source, along_x).wait_send()
            return carry

        lax.fori_loop(1, nx if along_x else ny, step, 0)

    def ar_sum(phase, count):
        total = ar_in[phase, 0]
        for i in range(1, count):
            total = total + ar_in[phase, i]
        return total

    source0 = lambda other: ar_out.at[other]
    source1 = lambda other: ar_part.at[0]
    source2 = lambda other: ar_part.at[1]
    ar_in[0, gy] = ar_out[gy]
    ar_start(0, source0, False)

    ar_wait(0, source0, False)
    total = ar_sum(0, ny)
    ar_part[0] = total
    ar_in[1, gx] = total
    ar_start(1, source1, True)

    synthesize_lines(3, copies4)

    ar_wait(1, source1, True)
    total = ar_sum(1, nx)
    ar_part[1] = total
    ar_in[2, gy] = total
    ar_start(2, source2, False)

    stores = []
    for half in range(2):

        def last_column(index, carry):
            rows = pl.multiple_of(index * 8, 8)
            walk = synthesis_column(rows, 128 * half)
            for x in range(CELLS):
                here = pl.ds(pl.multiple_of(x * CH + rows, 8), 8)
                value = walk.get(0, x) + mixed_skip[here, 128 * half : 128 * half + 128]
                out[2 * half, x, pl.ds(rows, 8), :] = value[:, :CELLS]
                out[2 * half + 1, x, pl.ds(rows, 8), :] = value[:, 64 : 64 + CELLS]
            return carry

        lax.fori_loop(0, 4, last_column, 0)
        part = pl.ds(2 * half, 2)
        store = pltpu.make_async_copy(out.at[part], out_hbm.at[part], out_sems.at[half])
        store.start()
        stores.append(store)

    ar_wait(2, source2, False)
    scale = F32(1.0 / (BATCH * CELLS * CELLS * nx * ny))
    for i in range(ny):
        rows = slice(i * chunk, (i + 1) * chunk)
        values = ar_in[2, i, :chunk] * scale
        gc_ref[rows, :] = values[:, :32]
        gd_ref[rows, :] = values[:, 32:64]
        gs_ref[rows, :] = values[:, 64:96]

    for copies in (copies1, copies2, copies3, copies4):
        for copy in copies:
            copy.wait_send()
    ar_wait_send(0, source0, False)
    ar_wait_send(1, source1, True)
    ar_wait_send(2, source2, False)
    for store in stores:
        store.wait()


def shards(nx, ny, field, w_coarse, w_detail, w_skip, cotangent):
    bank = bank_matrix()
    bank_high = bank.astype(jnp.bfloat16)
    bank_low = (bank - bank_high.astype(np.float32)).astype(jnp.bfloat16)
    block = (BATCH, CELLS, CH, CELLS)
    cells = CELLS * CH
    vmem = pl.BlockSpec(memory_space=pltpu.VMEM)
    hbm = pl.BlockSpec(memory_space=pl.ANY)
    small = jax.ShapeDtypeStruct((CH, CH), F32)
    peers = max(nx, ny)


    result = pl.pallas_call(
        functools.partial(kernel, nx, ny),
        out_shape=(jax.ShapeDtypeStruct(block, F32), small, small, small),
        in_specs=[hbm, hbm, vmem, vmem, vmem, vmem, vmem],
        out_specs=(hbm, vmem, vmem, vmem),
        scratch_shapes=[
            pltpu.VMEM(block, F32),
            pltpu.VMEM(block, F32),
            pltpu.VMEM((cells, 256), F32),
            pltpu.VMEM((cells, 256), F32),
            pltpu.VMEM((cells, 256), F32),
            pltpu.VMEM((cells, 256), F32),
            pltpu.VMEM((2 * ROWS, 512), F32),
            pltpu.VMEM((4, 256, 256), F32),
            pltpu.VMEM(block, F32),
            pltpu.VMEM((2, 3, ROWS, 128), F32),
            pltpu.VMEM((2, ROWS, 128), F32),
            pltpu.VMEM((4, 3, ROWS, 128), F32),
            pltpu.VMEM((ROWS, 128), F32),
            pltpu.VMEM((2 * ROWS, 256), F32),
            pltpu.VMEM((ny, 8, 128), F32),
            pltpu.VMEM((3, peers, 8, 128), F32),
            pltpu.VMEM((2, 8, 128), F32),
            pltpu.VMEM((CH, 128), F32),
            pltpu.SemaphoreType.DMA((3,)),
            pltpu.SemaphoreType.DMA((2,)),
            pltpu.SemaphoreType.DMA((4, 3)),
            pltpu.SemaphoreType.DMA((4, 3)),
            pltpu.SemaphoreType.DMA((3, peers)),
            pltpu.SemaphoreType.DMA((3, peers)),
        ],
        compiler_params=pltpu.CompilerParams(
            collective_id=0, has_side_effects=True, vmem_limit_bytes=48 * 1024 * 1024
        ),
    )(
        jnp.transpose(field, (0, 1, 3, 2)),
        jnp.transpose(cotangent, (0, 1, 3, 2)),
        w_coarse,
        w_detail,
        w_skip,
        jnp.asarray(bank_high),
        jnp.asarray(bank_low),
    )
    return (jnp.transpose(result[0], (0, 1, 3, 2)),) + tuple(result[1:])


def solution(mesh):
    nx, ny = mesh.shape["gx"], mesh.shape["gy"]
    in_specs = (P(None, "gx", "gy", None), P(), P(), P(), P(None, "gx", "gy", None))
    out_specs = (P(None, "gx", "gy", None), P(), P(), P())

    def run(*args):
        return shards(nx, ny, *args)

    return jax.shard_map(run, mesh=mesh, in_specs=in_specs, out_specs=out_specs, check_vma=False)
```

```python
import functools

import jax
import jax.numpy as jnp
import numpy as np
from jax import lax
from jax.experimental import pallas as pl
from jax.experimental.pallas import tpu as pltpu
from jax.sharding import PartitionSpec as P

LOW_TAPS = [
    0.23037781330885523,
    0.7148465705525415,
    0.6308807679295904,
    -0.02798376941698385,
    -0.18703481171888114,
    0.030841381835986965,
    0.032883011666982945,
    -0.010597401784997278,
]
HIGH_TAPS = [(-1) ** offset * LOW_TAPS[7 - offset] for offset in range(8)]

F32 = jnp.float32
BF16 = jnp.bfloat16
MESH = pl.DeviceIdType.MESH
CH = 32
BATCH = 4
CELLS = 48
COARSE = 6
ROWS = COARSE * CH
GELU_A = 0.7978845608028654
GELU_B = GELU_A * 0.044715


def bounds(low, high):
    return -((7 - low) // 2), high // 2


LEVELS = [(0, CELLS - 1)]
for _ in range(3):
    LEVELS.append(bounds(*LEVELS[-1]))


def line_matrix():
    values = np.eye(CELLS)
    low, high = LEVELS[0]
    outputs = []
    for level in range(3):
        bank = [LOW_TAPS] if level < 2 else [LOW_TAPS, HIGH_TAPS]
        first, last = LEVELS[level + 1]
        outputs = []
        for taps in bank:
            result = np.zeros((last - first + 1, CELLS))
            for k in range(first, last + 1):
                for j in range(8):
                    if low <= 2 * k + j <= high:
                        result[k - first] += taps[j] * values[2 * k + j - low]
            outputs.append(result)
        values, low, high = outputs[0], first, last
    return np.stack(outputs)


def bank_matrix():
    line = line_matrix()
    result = np.zeros((2, BATCH, 64, 2, 2, 2, 32))
    for xband in range(2):
        for b in range(BATCH):
            for part in range(2):
                for yband in range(2):
                    for k in range(COARSE):
                        result[xband, b, :CELLS, part, xband, yband, k * BATCH + b] = line[yband, part * COARSE + k]
    return result.reshape(512, 256).astype(np.float32)


def split(values):
    high = values.astype(BF16)
    return high, (values - high.astype(F32)).astype(BF16)


def dot3(left, right, dims=((1,), (0,))):
    form = (dims, ((), ()))
    total = lax.dot_general(left[0], right[0], form, preferred_element_type=F32)
    total += lax.dot_general(left[1], right[0], form, preferred_element_type=F32)
    return total + lax.dot_general(left[0], right[1], form, preferred_element_type=F32)


NT = ((1,), (1,))


class Analysis:
    def __init__(self, load):
        self.load = load
        self.memo = {}

    def get(self, level, k, taps=LOW_TAPS, band=0):
        if level == 0:
            if (0, k) not in self.memo:
                self.memo[0, k] = self.load(k)
            return self.memo[0, k]
        key = (level, k, band)
        if key not in self.memo:
            low, high = LEVELS[level - 1]
            total = None
            for j in range(8):
                if low <= 2 * k + j <= high:
                    term = self.get(level - 1, 2 * k + j) * F32(taps[j])
                    total = term if total is None else total + term
            self.memo[key] = total
        return self.memo[key]


class Synthesis:
    def __init__(self, load):
        self.load = load
        self.memo = {}

    def top(self, band, k):
        if (band, k) not in self.memo:
            self.memo[band, k] = self.load(band, k)
        return self.memo[band, k]

    def get(self, level, i):
        key = (level, i, "s")
        if key not in self.memo:
            low, high = LEVELS[level + 1]
            total = None
            for k in range(low, high + 1):
                j = i - 2 * k
                if 0 <= j < 8:
                    if level == 2:
                        term = self.top(0, k) * F32(LOW_TAPS[j]) + self.top(1, k) * F32(HIGH_TAPS[j])
                    else:
                        term = self.get(level + 1, k) * F32(LOW_TAPS[j])
                    total = term if total is None else total + term
            self.memo[key] = total
        return self.memo[key]


def column_at(index):
    rows = pl.multiple_of(lax.rem(index, 4) * 8, 8)
    lanes = pl.multiple_of(lax.div(index, 4) * 128, 128)
    return rows, lanes


def synthesis_column(lines, rows, lanes):
    def load(band, k):
        return lines[
            pl.ds(pl.multiple_of((k + COARSE) * CH + rows, 8), 8),
            pl.ds(pl.multiple_of(band * 256 + lanes, 128), 128),
        ]

    return Synthesis(load)


def last_kernel(
    lines_hbm, base_hbm, sum_hbm, out_hbm, gc_ref, gd_ref, gs_ref, lines, base, summed, out, in_sems, out_sems
):
    loads = [pltpu.make_async_copy(lines_hbm, lines, in_sems.at[0])]
    for half in range(2):
        lanes = pl.ds(128 * half, 128)
        loads.append(pltpu.make_async_copy(base_hbm.at[:, lanes], base.at[:, lanes], in_sems.at[1 + half]))
    loads.append(pltpu.make_async_copy(sum_hbm, summed, in_sems.at[3]))
    for load in loads:
        load.start()
    loads[0].wait()
    stores = []
    for half in range(2):
        loads[1 + half].wait()

        def last_column(index, carry):
            rows = pl.multiple_of(index * 8, 8)
            walk = synthesis_column(lines, rows, 128 * half)
            for x in range(CELLS):
                here = pl.ds(pl.multiple_of(x * CH + rows, 8), 8)
                value = walk.get(0, x) + base[here, 128 * half : 128 * half + 128]
                out[2 * half, x, pl.ds(rows, 8), :] = value[:, :CELLS]
                out[2 * half + 1, x, pl.ds(rows, 8), :] = value[:, 64 : 64 + CELLS]
            return carry

        lax.fori_loop(0, 4, last_column, 0)
        part = pl.ds(2 * half, 2)
        store = pltpu.make_async_copy(out.at[part], out_hbm.at[part], out_sems.at[half])
        store.start()
        stores.append(store)
    loads[3].wait()
    gc_ref[...] = summed[:, :32]
    gd_ref[...] = summed[:, 32:64]
    gs_ref[...] = summed[:, 64:96]
    for store in stores:
        store.wait()


def kernel(
    nx, ny, field_hbm, cot_hbm, wc_hbm, wd_hbm, ws_hbm, bank_hbm,
    lines_hbm, base_hbm, sum_hbm,
    raw, raw_cot, field, cot, grad, mixed_skip, lines, kron, wc_ref, wd_ref, ws_ref, bank_ref, bank_parts,
    send_fwd, send_mix, recv, wide, ar_out, ar_in, ar_part, gsum,
    in_sems, out_sems, ex_send, ex_recv, ar_send, ar_recv,
):
    gx = lax.axis_index("gx")
    gy = lax.axis_index("gy")
    right, left = lax.rem(gx + 1, nx), lax.rem(gx + nx - 1, nx)
    up, down = lax.rem(gy + 1, ny), lax.rem(gy + ny - 1, ny)

    loads = []
    for half in range(2):
        part = pl.ds(2 * half, 2)
        loads.append(pltpu.make_async_copy(field_hbm.at[part], raw.at[part], in_sems.at[half]))
    small = [(bank_hbm, bank_ref), (wc_hbm, wc_ref), (wd_hbm, wd_ref), (ws_hbm, ws_ref)]
    for slot, (source, target) in enumerate(small + [(cot_hbm, raw_cot)]):
        loads.append(pltpu.make_async_copy(source, target, in_sems.at[2 + slot]))
    for load in loads:
        load.start()

    barrier = pltpu.get_barrier_semaphore()

    def greet_y(r, carry):
        pl.semaphore_signal(barrier, inc=1, device_id=(gx, lax.rem(gy + r, ny)), device_id_type=MESH)
        return carry

    def greet_x(r, carry):
        pl.semaphore_signal(barrier, inc=1, device_id=(lax.rem(gx + r, nx), gy), device_id_type=MESH)
        return carry

    lax.fori_loop(1, nx, greet_x, 0)
    lax.fori_loop(1, ny, greet_y, 0)
    pl.semaphore_signal(barrier, inc=1, device_id=(right, up), device_id_type=MESH)
    pl.semaphore_signal(barrier, inc=1, device_id=(left, down), device_id_type=MESH)

    def pack(source, target, half):
        columns = 128 * half
        target[:, columns : columns + 128] = jnp.zeros((CELLS * CH, 128), F32)
        for pair in range(2):
            values = source[2 * half + pair].reshape(CELLS * CH, CELLS)
            start = columns + 64 * pair
            target[:, start : start + CELLS] = values

    def analyze_column(load, rows, lanes):
        walk = Analysis(load)
        for k in range(2 * COARSE):
            for band, taps in enumerate((LOW_TAPS, HIGH_TAPS)):
                value = walk.get(3, k - COARSE, taps, band)
                lines[pl.ds(pl.multiple_of(k * CH + rows, 8), 8), pl.ds(pl.multiple_of(band * 256 + lanes, 128), 128)] = value

    def exchange(step, sources, devices):
        copies = []
        for slot, (source, device) in enumerate(zip(sources, devices)):
            copy = pltpu.make_async_remote_copy(
                src_ref=source,
                dst_ref=recv.at[step, slot],
                send_sem=ex_send.at[step, slot],
                recv_sem=ex_recv.at[step, slot],
                device_id=device,
                device_id_type=MESH,
            )
            copy.start()
            copies.append(copy)
        return copies

    back_devices = [(left, gy), (gx, down), (left, down)]
    next_devices = [(right, gy), (gx, up), (right, up)]

    def send_partials(step):
        parts = dot3(split(lines[...]), (bank_parts[0], bank_parts[1]))
        send_fwd[step // 2, 0] = parts[:ROWS, 128:]
        send_fwd[step // 2, 1] = parts[ROWS:, :128]
        send_fwd[step // 2, 2] = parts[:ROWS, :128]
        return parts, exchange(step, [send_fwd.at[step // 2, s] for s in range(3)], back_devices)

    def gather_sum(step, parts, copies):
        total = parts[ROWS:, 128:]
        for slot, copy in enumerate(copies):
            copy.wait_recv()
            total = total + recv[step, slot]
        return total

    def side_by_side(values):
        return jnp.concatenate([values[k : k + CH] for k in range(0, values.shape[0], CH)], axis=1)

    def mix(values, weights):
        count, width = values.shape[0] // CH, values.shape[1]
        both = dot3(weights, split(side_by_side(values)))
        coarse = lax.rem(lax.broadcasted_iota(jnp.int32, both[:CH].shape, 1), 128) < 32
        chosen = jnp.where(coarse, both[:CH], both[CH:])
        return jnp.concatenate([chosen[:, k * width : (k + 1) * width] for k in range(count)], axis=0)

    def send_next(step, values):
        send_mix[step // 2] = values
        return exchange(step, [send_mix.at[step // 2]] * 3, next_devices)

    def gather_wide(step, copies):
        wide[ROWS:, 128:] = send_mix[step // 2]
        for copy in copies:
            copy.wait_recv()
        wide[:ROWS, :128] = recv[step, 2]
        wide[:ROWS, 128:] = recv[step, 0]
        wide[ROWS:, :128] = recv[step, 1]

    loads[2].wait()
    bank_parts[0], bank_parts[1] = split(bank_ref[...])
    for half in range(2):
        loads[half].wait()
        pack(raw, field, half)

    def first_column(index, carry):
        rows, lanes = column_at(index)
        analyze_column(
            lambda x: field[pl.ds(pl.multiple_of(x * CH + rows, 8), 8), pl.ds(lanes, 128)], rows, lanes
        )
        return carry

    lax.fori_loop(0, 8, first_column, 0)
    pl.semaphore_wait(barrier, nx + ny)
    parts, copies1 = send_partials(0)

    eye = (
        lax.broadcasted_iota(jnp.int32, (CH, CH), 0) == lax.broadcasted_iota(jnp.int32, (CH, CH), 1)
    ).astype(BF16)

    def transposed(weight):
        form = (NT, ((), ()))
        return lax.dot_general(eye, weight, form, preferred_element_type=F32).astype(BF16)

    for load in loads[3:6]:
        load.wait()
    coarse_parts = split(wc_ref[...])
    detail_parts = split(wd_ref[...])
    skip_parts = split(ws_ref[...])
    weights_forward = tuple(
        jnp.concatenate([transposed(c), transposed(d)], axis=0) for c, d in zip(coarse_parts, detail_parts)
    )
    weights_back = tuple(jnp.concatenate([c, d], axis=0) for c, d in zip(coarse_parts, detail_parts))

    kron[...] = jnp.zeros((4, 256, 256), F32)
    for which in range(2):
        forward = transposed(skip_parts[which]).astype(F32)
        backward = skip_parts[which].astype(F32)
        for i in range(8):
            block = slice(i * CH, (i + 1) * CH)
            kron[which, block, block] = forward
            kron[2 + which, block, block] = backward

    def skip_mix(source, first):
        weights = (kron[first].astype(BF16), kron[first + 1].astype(BF16))
        for g in range(6):
            block = slice(256 * g, 256 * g + 256)
            mixed_skip[block] = dot3(weights, split(source[block]))

    loads[6].wait()
    for half in range(2):
        pack(raw_cot, cot, half)

    copies2 = send_next(1, gather_sum(0, parts, copies1))

    skip_mix(field, 0)

    gather_wide(1, copies2)
    lines[...] = dot3(split(mix(wide[...], weights_forward)), (bank_parts[0], bank_parts[1]), NT)

    def middle_column(index, carry):
        rows, lanes = column_at(index)
        walk = synthesis_column(lines, rows, lanes)
        cells = pl.ds(lanes, 128)

        def load(x):
            here = pl.ds(pl.multiple_of(x * CH + rows, 8), 8)
            pre = walk.get(0, x) + mixed_skip[here, cells]
            cube = F32(GELU_B) * (pre * pre)
            tanh = jnp.tanh(pre * (F32(GELU_A) + cube))
            slope = pre * (F32(GELU_A) + F32(3.0) * cube)
            rise = (F32(0.5) + F32(0.5) * tanh) * (F32(1.0) + (slope - slope * tanh))
            value = cot[here, cells] * rise
            grad[here, cells] = value
            return value

        analyze_column(load, rows, lanes)
        return carry

    lax.fori_loop(0, 8, middle_column, 0)
    parts, copies3 = send_partials(2)

    flat = side_by_side(parts)
    coarse = lax.rem(lax.broadcasted_iota(jnp.int32, flat.shape, 1), 128) < 32
    masked = jnp.concatenate([jnp.where(coarse, flat, 0.0), jnp.where(coarse, 0.0, flat)], axis=0)
    gsum[...] = jnp.zeros((CH, 128), F32)
    gsum[:, :64] = dot3(split(side_by_side(wide[...])), split(masked), NT)
    pair = jnp.zeros((256, 256), F32)
    for g in range(6):
        block = slice(256 * g, 256 * g + 256)
        pair = pair + dot3(split(field[block]), split(grad[block]), NT)
    skip_sum = pair[:CH, :CH]
    for i in range(1, 8):
        block = slice(i * CH, (i + 1) * CH)
        skip_sum = skip_sum + pair[block, block]
    gsum[:, 64:96] = skip_sum

    chunk = CH // ny
    for i in range(ny):
        ar_out[i, :chunk] = gsum[i * chunk : (i + 1) * chunk]

    def ar_copy(phase, r, source, along_x):
        size, me = (nx, gx) if along_x else (ny, gy)
        other = lax.rem(me + r, size)
        device = (other, gy) if along_x else (gx, other)
        return pltpu.make_async_remote_copy(
            src_ref=source(other),
            dst_ref=ar_in.at[phase, me],
            send_sem=ar_send.at[phase, r],
            recv_sem=ar_recv.at[phase, me],
            device_id=device,
            device_id_type=MESH,
        )

    def ar_start(phase, source, along_x):
        def step(r, carry):
            ar_copy(phase, r, source, along_x).start()
            return carry

        lax.fori_loop(1, nx if along_x else ny, step, 0)

    def ar_wait(phase, source, along_x):
        size, me = (nx, gx) if along_x else (ny, gy)

        def step(r, carry):
            other = lax.rem(me + r, size)
            arrived = ar_in.at[phase, other]
            pltpu.make_async_copy(arrived, arrived, ar_recv.at[phase, other]).wait()
            return carry

        lax.fori_loop(1, size, step, 0)

    def ar_wait_send(phase, source, along_x):
        def step(r, carry):
            ar_copy(phase, r, source, along_x).wait_send()
            return carry

        lax.fori_loop(1, nx if along_x else ny, step, 0)

    def ar_sum(phase, count):
        total = ar_in[phase, 0]
        for i in range(1, count):
            total = total + ar_in[phase, i]
        return total

    source0 = lambda other: ar_out.at[other]
    source1 = lambda other: ar_part.at[0]
    source2 = lambda other: ar_part.at[1]
    ar_in[0, gy] = ar_out[gy]
    ar_start(0, source0, False)

    copies4 = send_next(3, mix(gather_sum(2, parts, copies3), weights_back))

    ar_wait(0, source0, False)
    total = ar_sum(0, ny)
    ar_part[0] = total
    ar_in[1, gx] = total
    ar_start(1, source1, True)

    skip_mix(grad, 2)
    base_store = pltpu.make_async_copy(mixed_skip, base_hbm, out_sems.at[0])
    base_store.start()

    ar_wait(1, source1, True)
    total = ar_sum(1, nx)
    ar_part[1] = total
    ar_in[2, gy] = total
    ar_start(2, source2, False)

    gather_wide(3, copies4)
    lines[...] = dot3(split(wide[...]), (bank_parts[0], bank_parts[1]), NT)
    lines_store = pltpu.make_async_copy(lines, lines_hbm, out_sems.at[1])
    lines_store.start()

    for copies in (copies1, copies2, copies3, copies4):
        for copy in copies:
            copy.wait_send()
    ar_wait_send(0, source0, False)
    ar_wait_send(1, source1, True)

    ar_wait(2, source2, False)
    scale = F32(1.0 / (BATCH * CELLS * CELLS * nx * ny))
    for i in range(ny):
        gsum[i * chunk : (i + 1) * chunk] = ar_in[2, i, :chunk] * scale
    sum_store = pltpu.make_async_copy(gsum, sum_hbm, out_sems.at[2])
    sum_store.start()
    ar_wait_send(2, source2, False)
    base_store.wait()
    lines_store.wait()
    sum_store.wait()


def shards(nx, ny, field, w_coarse, w_detail, w_skip, cotangent):
    bank = bank_matrix()
    block = (BATCH, CELLS, CH, CELLS)
    cells = CELLS * CH
    vmem = pl.BlockSpec(memory_space=pltpu.VMEM)
    hbm = pl.BlockSpec(memory_space=pl.ANY)
    small = jax.ShapeDtypeStruct((CH, CH), F32)
    peers = max(nx, ny)


    weight = pltpu.VMEM((CH, CH), F32)
    lines, base, summed = pl.pallas_call(
        functools.partial(kernel, nx, ny),
        out_shape=(
            jax.ShapeDtypeStruct((2 * ROWS, 512), F32),
            jax.ShapeDtypeStruct((cells, 256), F32),
            jax.ShapeDtypeStruct((CH, 128), F32),
        ),
        in_specs=[hbm] * 6,
        out_specs=(hbm, hbm, hbm),
        scratch_shapes=[
            pltpu.VMEM(block, F32),
            pltpu.VMEM(block, F32),
            pltpu.VMEM((cells, 256), F32),
            pltpu.VMEM((cells, 256), F32),
            pltpu.VMEM((cells, 256), F32),
            pltpu.VMEM((cells, 256), F32),
            pltpu.VMEM((2 * ROWS, 512), F32),
            pltpu.VMEM((4, 256, 256), F32),
            weight,
            weight,
            weight,
            pltpu.VMEM((512, 256), F32),
            pltpu.VMEM((2, 512, 256), BF16),
            pltpu.VMEM((2, 3, ROWS, 128), F32),
            pltpu.VMEM((2, ROWS, 128), F32),
            pltpu.VMEM((4, 3, ROWS, 128), F32),
            pltpu.VMEM((2 * ROWS, 256), F32),
            pltpu.VMEM((ny, 8, 128), F32),
            pltpu.VMEM((3, peers, 8, 128), F32),
            pltpu.VMEM((2, 8, 128), F32),
            pltpu.VMEM((CH, 128), F32),
            pltpu.SemaphoreType.DMA((7,)),
            pltpu.SemaphoreType.DMA((3,)),
            pltpu.SemaphoreType.DMA((4, 3)),
            pltpu.SemaphoreType.DMA((4, 3)),
            pltpu.SemaphoreType.DMA((3, peers)),
            pltpu.SemaphoreType.DMA((3, peers)),
        ],
        compiler_params=pltpu.CompilerParams(
            collective_id=0, has_side_effects=True, vmem_limit_bytes=60 * 1024 * 1024
        ),
    )(
        jnp.transpose(field, (0, 1, 3, 2)),
        jnp.transpose(cotangent, (0, 1, 3, 2)),
        w_coarse,
        w_detail,
        w_skip,
        jnp.asarray(bank),
    )
    result = pl.pallas_call(
        last_kernel,
        out_shape=(jax.ShapeDtypeStruct(block, F32), small, small, small),
        in_specs=[hbm] * 3,
        out_specs=(hbm, vmem, vmem, vmem),
        scratch_shapes=[
            pltpu.VMEM((2 * ROWS, 512), F32),
            pltpu.VMEM((cells, 256), F32),
            pltpu.VMEM((CH, 128), F32),
            pltpu.VMEM(block, F32),
            pltpu.SemaphoreType.DMA((4,)),
            pltpu.SemaphoreType.DMA((2,)),
        ],
        compiler_params=pltpu.CompilerParams(vmem_limit_bytes=60 * 1024 * 1024),
    )(lines, base, summed)
    return (jnp.transpose(result[0], (0, 1, 3, 2)),) + tuple(result[1:])


def solution(mesh):
    nx, ny = mesh.shape["gx"], mesh.shape["gy"]
    in_specs = (P(None, "gx", "gy", None), P(), P(), P(), P(None, "gx", "gy", None))
    out_specs = (P(None, "gx", "gy", None), P(), P(), P())

    def run(*args):
        return shards(nx, ny, *args)

    return jax.shard_map(run, mesh=mesh, in_specs=in_specs, out_specs=out_specs, check_vma=False)
```

```python
import functools

import jax
import jax.numpy as jnp
import numpy as np
from jax import lax
from jax.experimental import pallas as pl
from jax.experimental.pallas import tpu as pltpu
from jax.sharding import PartitionSpec as P

LOW_TAPS = [
    0.23037781330885523,
    0.7148465705525415,
    0.6308807679295904,
    -0.02798376941698385,
    -0.18703481171888114,
    0.030841381835986965,
    0.032883011666982945,
    -0.010597401784997278,
]
HIGH_TAPS = [(-1) ** offset * LOW_TAPS[7 - offset] for offset in range(8)]

F32 = jnp.float32
BF16 = jnp.bfloat16
MESH = pl.DeviceIdType.MESH
CH = 32
BATCH = 4
CELLS = 48
COARSE = 6
ROWS = COARSE * CH // 2
GELU_A = 0.7978845608028654
GELU_B = GELU_A * 0.044715


def bounds(low, high):
    return -((7 - low) // 2), high // 2


LEVELS = [(0, CELLS - 1)]
for _ in range(3):
    LEVELS.append(bounds(*LEVELS[-1]))


def line_matrix():
    values = np.eye(CELLS)
    low, high = LEVELS[0]
    outputs = []
    for level in range(3):
        bank = [LOW_TAPS] if level < 2 else [LOW_TAPS, HIGH_TAPS]
        first, last = LEVELS[level + 1]
        outputs = []
        for taps in bank:
            result = np.zeros((last - first + 1, CELLS))
            for k in range(first, last + 1):
                for j in range(8):
                    if low <= 2 * k + j <= high:
                        result[k - first] += taps[j] * values[2 * k + j - low]
            outputs.append(result)
        values, low, high = outputs[0], first, last
    return np.stack(outputs)


def bank_matrix():
    line = line_matrix()
    result = np.zeros((2, 2, 2, 64, 2, 2, 64))
    for group in range(2):
        for xband in range(2):
            for b in range(2):
                for part in range(2):
                    for yband in range(2):
                        for k in range(COARSE):
                            lane = ((xband * 2 + yband) * COARSE + k) * 2 + b
                            result[group, xband, b, :CELLS, part, group, lane] = line[yband, part * COARSE + k]
    return result.reshape(512, 256).astype(np.float32)


def split(values):
    high = values.astype(BF16)
    return high, (values - high.astype(F32)).astype(BF16)


def dot3(left, right, dims=((1,), (0,))):
    form = (dims, ((), ()))
    total = lax.dot_general(left[0], right[0], form, preferred_element_type=F32)
    total += lax.dot_general(left[1], right[0], form, preferred_element_type=F32)
    return total + lax.dot_general(left[0], right[1], form, preferred_element_type=F32)


NT = ((1,), (1,))


class Analysis:
    def __init__(self, load):
        self.load = load
        self.memo = {}

    def get(self, level, k, taps=LOW_TAPS, band=0):
        if level == 0:
            if (0, k) not in self.memo:
                self.memo[0, k] = self.load(k)
            return self.memo[0, k]
        key = (level, k, band)
        if key not in self.memo:
            low, high = LEVELS[level - 1]
            total = None
            for j in range(8):
                if low <= 2 * k + j <= high:
                    term = self.get(level - 1, 2 * k + j) * F32(taps[j])
                    total = term if total is None else total + term
            self.memo[key] = total
        return self.memo[key]


class Synthesis:
    def __init__(self, load):
        self.load = load
        self.memo = {}

    def top(self, band, k):
        if (band, k) not in self.memo:
            self.memo[band, k] = self.load(band, k)
        return self.memo[band, k]

    def get(self, level, i):
        key = (level, i, "s")
        if key not in self.memo:
            low, high = LEVELS[level + 1]
            total = None
            for k in range(low, high + 1):
                j = i - 2 * k
                if 0 <= j < 8:
                    if level == 2:
                        term = self.top(0, k) * F32(LOW_TAPS[j]) + self.top(1, k) * F32(HIGH_TAPS[j])
                    else:
                        term = self.get(level + 1, k) * F32(LOW_TAPS[j])
                    total = term if total is None else total + term
            self.memo[key] = total
        return self.memo[key]


def synthesis_column(lines, rows):
    def load(band, k):
        part, group, row = (k + COARSE) // 6, (k + COARSE) % 6 // 3, (k + COARSE) % 3
        start = (part * 3 + row) * CH
        lanes = group * 256 + band * 128
        return lines[pl.ds(pl.multiple_of(start + rows, 8), 8), lanes : lanes + 128]

    return Synthesis(load)


def analyze_column(lines, rows, load):
    walk = Analysis(load)
    for k in range(-COARSE, COARSE):
        part, group, row = (k + COARSE) // 6, (k + COARSE) % 6 // 3, (k + COARSE) % 3
        start = (part * 3 + row) * CH
        for band, taps in enumerate((LOW_TAPS, HIGH_TAPS)):
            lanes = group * 256 + band * 128
            lines[pl.ds(pl.multiple_of(start + rows, 8), 8), lanes : lanes + 128] = walk.get(3, k, taps, band)


def side_by_side(values):
    return jnp.concatenate([values[k : k + CH] for k in range(0, values.shape[0], CH)], axis=1)


def in_coarse(values):
    return lax.rem(lax.broadcasted_iota(jnp.int32, values.shape, 1), 64) < 12


def mix(values, weights):
    count, width = values.shape[0] // CH, values.shape[1]
    both = dot3(weights, split(side_by_side(values)))
    chosen = jnp.where(in_coarse(both[:CH]), both[:CH], both[CH:])
    return jnp.concatenate([chosen[:, k * width : (k + 1) * width] for k in range(count)], axis=0)


def pack(source, target, half):
    for pair in range(2):
        values = source[2 * half + pair].reshape(CELLS * CH, CELLS)
        target[half, :, 64 * pair : 64 * pair + CELLS] = values


def kernel(
    nx, ny, field_hbm, cot_hbm, wc_hbm, wd_hbm, ws_hbm, bank_hbm, out_hbm, sum_ref,
    raw, raw_cot, field, cot, grad, skip, base, lines, kron, wc_ref, wd_ref, ws_ref, bank_ref, bank_parts,
    send_fwd, send_mix, recv, wide, out, ar_out, ar_in, ar_part, gsum,
    in_sems, out_sems, ex_send, ex_recv, ar_send, ar_recv,
):
    gx = lax.axis_index("gx")
    gy = lax.axis_index("gy")
    right, left = lax.rem(gx + 1, nx), lax.rem(gx + nx - 1, nx)
    up, down = lax.rem(gy + 1, ny), lax.rem(gy + ny - 1, ny)

    halves = [pl.ds(0, 2), pl.ds(2, 2)]
    moves = [
        (field_hbm.at[halves[0]], raw.at[halves[0]]),
        (bank_hbm, bank_ref),
        (field_hbm.at[halves[1]], raw.at[halves[1]]),
        (wc_hbm, wc_ref),
        (wd_hbm, wd_ref),
        (ws_hbm, ws_ref),
        (cot_hbm.at[halves[0]], raw_cot.at[halves[0]]),
        (cot_hbm.at[halves[1]], raw_cot.at[halves[1]]),
    ]
    loads = [pltpu.make_async_copy(source, target, in_sems.at[i]) for i, (source, target) in enumerate(moves)]
    for load in loads:
        load.start()

    barrier = pltpu.get_barrier_semaphore()

    def greet_y(r, carry):
        pl.semaphore_signal(barrier, inc=1, device_id=(gx, lax.rem(gy + r, ny)), device_id_type=MESH)
        return carry

    def greet_x(r, carry):
        pl.semaphore_signal(barrier, inc=1, device_id=(lax.rem(gx + r, nx), gy), device_id_type=MESH)
        return carry

    lax.fori_loop(1, nx, greet_x, 0)
    lax.fori_loop(1, ny, greet_y, 0)
    pl.semaphore_signal(barrier, inc=1, device_id=(right, up), device_id_type=MESH)
    pl.semaphore_signal(barrier, inc=1, device_id=(left, down), device_id_type=MESH)

    field[...] = jnp.zeros(field.shape, F32)
    cot[...] = jnp.zeros(cot.shape, F32)
    kron[...] = jnp.zeros(kron.shape, F32)

    def bank():
        return bank_parts[0], bank_parts[1]

    def exchange(step, half, sources, devices):
        copies = []
        for slot, (source, device) in enumerate(zip(sources, devices)):
            copy = pltpu.make_async_remote_copy(
                src_ref=source,
                dst_ref=recv.at[step, half, slot],
                send_sem=ex_send.at[step, half, slot],
                recv_sem=ex_recv.at[step, half, slot],
                device_id=device,
                device_id_type=MESH,
            )
            copy.start()
            copies.append(copy)
        return copies

    back_devices = [(left, gy), (gx, down), (left, down)]
    next_devices = [(right, gy), (gx, up), (right, up)]

    def send_partials(step, half):
        parts = dot3(split(lines[half]), bank())
        out_refs = send_fwd.at[step // 2, half]
        out_refs[0] = parts[:ROWS, 128:]
        out_refs[1] = parts[ROWS:, :128]
        out_refs[2] = parts[:ROWS, :128]
        return parts, exchange(step, half, [out_refs.at[s] for s in range(3)], back_devices)

    def gather_sum(step, half, parts, copies):
        total = parts[ROWS:, 128:]
        for slot, copy in enumerate(copies):
            copy.wait_recv()
            total = total + recv[step, half, slot]
        return total

    def send_next(step, half, values):
        send_mix[step // 2, half] = values
        return exchange(step, half, [send_mix.at[step // 2, half]] * 3, next_devices)

    def gather_wide(step, half, copies):
        for copy in copies:
            copy.wait_recv()
        before = jnp.concatenate([recv[step, half, 2], recv[step, half, 0]], axis=1)
        own = jnp.concatenate([recv[step, half, 1], send_mix[step // 2, half]], axis=1)
        return jnp.concatenate([before, own], axis=0)

    def cells(x, rows):
        return pl.ds(pl.multiple_of(x * CH + rows, 8), 8)

    def first(half):
        pack(raw, field, half)

        def column(index, carry):
            rows = pl.multiple_of(index * 8, 8)
            analyze_column(lines.at[half], rows, lambda x: field[half, cells(x, rows), :])
            return carry

        lax.fori_loop(0, 4, column, 0)

    loads[1].wait()
    bank_parts[0], bank_parts[1] = split(bank_ref[...])
    loads[0].wait()
    first(0)
    pl.semaphore_wait(barrier, nx + ny)
    parts0, copies1a = send_partials(0, 0)
    loads[2].wait()
    first(1)
    parts1, copies1b = send_partials(0, 1)

    eye = (
        lax.broadcasted_iota(jnp.int32, (CH, CH), 0) == lax.broadcasted_iota(jnp.int32, (CH, CH), 1)
    ).astype(BF16)

    def transposed(weight):
        form = (NT, ((), ()))
        return lax.dot_general(eye, weight, form, preferred_element_type=F32).astype(BF16)

    for load in loads[3:6]:
        load.wait()
    coarse_parts = split(wc_ref[...])
    detail_parts = split(wd_ref[...])
    skip_parts = split(ws_ref[...])
    weights_forward = tuple(
        jnp.concatenate([transposed(c), transposed(d)], axis=0) for c, d in zip(coarse_parts, detail_parts)
    )
    weights_back = tuple(jnp.concatenate([c, d], axis=0) for c, d in zip(coarse_parts, detail_parts))

    for which in range(2):
        forward = transposed(skip_parts[which]).astype(F32)
        backward = skip_parts[which].astype(F32)
        for i in range(8):
            block = slice(i * CH, (i + 1) * CH)
            kron[which, block, block] = forward
            kron[2 + which, block, block] = backward

    def skip_mix(source, target, kind, half):
        weights = (kron[kind].astype(BF16), kron[kind + 1].astype(BF16))
        for g in range(6):
            block = slice(256 * g, 256 * g + 256)
            target[half, block] = dot3(weights, split(source[half, block]))

    skip_mix(field, skip, 0, 0)
    loads[6].wait()
    pack(raw_cot, cot, 0)

    copies2a = send_next(1, 0, gather_sum(0, 0, parts0, copies1a))

    loads[7].wait()
    pack(raw_cot, cot, 1)

    copies2b = send_next(1, 1, gather_sum(0, 1, parts1, copies1b))

    skip_mix(field, skip, 0, 1)

    def middle(half, copies):
        values = gather_wide(1, half, copies)
        wide[half] = values
        lines[half] = dot3(split(mix(values, weights_forward)), bank(), NT)

        def column(index, carry):
            rows = pl.multiple_of(index * 8, 8)
            walk = synthesis_column(lines.at[half], rows)

            def load(x):
                here = cells(x, rows)
                pre = walk.get(0, x) + skip[half, here, :]
                cube = F32(GELU_B) * (pre * pre)
                tanh = jnp.tanh(pre * (F32(GELU_A) + cube))
                slope = pre * (F32(GELU_A) + F32(3.0) * cube)
                rise = (F32(0.5) + F32(0.5) * tanh) * (F32(1.0) + (slope - slope * tanh))
                value = cot[half, here, :] * rise
                grad[half, here, :] = value
                return value

            analyze_column(lines.at[half], rows, load)
            return carry

        lax.fori_loop(0, 4, column, 0)
        return send_partials(2, half)

    parts0, copies3a = middle(0, copies2a)
    parts1, copies3b = middle(1, copies2b)

    def share(half, parts):
        flat = side_by_side(parts)
        coarse = in_coarse(flat)
        masked = jnp.concatenate([jnp.where(coarse, flat, 0.0), jnp.where(coarse, 0.0, flat)], axis=0)
        both = dot3(split(side_by_side(wide[half])), split(masked), NT)
        pair = jnp.zeros((256, 256), F32)
        for g in range(6):
            block = slice(256 * g, 256 * g + 256)
            pair = pair + dot3(split(field[half, block]), split(grad[half, block]), NT)
        return both, pair

    both0, pair0 = share(0, parts0)
    copies4a = send_next(3, 0, mix(gather_sum(2, 0, parts0, copies3a), weights_back))
    both1, pair1 = share(1, parts1)

    pair = pair0 + pair1
    skip_sum = pair[:CH, :CH]
    for i in range(1, 8):
        block = slice(i * CH, (i + 1) * CH)
        skip_sum = skip_sum + pair[block, block]
    gsum[...] = jnp.zeros((CH, 128), F32)
    gsum[:, :64] = both0 + both1
    gsum[:, 64:96] = skip_sum

    chunk = CH // ny
    for i in range(ny):
        ar_out[i] = gsum[i * chunk : (i + 1) * chunk]

    def ar_copy(phase, r, source, along_x):
        size, me = (nx, gx) if along_x else (ny, gy)
        other = lax.rem(me + r, size)
        device = (other, gy) if along_x else (gx, other)
        return pltpu.make_async_remote_copy(
            src_ref=source(other),
            dst_ref=ar_in.at[phase, me],
            send_sem=ar_send.at[phase, r],
            recv_sem=ar_recv.at[phase, me],
            device_id=device,
            device_id_type=MESH,
        )

    def ar_start(phase, source, along_x):
        def step(r, carry):
            ar_copy(phase, r, source, along_x).start()
            return carry

        lax.fori_loop(1, nx if along_x else ny, step, 0)

    def ar_wait(phase, source, along_x):
        size, me = (nx, gx) if along_x else (ny, gy)

        def step(r, carry):
            other = lax.rem(me + r, size)
            arrived = ar_in.at[phase, other]
            pltpu.make_async_copy(arrived, arrived, ar_recv.at[phase, other]).wait()
            return carry

        lax.fori_loop(1, size, step, 0)

    def ar_wait_send(phase, source, along_x):
        def step(r, carry):
            ar_copy(phase, r, source, along_x).wait_send()
            return carry

        lax.fori_loop(1, nx if along_x else ny, step, 0)

    def ar_sum(phase, count):
        total = ar_in[phase, 0]
        for i in range(1, count):
            total = total + ar_in[phase, i]
        return total

    source0 = lambda other: ar_out.at[other]
    source1 = lambda other: ar_part.at[0]
    source2 = lambda other: ar_part.at[1]
    ar_in[0, gy] = ar_out[gy]
    ar_start(0, source0, False)

    skip_mix(grad, base, 2, 0)
    copies4b = send_next(3, 1, mix(gather_sum(2, 1, parts1, copies3b), weights_back))

    skip_mix(grad, base, 2, 1)

    ar_wait(0, source0, False)
    total = ar_sum(0, ny)
    ar_part[0] = total
    ar_in[1, gx] = total
    ar_start(1, source1, True)

    def last(half, copies):
        lines[half] = dot3(split(gather_wide(3, half, copies)), bank(), NT)

        def column(index, carry):
            rows = pl.multiple_of(index * 8, 8)
            walk = synthesis_column(lines.at[half], rows)
            for x in range(CELLS):
                value = walk.get(0, x) + base[half, cells(x, rows), :]
                out[2 * half, x, pl.ds(rows, 8), :] = value[:, :CELLS]
                out[2 * half + 1, x, pl.ds(rows, 8), :] = value[:, 64 : 64 + CELLS]
            return carry

        lax.fori_loop(0, 4, column, 0)
        store = pltpu.make_async_copy(out.at[halves[half]], out_hbm.at[halves[half]], out_sems.at[half])
        store.start()
        return store

    store0 = last(0, copies4a)

    ar_wait(1, source1, True)
    total = ar_sum(1, nx)
    ar_part[1] = total
    ar_in[2, gy] = total
    ar_start(2, source2, False)

    store1 = last(1, copies4b)

    for copies in (copies1a, copies1b, copies2a, copies2b, copies3a, copies3b, copies4a, copies4b):
        for copy in copies:
            copy.wait_send()
    ar_wait_send(0, source0, False)
    ar_wait_send(1, source1, True)

    ar_wait(2, source2, False)
    scale = F32(1.0 / (BATCH * CELLS * CELLS * nx * ny))
    for i in range(ny):
        sum_ref[i * chunk : (i + 1) * chunk] = ar_in[2, i] * scale
    ar_wait_send(2, source2, False)
    store0.wait()
    store1.wait()


def shards(nx, ny, field, w_coarse, w_detail, w_skip, cotangent):
    block = (BATCH, CELLS, CH, CELLS)
    packed = pltpu.VMEM((2, CELLS * CH, 128), F32)
    hbm = pl.BlockSpec(memory_space=pl.ANY)
    weight = pltpu.VMEM((CH, CH), F32)
    peers = max(nx, ny)
    chunk = CH // ny
    grad_field, summed = pl.pallas_call(
        functools.partial(kernel, nx, ny),
        out_shape=(jax.ShapeDtypeStruct(block, F32), jax.ShapeDtypeStruct((CH, 128), F32)),
        in_specs=[hbm] * 6,
        out_specs=(hbm, pl.BlockSpec(memory_space=pltpu.VMEM)),
        scratch_shapes=[
            pltpu.VMEM(block, F32),
            pltpu.VMEM(block, F32),
            packed,
            packed,
            packed,
            packed,
            packed,
            pltpu.VMEM((2, 2 * ROWS, 512), F32),
            pltpu.VMEM((4, 256, 256), F32),
            weight,
            weight,
            weight,
            pltpu.VMEM((512, 256), F32),
            pltpu.VMEM((2, 512, 256), BF16),
            pltpu.VMEM((2, 2, 3, ROWS, 128), F32),
            pltpu.VMEM((2, 2, ROWS, 128), F32),
            pltpu.VMEM((4, 2, 3, ROWS, 128), F32),
            pltpu.VMEM((2, 2 * ROWS, 256), F32),
            pltpu.VMEM(block, F32),
            pltpu.VMEM((ny, chunk, 128), F32),
            pltpu.VMEM((3, peers, chunk, 128), F32),
            pltpu.VMEM((2, chunk, 128), F32),
            pltpu.VMEM((CH, 128), F32),
            pltpu.SemaphoreType.DMA((8,)),
            pltpu.SemaphoreType.DMA((2,)),
            pltpu.SemaphoreType.DMA((4, 2, 3)),
            pltpu.SemaphoreType.DMA((4, 2, 3)),
            pltpu.SemaphoreType.DMA((3, peers)),
            pltpu.SemaphoreType.DMA((3, peers)),
        ],
        compiler_params=pltpu.CompilerParams(
            collective_id=0, has_side_effects=True, vmem_limit_bytes=60 * 1024 * 1024
        ),
    )(
        jnp.transpose(field, (0, 1, 3, 2)),
        jnp.transpose(cotangent, (0, 1, 3, 2)),
        w_coarse,
        w_detail,
        w_skip,
        jnp.asarray(bank_matrix()),
    )
    return (
        jnp.transpose(grad_field, (0, 1, 3, 2)),
        summed[:, :CH],
        summed[:, CH : 2 * CH],
        summed[:, 2 * CH : 3 * CH],
    )


def solution(mesh):
    nx, ny = mesh.shape["gx"], mesh.shape["gy"]
    in_specs = (P(None, "gx", "gy", None), P(), P(), P(), P(None, "gx", "gy", None))
    out_specs = (P(None, "gx", "gy", None), P(), P(), P())

    def run(*args):
        return shards(nx, ny, *args)

    return jax.shard_map(run, mesh=mesh, in_specs=in_specs, out_specs=out_specs, check_vma=False)
```

```python
import functools

import jax
import jax.numpy as jnp
import numpy as np
from jax import lax
from jax.experimental import pallas as pl
from jax.experimental.pallas import tpu as pltpu
from jax.sharding import PartitionSpec as P

LOW_TAPS = [
    0.23037781330885523,
    0.7148465705525415,
    0.6308807679295904,
    -0.02798376941698385,
    -0.18703481171888114,
    0.030841381835986965,
    0.032883011666982945,
    -0.010597401784997278,
]
HIGH_TAPS = [(-1) ** offset * LOW_TAPS[7 - offset] for offset in range(8)]

F32 = jnp.float32
BF16 = jnp.bfloat16
MESH = pl.DeviceIdType.MESH
CH = 32
BATCH = 4
CELLS = 48
COARSE = 6
ROWS = COARSE * CH // 2
GELU_A = 0.7978845608028654
GELU_B = GELU_A * 0.044715


def bounds(low, high):
    return -((7 - low) // 2), high // 2


LEVELS = [(0, CELLS - 1)]
for _ in range(3):
    LEVELS.append(bounds(*LEVELS[-1]))


def line_matrix():
    values = np.eye(CELLS)
    low, high = LEVELS[0]
    outputs = []
    for level in range(3):
        bank = [LOW_TAPS] if level < 2 else [LOW_TAPS, HIGH_TAPS]
        first, last = LEVELS[level + 1]
        outputs = []
        for taps in bank:
            result = np.zeros((last - first + 1, CELLS))
            for k in range(first, last + 1):
                for j in range(8):
                    if low <= 2 * k + j <= high:
                        result[k - first] += taps[j] * values[2 * k + j - low]
            outputs.append(result)
        values, low, high = outputs[0], first, last
    return np.stack(outputs)


def bank_matrix():
    line = line_matrix()
    result = np.zeros((2, 2, 2, 64, 2, 2, 64))
    for group in range(2):
        for xband in range(2):
            for b in range(2):
                for part in range(2):
                    for yband in range(2):
                        for k in range(COARSE):
                            lane = ((xband * 2 + yband) * COARSE + k) * 2 + b
                            result[group, xband, b, :CELLS, part, group, lane] = line[yband, part * COARSE + k]
    return result.reshape(512, 256).astype(np.float32)


def split(values):
    high = values.astype(BF16)
    return high, (values - high.astype(F32)).astype(BF16)


def dot3(left, right, dims=((1,), (0,))):
    form = (dims, ((), ()))
    rows = left[0].shape[0]
    both = lax.dot_general(jnp.concatenate(left, axis=0), right[0], form, preferred_element_type=F32)
    return both[:rows] + both[rows:] + lax.dot_general(left[0], right[1], form, preferred_element_type=F32)


NT = ((1,), (1,))


class Analysis:
    def __init__(self, load):
        self.load = load
        self.memo = {}

    def get(self, level, k, taps=LOW_TAPS, band=0):
        if level == 0:
            if (0, k) not in self.memo:
                self.memo[0, k] = self.load(k)
            return self.memo[0, k]
        key = (level, k, band)
        if key not in self.memo:
            low, high = LEVELS[level - 1]
            total = None
            for j in range(8):
                if low <= 2 * k + j <= high:
                    term = self.get(level - 1, 2 * k + j) * F32(taps[j])
                    total = term if total is None else total + term
            self.memo[key] = total
        return self.memo[key]


class Synthesis:
    def __init__(self, load):
        self.load = load
        self.memo = {}

    def top(self, band, k):
        if (band, k) not in self.memo:
            self.memo[band, k] = self.load(band, k)
        return self.memo[band, k]

    def get(self, level, i):
        key = (level, i, "s")
        if key not in self.memo:
            low, high = LEVELS[level + 1]
            total = None
            for k in range(low, high + 1):
                j = i - 2 * k
                if 0 <= j < 8:
                    if level == 2:
                        term = self.top(0, k) * F32(LOW_TAPS[j]) + self.top(1, k) * F32(HIGH_TAPS[j])
                    else:
                        term = self.get(level + 1, k) * F32(LOW_TAPS[j])
                    total = term if total is None else total + term
            self.memo[key] = total
        return self.memo[key]


def synthesis_column(lines, rows):
    def load(band, k):
        part, group, row = (k + COARSE) // 6, (k + COARSE) % 6 // 3, (k + COARSE) % 3
        start = (part * 3 + row) * CH
        lanes = group * 256 + band * 128
        return lines[pl.ds(pl.multiple_of(start + rows, 8), 8), lanes : lanes + 128]

    return Synthesis(load)


def analyze_column(lines, rows, load):
    walk = Analysis(load)
    for k in range(-COARSE, COARSE):
        part, group, row = (k + COARSE) // 6, (k + COARSE) % 6 // 3, (k + COARSE) % 3
        start = (part * 3 + row) * CH
        for band, taps in enumerate((LOW_TAPS, HIGH_TAPS)):
            lanes = group * 256 + band * 128
            lines[pl.ds(pl.multiple_of(start + rows, 8), 8), lanes : lanes + 128] = walk.get(3, k, taps, band)


def side_by_side(values):
    return jnp.concatenate([values[k : k + CH] for k in range(0, values.shape[0], CH)], axis=1)


def in_coarse(values):
    return lax.rem(lax.broadcasted_iota(jnp.int32, values.shape, 1), 64) < 12


def mix(values, weights):
    count, width = values.shape[0] // CH, values.shape[1]
    both = dot3(weights, split(side_by_side(values)))
    chosen = jnp.where(in_coarse(both[:CH]), both[:CH], both[CH:])
    return jnp.concatenate([chosen[:, k * width : (k + 1) * width] for k in range(count)], axis=0)


def pack(source, target, half):
    for pair in range(2):
        values = source[2 * half + pair].reshape(CELLS * CH, CELLS)
        target[half, :, 64 * pair : 64 * pair + CELLS] = values


def kernel(
    nx, ny, field_hbm, cot_hbm, wc_hbm, wd_hbm, ws_hbm, bank_hbm, back_hbm, packed_hbm, sum_hbm,
    raw, raw_cot, field, cot, grad, skip, base, lines, kron, wc_ref, wd_ref, ws_ref, bank_ref, bank_parts, back_ref, back_parts,
    send_fwd, send_mix, recv, wide, packed, ar_out, ar_in, ar_part, gsum,
    in_sems, out_sems, ex_send, ex_recv, ar_send, ar_recv,
):
    gx = lax.axis_index("gx")
    gy = lax.axis_index("gy")
    right, left = lax.rem(gx + 1, nx), lax.rem(gx + nx - 1, nx)
    up, down = lax.rem(gy + 1, ny), lax.rem(gy + ny - 1, ny)

    halves = [pl.ds(0, 2), pl.ds(2, 2)]
    moves = [
        (field_hbm.at[halves[0]], raw.at[halves[0]]),
        (bank_hbm, bank_ref),
        (field_hbm.at[halves[1]], raw.at[halves[1]]),
        (wc_hbm, wc_ref),
        (wd_hbm, wd_ref),
        (ws_hbm, ws_ref),
        (back_hbm, back_ref),
        (cot_hbm.at[halves[0]], raw_cot.at[halves[0]]),
        (cot_hbm.at[halves[1]], raw_cot.at[halves[1]]),
    ]
    loads = [pltpu.make_async_copy(source, target, in_sems.at[i]) for i, (source, target) in enumerate(moves)]
    for load in loads:
        load.start()

    barrier = pltpu.get_barrier_semaphore()

    across, cores = 4 if nx % 4 == 0 else nx, 2
    near, far = across * cores, (nx // across) * (ny // cores)
    my_x, my_y = lax.rem(gx, across), lax.div(gx, across)
    my_core, my_z = lax.rem(gy, cores), lax.div(gy, cores)
    near_me = my_x * cores + my_core
    far_me = my_y * (ny // cores) + my_z

    def near_device(other):
        return my_y * across + lax.div(other, cores), my_z * cores + lax.rem(other, cores)

    def far_device(other):
        depth = ny // cores
        return lax.div(other, depth) * across + my_x, lax.rem(other, depth) * cores + my_core

    def greet(device):
        pl.semaphore_signal(barrier, inc=1, device_id=device, device_id_type=MESH)

    def greet_near(r, carry):
        greet(near_device(lax.rem(near_me + r, near)))
        return carry

    def greet_far(r, carry):
        greet(far_device(lax.rem(far_me + r, far)))
        return carry

    for device in ((right, gy), (left, gy), (gx, up), (gx, down), (right, up), (left, down)):
        greet(device)
    lax.fori_loop(1, near, greet_near, 0)
    lax.fori_loop(1, far, greet_far, 0)

    field[...] = jnp.zeros(field.shape, F32)
    cot[...] = jnp.zeros(cot.shape, F32)
    kron[...] = jnp.zeros(kron.shape, F32)

    def bank():
        return bank_parts[0], bank_parts[1]

    def bank_back():
        return back_parts[0], back_parts[1]

    def exchange(step, half, sources, devices):
        copies = []
        for slot, (source, device) in enumerate(zip(sources, devices)):
            copy = pltpu.make_async_remote_copy(
                src_ref=source,
                dst_ref=recv.at[step, half, slot],
                send_sem=ex_send.at[step, half, slot],
                recv_sem=ex_recv.at[step, half, slot],
                device_id=device,
                device_id_type=MESH,
            )
            copy.start()
            copies.append(copy)
        return copies

    back_devices = [(left, gy), (gx, down), (left, down)]
    next_devices = [(right, gy), (gx, up), (right, up)]

    def send_partials(step, half):
        parts = dot3(split(lines[half]), bank())
        out_refs = send_fwd.at[step // 2, half]
        out_refs[0] = parts[:ROWS, 128:]
        out_refs[1] = parts[ROWS:, :128]
        out_refs[2] = parts[:ROWS, :128]
        return parts, exchange(step, half, [out_refs.at[s] for s in range(3)], back_devices)

    def gather_sum(step, half, parts, copies):
        total = parts[ROWS:, 128:]
        for slot, copy in enumerate(copies):
            copy.wait_recv()
            total = total + recv[step, half, slot]
        return total

    def send_next(step, half, values):
        send_mix[step // 2, half] = values
        return exchange(step, half, [send_mix.at[step // 2, half]] * 3, next_devices)

    def gather_wide(step, half, copies):
        for copy in copies:
            copy.wait_recv()
        before = jnp.concatenate([recv[step, half, 2], recv[step, half, 0]], axis=1)
        own = jnp.concatenate([recv[step, half, 1], send_mix[step // 2, half]], axis=1)
        return jnp.concatenate([before, own], axis=0)

    def cells(x, rows):
        return pl.ds(pl.multiple_of(x * CH + rows, 8), 8)

    def first(half):
        pack(raw, field, half)

        def column(index, carry):
            rows = pl.multiple_of(index * 8, 8)
            analyze_column(lines.at[half], rows, lambda x: field[half, cells(x, rows), :])
            return carry

        lax.fori_loop(0, 4, column, 0)

    loads[1].wait()
    bank_parts[0], bank_parts[1] = split(bank_ref[...])
    loads[0].wait()
    first(0)
    pl.semaphore_wait(barrier, near + far + 4)
    parts0, copies1a = send_partials(0, 0)
    loads[2].wait()
    first(1)
    parts1, copies1b = send_partials(0, 1)

    eye = (
        lax.broadcasted_iota(jnp.int32, (CH, CH), 0) == lax.broadcasted_iota(jnp.int32, (CH, CH), 1)
    ).astype(BF16)

    def transposed(weight):
        form = (NT, ((), ()))
        return lax.dot_general(eye, weight, form, preferred_element_type=F32).astype(BF16)

    for load in loads[3:7]:
        load.wait()
    back_parts[0], back_parts[1] = split(back_ref[...])
    coarse_parts = split(wc_ref[...])
    detail_parts = split(wd_ref[...])
    skip_parts = split(ws_ref[...])
    weights_forward = tuple(
        jnp.concatenate([transposed(c), transposed(d)], axis=0) for c, d in zip(coarse_parts, detail_parts)
    )
    weights_back = tuple(jnp.concatenate([c, d], axis=0) for c, d in zip(coarse_parts, detail_parts))

    for which in range(2):
        forward = transposed(skip_parts[which]).astype(F32)
        backward = skip_parts[which].astype(F32)
        for i in range(8):
            block = slice(i * CH, (i + 1) * CH)
            kron[which, block, block] = forward
            kron[2 + which, block, block] = backward

    def skip_mix(source, target, kind, half):
        weights = (kron[kind].astype(BF16), kron[kind + 1].astype(BF16))
        for g in range(6):
            block = slice(256 * g, 256 * g + 256)
            target[half, block] = dot3(weights, split(source[half, block]))

    skip_mix(field, skip, 0, 0)
    loads[7].wait()
    pack(raw_cot, cot, 0)

    copies2a = send_next(1, 0, gather_sum(0, 0, parts0, copies1a))

    loads[8].wait()
    pack(raw_cot, cot, 1)

    copies2b = send_next(1, 1, gather_sum(0, 1, parts1, copies1b))

    skip_mix(field, skip, 0, 1)

    def middle(half, copies):
        values = gather_wide(1, half, copies)
        wide[half] = values
        lines[half] = dot3(split(mix(values, weights_forward)), bank_back())

        def column(index, carry):
            rows = pl.multiple_of(index * 8, 8)
            walk = synthesis_column(lines.at[half], rows)

            def load(x):
                here = cells(x, rows)
                pre = walk.get(0, x) + skip[half, here, :]
                cube = F32(GELU_B) * (pre * pre)
                tanh = jnp.tanh(pre * (F32(GELU_A) + cube))
                slope = pre * (F32(GELU_A) + F32(3.0) * cube)
                rise = (F32(0.5) + F32(0.5) * tanh) * (F32(1.0) + (slope - slope * tanh))
                value = cot[half, here, :] * rise
                grad[half, here, :] = value
                return value

            analyze_column(lines.at[half], rows, load)
            return carry

        lax.fori_loop(0, 4, column, 0)
        return send_partials(2, half)

    parts0, copies3a = middle(0, copies2a)
    parts1, copies3b = middle(1, copies2b)

    def share(half, parts):
        flat = side_by_side(parts)
        coarse = in_coarse(flat)
        masked = jnp.concatenate([jnp.where(coarse, flat, 0.0), jnp.where(coarse, 0.0, flat)], axis=0)
        both = dot3(split(side_by_side(wide[half])), split(masked), NT)
        pair = jnp.zeros((256, 256), F32)
        for g in range(6):
            block = slice(256 * g, 256 * g + 256)
            pair = pair + dot3(split(field[half, block]), split(grad[half, block]), NT)
        return both, pair

    both0, pair0 = share(0, parts0)
    both1, pair1 = share(1, parts1)

    pair = pair0 + pair1
    skip_sum = pair[:CH, :CH]
    for i in range(1, 8):
        block = slice(i * CH, (i + 1) * CH)
        skip_sum = skip_sum + pair[block, block]
    gsum[...] = jnp.zeros((CH, 128), F32)
    gsum[:, :64] = both0 + both1
    gsum[:, 64:96] = skip_sum

    chunk = CH // near
    for i in range(near):
        ar_out[i] = gsum[i * chunk : (i + 1) * chunk]

    def peer(far_round, r):
        if far_round:
            other = lax.rem(far_me + r, far)
            return other, far_device(other)
        other = lax.rem(near_me + r, near)
        return other, near_device(other)

    def ar_copy(phase, r, source):
        other, device = peer(phase == 1, r)
        me = far_me if phase == 1 else near_me
        return pltpu.make_async_remote_copy(
            src_ref=source(other),
            dst_ref=ar_in.at[phase, me],
            send_sem=ar_send.at[phase, r],
            recv_sem=ar_recv.at[phase, me],
            device_id=device,
            device_id_type=MESH,
        )

    def ar_each(phase, action):
        def step(r, carry):
            action(r)
            return carry

        lax.fori_loop(1, far if phase == 1 else near, step, 0)

    def ar_start(phase, source):
        ar_each(phase, lambda r: ar_copy(phase, r, source).start())

    def ar_wait(phase):
        def action(r):
            other, _ = peer(phase == 1, r)
            arrived = ar_in.at[phase, other]
            pltpu.make_async_copy(arrived, arrived, ar_recv.at[phase, other]).wait()

        ar_each(phase, action)

    def ar_wait_send(phase, source):
        ar_each(phase, lambda r: ar_copy(phase, r, source).wait_send())

    def ar_sum(phase, count):
        total = ar_in[phase, 0]
        for i in range(1, count):
            total = total + ar_in[phase, i]
        return total

    source0 = lambda other: ar_out.at[other]
    source1 = lambda other: ar_part.at[0]
    source2 = lambda other: ar_part.at[1]
    ar_in[0, near_me] = ar_out[near_me]
    ar_start(0, source0)

    copies4a = send_next(3, 0, mix(gather_sum(2, 0, parts0, copies3a), weights_back))
    skip_mix(grad, base, 2, 0)

    ar_wait(0)
    total = ar_sum(0, near)
    ar_part[0] = total
    ar_in[1, far_me] = total
    ar_start(1, source1)

    copies4b = send_next(3, 1, mix(gather_sum(2, 1, parts1, copies3b), weights_back))

    skip_mix(grad, base, 2, 1)

    def last(half, copies):
        lines[half] = dot3(split(gather_wide(3, half, copies)), bank_back())

        def column(index, carry):
            rows = pl.multiple_of(index * 8, 8)
            walk = synthesis_column(lines.at[half], rows)
            for x in range(CELLS):
                packed[half, cells(x, rows), :] = walk.get(0, x) + base[half, cells(x, rows), :]
            return carry

        lax.fori_loop(0, 4, column, 0)
        store = pltpu.make_async_copy(packed.at[half], packed_hbm.at[half], out_sems.at[half])
        store.start()
        return store

    store0 = last(0, copies4a)
    store1 = last(1, copies4b)

    ar_wait(1)
    total = ar_sum(1, far)
    ar_part[1] = total
    ar_in[2, near_me] = total
    ar_start(2, source2)

    for copies in (copies1a, copies1b, copies2a, copies2b, copies3a, copies3b, copies4a, copies4b):
        for copy in copies:
            copy.wait_send()
    ar_wait_send(0, source0)
    ar_wait_send(1, source1)
    store0.wait()
    store1.wait()

    ar_wait(2)
    scale = F32(1.0 / (BATCH * CELLS * CELLS * nx * ny))
    for i in range(near):
        gsum[i * chunk : (i + 1) * chunk] = ar_in[2, i] * scale
    store = pltpu.make_async_copy(gsum, sum_hbm, out_sems.at[2])
    store.start()
    ar_wait_send(2, source2)
    store.wait()


def unpack_kernel(packed_hbm, sum_hbm, out_hbm, gc_ref, gd_ref, gs_ref, packed, summed, out, in_sems, out_sems):
    cells = CELLS // 2
    rows = cells * CH
    loads = []
    for half in range(2):
        for part in range(2):
            here = pl.ds(part * rows, rows)
            loads.append(
                pltpu.make_async_copy(
                    packed_hbm.at[half, here], packed.at[half, here], in_sems.at[2 * half + part]
                )
            )
    loads.append(pltpu.make_async_copy(sum_hbm, summed, in_sems.at[4]))
    for load in loads:
        load.start()
    stores = []
    for half in range(2):
        for part in range(2):
            loads[2 * half + part].wait()
            values = packed[half, part * rows : (part + 1) * rows]
            there = slice(part * cells, (part + 1) * cells)
            for pair in range(2):
                lanes = slice(64 * pair, 64 * pair + CELLS)
                out[2 * half + pair, there] = values[:, lanes].reshape(cells, CH, CELLS)
            target = (pl.ds(2 * half, 2), pl.ds(part * cells, cells))
            store = pltpu.make_async_copy(out.at[target], out_hbm.at[target], out_sems.at[2 * half + part])
            store.start()
            stores.append(store)
    loads[4].wait()
    gc_ref[...] = summed[:, :CH]
    gd_ref[...] = summed[:, CH : 2 * CH]
    gs_ref[...] = summed[:, 2 * CH : 3 * CH]
    for store in stores:
        store.wait()


def shards(nx, ny, field, w_coarse, w_detail, w_skip, cotangent):
    block = (BATCH, CELLS, CH, CELLS)
    packed = pltpu.VMEM((2, CELLS * CH, 128), F32)
    hbm = pl.BlockSpec(memory_space=pl.ANY)
    vmem = pl.BlockSpec(memory_space=pltpu.VMEM)
    weight = pltpu.VMEM((CH, CH), F32)
    small = jax.ShapeDtypeStruct((CH, CH), F32)
    near = 2 * (4 if nx % 4 == 0 else nx)
    peers = max(near, nx * ny // near)
    chunk = CH // near
    bank = bank_matrix()
    result, summed = pl.pallas_call(
        functools.partial(kernel, nx, ny),
        out_shape=(
            jax.ShapeDtypeStruct((2, CELLS * CH, 128), F32),
            jax.ShapeDtypeStruct((CH, 128), F32),
        ),
        in_specs=[hbm] * 7,
        out_specs=(hbm, hbm),
        scratch_shapes=[
            pltpu.VMEM(block, F32),
            pltpu.VMEM(block, F32),
            packed,
            packed,
            packed,
            packed,
            packed,
            pltpu.VMEM((2, 2 * ROWS, 512), F32),
            pltpu.VMEM((4, 256, 256), F32),
            weight,
            weight,
            weight,
            pltpu.VMEM((512, 256), F32),
            pltpu.VMEM((2, 512, 256), BF16),
            pltpu.VMEM((256, 512), F32),
            pltpu.VMEM((2, 256, 512), BF16),
            pltpu.VMEM((2, 2, 3, ROWS, 128), F32),
            pltpu.VMEM((2, 2, ROWS, 128), F32),
            pltpu.VMEM((4, 2, 3, ROWS, 128), F32),
            pltpu.VMEM((2, 2 * ROWS, 256), F32),
            packed,
            pltpu.VMEM((near, chunk, 128), F32),
            pltpu.VMEM((3, peers, chunk, 128), F32),
            pltpu.VMEM((2, chunk, 128), F32),
            pltpu.VMEM((CH, 128), F32),
            pltpu.SemaphoreType.DMA((9,)),
            pltpu.SemaphoreType.DMA((3,)),
            pltpu.SemaphoreType.DMA((4, 2, 3)),
            pltpu.SemaphoreType.DMA((4, 2, 3)),
            pltpu.SemaphoreType.DMA((3, peers)),
            pltpu.SemaphoreType.DMA((3, peers)),
        ],
        compiler_params=pltpu.CompilerParams(
            collective_id=0, has_side_effects=True, vmem_limit_bytes=60 * 1024 * 1024
        ),
    )(
        jnp.transpose(field, (0, 1, 3, 2)),
        jnp.transpose(cotangent, (0, 1, 3, 2)),
        w_coarse,
        w_detail,
        w_skip,
        jnp.asarray(bank),
        jnp.asarray(np.ascontiguousarray(bank.T)),
    )
    grad_field, *grads = pl.pallas_call(
        unpack_kernel,
        out_shape=(jax.ShapeDtypeStruct(block, F32), small, small, small),
        in_specs=[hbm, hbm],
        out_specs=(hbm, vmem, vmem, vmem),
        scratch_shapes=[
            packed,
            pltpu.VMEM((CH, 128), F32),
            pltpu.VMEM(block, F32),
            pltpu.SemaphoreType.DMA((5,)),
            pltpu.SemaphoreType.DMA((4,)),
        ],
        compiler_params=pltpu.CompilerParams(vmem_limit_bytes=60 * 1024 * 1024),
    )(result, summed)
    return (jnp.transpose(grad_field, (0, 1, 3, 2)), *grads)


def solution(mesh):
    nx, ny = mesh.shape["gx"], mesh.shape["gy"]
    in_specs = (P(None, "gx", "gy", None), P(), P(), P(), P(None, "gx", "gy", None))
    out_specs = (P(None, "gx", "gy", None), P(), P(), P())

    def run(*args):
        return shards(nx, ny, *args)

    return jax.shard_map(run, mesh=mesh, in_specs=in_specs, out_specs=out_specs, check_vma=False)
```

```python
import functools

import jax
import jax.numpy as jnp
import numpy as np
from jax import lax
from jax.experimental import pallas as pl
from jax.experimental.pallas import tpu as pltpu
from jax.sharding import PartitionSpec as P

LOW_TAPS = [
    0.23037781330885523,
    0.7148465705525415,
    0.6308807679295904,
    -0.02798376941698385,
    -0.18703481171888114,
    0.030841381835986965,
    0.032883011666982945,
    -0.010597401784997278,
]
HIGH_TAPS = [(-1) ** offset * LOW_TAPS[7 - offset] for offset in range(8)]

F32 = jnp.float32
BF16 = jnp.bfloat16
MESH = pl.DeviceIdType.MESH
CH = 32
BATCH = 4
CELLS = 48
COARSE = 6
ROWS = COARSE * CH // 2
GELU_A = 0.7978845608028654
GELU_B = GELU_A * 0.044715


def bounds(low, high):
    return -((7 - low) // 2), high // 2


LEVELS = [(0, CELLS - 1)]
for _ in range(3):
    LEVELS.append(bounds(*LEVELS[-1]))


def line_matrix():
    values = np.eye(CELLS)
    low, high = LEVELS[0]
    outputs = []
    for level in range(3):
        bank = [LOW_TAPS] if level < 2 else [LOW_TAPS, HIGH_TAPS]
        first, last = LEVELS[level + 1]
        outputs = []
        for taps in bank:
            result = np.zeros((last - first + 1, CELLS))
            for k in range(first, last + 1):
                for j in range(8):
                    if low <= 2 * k + j <= high:
                        result[k - first] += taps[j] * values[2 * k + j - low]
            outputs.append(result)
        values, low, high = outputs[0], first, last
    return np.stack(outputs)


def bank_matrix():
    line = line_matrix()
    result = np.zeros((2, 2, 2, 64, 2, 2, 64))
    for group in range(2):
        for xband in range(2):
            for b in range(2):
                for part in range(2):
                    for yband in range(2):
                        for k in range(COARSE):
                            lane = ((xband * 2 + yband) * COARSE + k) * 2 + b
                            result[group, xband, b, :CELLS, part, group, lane] = line[yband, part * COARSE + k]
    return result.reshape(512, 256).astype(np.float32)


def split(values):
    high = values.astype(BF16)
    return high, (values - high.astype(F32)).astype(BF16)


def dot3(left, right, dims=((1,), (0,))):
    form = (dims, ((), ()))
    rows = left[0].shape[0]
    both = lax.dot_general(jnp.concatenate(left, axis=0), right[0], form, preferred_element_type=F32)
    return both[:rows] + both[rows:] + lax.dot_general(left[0], right[1], form, preferred_element_type=F32)


NT = ((1,), (1,))


class Analysis:
    def __init__(self, load):
        self.load = load
        self.memo = {}

    def get(self, level, k, taps=LOW_TAPS, band=0):
        if level == 0:
            if (0, k) not in self.memo:
                self.memo[0, k] = self.load(k)
            return self.memo[0, k]
        key = (level, k, band)
        if key not in self.memo:
            low, high = LEVELS[level - 1]
            total = None
            for j in range(8):
                if low <= 2 * k + j <= high:
                    term = self.get(level - 1, 2 * k + j) * F32(taps[j])
                    total = term if total is None else total + term
            self.memo[key] = total
        return self.memo[key]


class Synthesis:
    def __init__(self, load):
        self.load = load
        self.memo = {}

    def top(self, band, k):
        if (band, k) not in self.memo:
            self.memo[band, k] = self.load(band, k)
        return self.memo[band, k]

    def get(self, level, i):
        key = (level, i, "s")
        if key not in self.memo:
            low, high = LEVELS[level + 1]
            total = None
            for k in range(low, high + 1):
                j = i - 2 * k
                if 0 <= j < 8:
                    if level == 2:
                        term = self.top(0, k) * F32(LOW_TAPS[j]) + self.top(1, k) * F32(HIGH_TAPS[j])
                    else:
                        term = self.get(level + 1, k) * F32(LOW_TAPS[j])
                    total = term if total is None else total + term
            self.memo[key] = total
        return self.memo[key]


def synthesis_column(lines, rows):
    def load(band, k):
        part, group, row = (k + COARSE) // 6, (k + COARSE) % 6 // 3, (k + COARSE) % 3
        start = (part * 3 + row) * CH
        lanes = group * 256 + band * 128
        return lines[pl.ds(pl.multiple_of(start + rows, 8), 8), lanes : lanes + 128]

    return Synthesis(load)


def analyze_column(lines, rows, load):
    walk = Analysis(load)
    for k in range(-COARSE, COARSE):
        part, group, row = (k + COARSE) // 6, (k + COARSE) % 6 // 3, (k + COARSE) % 3
        start = (part * 3 + row) * CH
        for band, taps in enumerate((LOW_TAPS, HIGH_TAPS)):
            lanes = group * 256 + band * 128
            lines[pl.ds(pl.multiple_of(start + rows, 8), 8), lanes : lanes + 128] = walk.get(3, k, taps, band)


def side_by_side(values):
    return jnp.concatenate([values[k : k + CH] for k in range(0, values.shape[0], CH)], axis=1)


def in_coarse(values):
    return lax.rem(lax.broadcasted_iota(jnp.int32, values.shape, 1), 64) < 12


def mix(values, weights):
    count, width = values.shape[0] // CH, values.shape[1]
    both = dot3(weights, split(side_by_side(values)))
    chosen = jnp.where(in_coarse(both[:CH]), both[:CH], both[CH:])
    return jnp.concatenate([chosen[:, k * width : (k + 1) * width] for k in range(count)], axis=0)


def pack(source, target, half):
    for pair in range(2):
        values = source[2 * half + pair].reshape(CELLS * CH, CELLS)
        target[half, :, 64 * pair : 64 * pair + CELLS] = values


def kernel(
    nx, ny, field_hbm, cot_hbm, wc_hbm, wd_hbm, ws_hbm, bank_hbm, back_hbm, packed_hbm, sum_hbm,
    raw, raw_cot, field, cot, grad, skip, base, lines, kron, wc_ref, wd_ref, ws_ref, bank_ref, bank_parts, back_ref, back_parts,
    send_fwd, send_mix, recv_sum, recv_next, wide, packed, ar_out, ar_in, ar_part, gsum,
    in_sems, out_sems, ex_send, ex_recv, ar_send, ar_recv,
):
    gx = lax.axis_index("gx")
    gy = lax.axis_index("gy")
    right, left = lax.rem(gx + 1, nx), lax.rem(gx + nx - 1, nx)
    up, down = lax.rem(gy + 1, ny), lax.rem(gy + ny - 1, ny)

    halves = [pl.ds(0, 2), pl.ds(2, 2)]
    moves = [
        (field_hbm.at[halves[0]], raw.at[halves[0]]),
        (bank_hbm, bank_ref),
        (field_hbm.at[halves[1]], raw.at[halves[1]]),
        (wc_hbm, wc_ref),
        (wd_hbm, wd_ref),
        (ws_hbm, ws_ref),
        (back_hbm, back_ref),
        (cot_hbm.at[halves[0]], raw_cot.at[halves[0]]),
        (cot_hbm.at[halves[1]], raw_cot.at[halves[1]]),
    ]
    loads = [pltpu.make_async_copy(source, target, in_sems.at[i]) for i, (source, target) in enumerate(moves)]
    for load in loads:
        load.start()

    barrier = pltpu.get_barrier_semaphore()

    across, cores = 4 if nx % 4 == 0 else nx, 2
    near, far = across * cores, (nx // across) * (ny // cores)
    my_x, my_y = lax.rem(gx, across), lax.div(gx, across)
    my_core, my_z = lax.rem(gy, cores), lax.div(gy, cores)
    near_me = my_x * cores + my_core
    far_me = my_y * (ny // cores) + my_z

    def near_device(other):
        return my_y * across + lax.div(other, cores), my_z * cores + lax.rem(other, cores)

    def far_device(other):
        depth = ny // cores
        return lax.div(other, depth) * across + my_x, lax.rem(other, depth) * cores + my_core

    def greet(device):
        pl.semaphore_signal(barrier, inc=1, device_id=device, device_id_type=MESH)

    def greet_near(r, carry):
        greet(near_device(lax.rem(near_me + r, near)))
        return carry

    def greet_far(r, carry):
        greet(far_device(lax.rem(far_me + r, far)))
        return carry

    for device in ((right, gy), (left, gy), (gx, up), (gx, down)):
        greet(device)
    for device in ((right, up), (left, down), (right, down), (left, up)):
        greet(device)
    lax.fori_loop(1, near, greet_near, 0)
    lax.fori_loop(1, far, greet_far, 0)

    field[...] = jnp.zeros(field.shape, F32)
    cot[...] = jnp.zeros(cot.shape, F32)
    kron[...] = jnp.zeros(kron.shape, F32)

    def bank():
        return bank_parts[0], bank_parts[1]

    def bank_back():
        return back_parts[0], back_parts[1]

    def exchange(step, half, moves):
        copies = []
        for slot, (source, target, device) in enumerate(moves):
            copy = pltpu.make_async_remote_copy(
                src_ref=source,
                dst_ref=target,
                send_sem=ex_send.at[step, half, slot],
                recv_sem=ex_recv.at[step, half, slot],
                device_id=device,
                device_id_type=MESH,
            )
            copy.start()
            copies.append(copy)
        return copies

    def send_partials(step, half):
        parts = dot3(split(lines[half]), bank())
        before, own = send_fwd.at[step // 2, half, 0], send_fwd.at[step // 2, half, 1]
        before[...] = parts[:, :128]
        own[...] = parts[:, 128:]
        arrived = recv_sum.at[step // 2, half]
        first, second = pl.ds(0, ROWS), pl.ds(ROWS, ROWS)
        moves = [
            (before.at[first], arrived.at[pl.ds(0, ROWS)], (left, down)),
            (before.at[second], arrived.at[pl.ds(ROWS, ROWS)], (right, down)),
            (own.at[first], arrived.at[pl.ds(2 * ROWS, ROWS)], (left, gy)),
            (own.at[second], arrived.at[pl.ds(3 * ROWS, ROWS)], (right, gy)),
            (before, arrived.at[pl.ds(4 * ROWS, 2 * ROWS)], (gx, down)),
        ]
        return parts, exchange(step, half, moves)

    def gather_sum(step, half, parts, copies):
        for copy in copies:
            copy.wait_recv()
        arrived = recv_sum[step // 2, half]
        total = parts[:, 128:] + arrived[4 * ROWS :]
        above = arrived[ROWS : 2 * ROWS] + arrived[3 * ROWS : 4 * ROWS]
        below = arrived[:ROWS] + arrived[2 * ROWS : 3 * ROWS]
        return total + jnp.concatenate([above, below], axis=0)

    def send_next(step, half, values):
        send_mix[step // 2, half] = values
        return exchange(step, half, [(send_mix.at[step // 2, half], recv_next.at[step // 2, half], (gx, up))])

    def gather_wide(step, half, copies):
        for copy in copies:
            copy.wait_recv()
        return jnp.concatenate([recv_next[step // 2, half], send_mix[step // 2, half]], axis=1)

    def cells(x, rows):
        return pl.ds(pl.multiple_of(x * CH + rows, 8), 8)

    def first(half):
        pack(raw, field, half)

        def column(index, carry):
            rows = pl.multiple_of(index * 8, 8)
            analyze_column(lines.at[half], rows, lambda x: field[half, cells(x, rows), :])
            return carry

        lax.fori_loop(0, 4, column, 0)

    loads[1].wait()
    bank_parts[0], bank_parts[1] = split(bank_ref[...])
    loads[0].wait()
    first(0)
    pl.semaphore_wait(barrier, near + far + 6)
    parts0, copies1a = send_partials(0, 0)
    loads[2].wait()
    first(1)
    parts1, copies1b = send_partials(0, 1)

    eye = (
        lax.broadcasted_iota(jnp.int32, (CH, CH), 0) == lax.broadcasted_iota(jnp.int32, (CH, CH), 1)
    ).astype(BF16)

    def transposed(weight):
        form = (NT, ((), ()))
        return lax.dot_general(eye, weight, form, preferred_element_type=F32).astype(BF16)

    for load in loads[3:7]:
        load.wait()
    back_parts[0], back_parts[1] = split(back_ref[...])
    coarse_parts = split(wc_ref[...])
    detail_parts = split(wd_ref[...])
    skip_parts = split(ws_ref[...])
    weights_forward = tuple(
        jnp.concatenate([transposed(c), transposed(d)], axis=0) for c, d in zip(coarse_parts, detail_parts)
    )
    weights_back = tuple(jnp.concatenate([c, d], axis=0) for c, d in zip(coarse_parts, detail_parts))

    for which in range(2):
        forward = transposed(skip_parts[which]).astype(F32)
        backward = skip_parts[which].astype(F32)
        for i in range(8):
            block = slice(i * CH, (i + 1) * CH)
            kron[which, block, block] = forward
            kron[2 + which, block, block] = backward

    def skip_mix(source, target, kind, half):
        weights = (kron[kind].astype(BF16), kron[kind + 1].astype(BF16))
        for g in range(6):
            block = slice(256 * g, 256 * g + 256)
            target[half, block] = dot3(weights, split(source[half, block]))

    skip_mix(field, skip, 0, 0)
    loads[7].wait()
    pack(raw_cot, cot, 0)

    copies2a = send_next(1, 0, gather_sum(0, 0, parts0, copies1a))

    loads[8].wait()
    pack(raw_cot, cot, 1)

    copies2b = send_next(1, 1, gather_sum(0, 1, parts1, copies1b))

    skip_mix(field, skip, 0, 1)

    def middle(half, copies):
        values = gather_wide(1, half, copies)
        wide[half] = values
        lines[half] = dot3(split(mix(values, weights_forward)), bank_back())

        def column(index, carry):
            rows = pl.multiple_of(index * 8, 8)
            walk = synthesis_column(lines.at[half], rows)

            def load(x):
                here = cells(x, rows)
                pre = walk.get(0, x) + skip[half, here, :]
                cube = F32(GELU_B) * (pre * pre)
                tanh = jnp.tanh(pre * (F32(GELU_A) + cube))
                slope = pre * (F32(GELU_A) + F32(3.0) * cube)
                rise = (F32(0.5) + F32(0.5) * tanh) * (F32(1.0) + (slope - slope * tanh))
                value = cot[half, here, :] * rise
                grad[half, here, :] = value
                return value

            analyze_column(lines.at[half], rows, load)
            return carry

        lax.fori_loop(0, 4, column, 0)
        return send_partials(2, half)

    parts0, copies3a = middle(0, copies2a)
    parts1, copies3b = middle(1, copies2b)

    def share(half, parts):
        flat = side_by_side(parts)
        coarse = in_coarse(flat)
        masked = jnp.concatenate([jnp.where(coarse, flat, 0.0), jnp.where(coarse, 0.0, flat)], axis=0)
        both = dot3(split(side_by_side(wide[half])), split(masked), NT)
        pair = jnp.zeros((256, 256), F32)
        for g in range(6):
            block = slice(256 * g, 256 * g + 256)
            pair = pair + dot3(split(field[half, block]), split(grad[half, block]), NT)
        return both, pair

    both0, pair0 = share(0, parts0)
    both1, pair1 = share(1, parts1)

    pair = pair0 + pair1
    skip_sum = pair[:CH, :CH]
    for i in range(1, 8):
        block = slice(i * CH, (i + 1) * CH)
        skip_sum = skip_sum + pair[block, block]
    gsum[...] = jnp.zeros((CH, 128), F32)
    gsum[:, :64] = both0 + both1
    gsum[:, 64:96] = skip_sum

    chunk = CH // near
    for i in range(near):
        ar_out[i] = gsum[i * chunk : (i + 1) * chunk]

    def peer(far_round, r):
        if far_round:
            other = lax.rem(far_me + r, far)
            return other, far_device(other)
        other = lax.rem(near_me + r, near)
        return other, near_device(other)

    def ar_copy(phase, r, source):
        other, device = peer(phase == 1, r)
        me = far_me if phase == 1 else near_me
        return pltpu.make_async_remote_copy(
            src_ref=source(other),
            dst_ref=ar_in.at[phase, me],
            send_sem=ar_send.at[phase, r],
            recv_sem=ar_recv.at[phase, me],
            device_id=device,
            device_id_type=MESH,
        )

    def ar_each(phase, action):
        def step(r, carry):
            action(r)
            return carry

        lax.fori_loop(1, far if phase == 1 else near, step, 0)

    def ar_start(phase, source):
        ar_each(phase, lambda r: ar_copy(phase, r, source).start())

    def ar_wait(phase):
        def action(r):
            other, _ = peer(phase == 1, r)
            arrived = ar_in.at[phase, other]
            pltpu.make_async_copy(arrived, arrived, ar_recv.at[phase, other]).wait()

        ar_each(phase, action)

    def ar_wait_send(phase, source):
        ar_each(phase, lambda r: ar_copy(phase, r, source).wait_send())

    def ar_sum(phase, count):
        total = ar_in[phase, 0]
        for i in range(1, count):
            total = total + ar_in[phase, i]
        return total

    source0 = lambda other: ar_out.at[other]
    source1 = lambda other: ar_part.at[0]
    source2 = lambda other: ar_part.at[1]
    ar_in[0, near_me] = ar_out[near_me]
    ar_start(0, source0)

    copies4a = send_next(3, 0, mix(gather_sum(2, 0, parts0, copies3a), weights_back))
    skip_mix(grad, base, 2, 0)

    ar_wait(0)
    total = ar_sum(0, near)
    ar_part[0] = total
    ar_in[1, far_me] = total
    ar_start(1, source1)

    copies4b = send_next(3, 1, mix(gather_sum(2, 1, parts1, copies3b), weights_back))

    skip_mix(grad, base, 2, 1)

    def last(half, copies):
        lines[half] = dot3(split(gather_wide(3, half, copies)), bank_back())

        def column(index, carry):
            rows = pl.multiple_of(index * 8, 8)
            walk = synthesis_column(lines.at[half], rows)
            for x in range(CELLS):
                packed[half, cells(x, rows), :] = walk.get(0, x) + base[half, cells(x, rows), :]
            return carry

        lax.fori_loop(0, 4, column, 0)
        store = pltpu.make_async_copy(packed.at[half], packed_hbm.at[half], out_sems.at[half])
        store.start()
        return store

    store0 = last(0, copies4a)
    store1 = last(1, copies4b)

    ar_wait(1)
    total = ar_sum(1, far)
    ar_part[1] = total
    ar_in[2, near_me] = total
    ar_start(2, source2)

    for copies in (copies1a, copies1b, copies2a, copies2b, copies3a, copies3b, copies4a, copies4b):
        for copy in copies:
            copy.wait_send()
    ar_wait_send(0, source0)
    ar_wait_send(1, source1)
    store0.wait()
    store1.wait()

    ar_wait(2)
    scale = F32(1.0 / (BATCH * CELLS * CELLS * nx * ny))
    for i in range(near):
        gsum[i * chunk : (i + 1) * chunk] = ar_in[2, i] * scale
    store = pltpu.make_async_copy(gsum, sum_hbm, out_sems.at[2])
    store.start()
    ar_wait_send(2, source2)
    store.wait()


def unpack_kernel(
    packed_hbm, sum_hbm, out_hbm, gc_hbm, gd_hbm, gs_hbm, packed, summed, grads, out, in_sems, out_sems
):
    cells = CELLS // 2
    rows = cells * CH
    loads = []
    for half in range(2):
        for part in range(2):
            here = pl.ds(part * rows, rows)
            loads.append(
                pltpu.make_async_copy(
                    packed_hbm.at[half, here], packed.at[half, here], in_sems.at[2 * half + part]
                )
            )
    loads.append(pltpu.make_async_copy(sum_hbm, summed, in_sems.at[4]))
    for load in loads[4:] + loads[:4]:
        load.start()
    stores = []
    loads[4].wait()
    for i, target in enumerate((gc_hbm, gd_hbm, gs_hbm)):
        grads[i] = summed[:, i * CH : (i + 1) * CH]
        store = pltpu.make_async_copy(grads.at[i], target, out_sems.at[4 + i])
        store.start()
        stores.append(store)
    for half in range(2):
        for part in range(2):
            loads[2 * half + part].wait()
            values = packed[half, part * rows : (part + 1) * rows]
            there = slice(part * cells, (part + 1) * cells)
            for pair in range(2):
                lanes = slice(64 * pair, 64 * pair + CELLS)
                out[2 * half + pair, there] = values[:, lanes].reshape(cells, CH, CELLS)
            target = (pl.ds(2 * half, 2), pl.ds(part * cells, cells))
            store = pltpu.make_async_copy(out.at[target], out_hbm.at[target], out_sems.at[2 * half + part])
            store.start()
            stores.append(store)
    for store in stores:
        store.wait()


def shards(nx, ny, field, w_coarse, w_detail, w_skip, cotangent):
    block = (BATCH, CELLS, CH, CELLS)
    packed = pltpu.VMEM((2, CELLS * CH, 128), F32)
    hbm = pl.BlockSpec(memory_space=pl.ANY)
    weight = pltpu.VMEM((CH, CH), F32)
    small = jax.ShapeDtypeStruct((CH, CH), F32)
    near = 2 * (4 if nx % 4 == 0 else nx)
    peers = max(near, nx * ny // near)
    chunk = CH // near
    bank = bank_matrix()
    result, summed = pl.pallas_call(
        functools.partial(kernel, nx, ny),
        out_shape=(
            jax.ShapeDtypeStruct((2, CELLS * CH, 128), F32),
            jax.ShapeDtypeStruct((CH, 128), F32),
        ),
        in_specs=[hbm] * 7,
        out_specs=(hbm, hbm),
        scratch_shapes=[
            pltpu.VMEM(block, F32),
            pltpu.VMEM(block, F32),
            packed,
            packed,
            packed,
            packed,
            packed,
            pltpu.VMEM((2, 2 * ROWS, 512), F32),
            pltpu.VMEM((4, 256, 256), F32),
            weight,
            weight,
            weight,
            pltpu.VMEM((512, 256), F32),
            pltpu.VMEM((2, 512, 256), BF16),
            pltpu.VMEM((256, 512), F32),
            pltpu.VMEM((2, 256, 512), BF16),
            pltpu.VMEM((2, 2, 2, 2 * ROWS, 128), F32),
            pltpu.VMEM((2, 2, 2 * ROWS, 128), F32),
            pltpu.VMEM((2, 2, 6 * ROWS, 128), F32),
            pltpu.VMEM((2, 2, 2 * ROWS, 128), F32),
            pltpu.VMEM((2, 2 * ROWS, 256), F32),
            packed,
            pltpu.VMEM((near, chunk, 128), F32),
            pltpu.VMEM((3, peers, chunk, 128), F32),
            pltpu.VMEM((2, chunk, 128), F32),
            pltpu.VMEM((CH, 128), F32),
            pltpu.SemaphoreType.DMA((9,)),
            pltpu.SemaphoreType.DMA((3,)),
            pltpu.SemaphoreType.DMA((4, 2, 5)),
            pltpu.SemaphoreType.DMA((4, 2, 5)),
            pltpu.SemaphoreType.DMA((3, peers)),
            pltpu.SemaphoreType.DMA((3, peers)),
        ],
        compiler_params=pltpu.CompilerParams(
            collective_id=0, has_side_effects=True, vmem_limit_bytes=60 * 1024 * 1024
        ),
    )(
        jnp.transpose(field, (0, 1, 3, 2)),
        jnp.transpose(cotangent, (0, 1, 3, 2)),
        w_coarse,
        w_detail,
        w_skip,
        jnp.asarray(bank),
        jnp.asarray(np.ascontiguousarray(bank.T)),
    )
    grad_field, *grads = pl.pallas_call(
        unpack_kernel,
        out_shape=(jax.ShapeDtypeStruct(block, F32), small, small, small),
        in_specs=[hbm, hbm],
        out_specs=(hbm, hbm, hbm, hbm),
        scratch_shapes=[
            packed,
            pltpu.VMEM((CH, 128), F32),
            pltpu.VMEM((3, CH, CH), F32),
            pltpu.VMEM(block, F32),
            pltpu.SemaphoreType.DMA((5,)),
            pltpu.SemaphoreType.DMA((7,)),
        ],
        compiler_params=pltpu.CompilerParams(vmem_limit_bytes=60 * 1024 * 1024),
    )(result, summed)
    return (jnp.transpose(grad_field, (0, 1, 3, 2)), *grads)


def solution(mesh):
    nx, ny = mesh.shape["gx"], mesh.shape["gy"]
    in_specs = (P(None, "gx", "gy", None), P(), P(), P(), P(None, "gx", "gy", None))
    out_specs = (P(None, "gx", "gy", None), P(), P(), P())

    def run(*args):
        return shards(nx, ny, *args)

    return jax.shard_map(run, mesh=mesh, in_specs=in_specs, out_specs=out_specs, check_vma=False)
```

```python
import functools

import jax
import jax.numpy as jnp
import numpy as np
from jax import lax
from jax.experimental import pallas as pl
from jax.experimental.pallas import tpu as pltpu
from jax.sharding import PartitionSpec as P

LOW_TAPS = [
    0.23037781330885523,
    0.7148465705525415,
    0.6308807679295904,
    -0.02798376941698385,
    -0.18703481171888114,
    0.030841381835986965,
    0.032883011666982945,
    -0.010597401784997278,
]
HIGH_TAPS = [(-1) ** offset * LOW_TAPS[7 - offset] for offset in range(8)]

F32 = jnp.float32
BF16 = jnp.bfloat16
MESH = pl.DeviceIdType.MESH
CH = 32
BATCH = 4
CELLS = 48
COARSE = 6
ROWS = COARSE * CH // 2
GELU_A = 0.7978845608028654
GELU_B = GELU_A * 0.044715


def bounds(low, high):
    return -((7 - low) // 2), high // 2


LEVELS = [(0, CELLS - 1)]
for _ in range(3):
    LEVELS.append(bounds(*LEVELS[-1]))


def line_matrix():
    values = np.eye(CELLS)
    low, high = LEVELS[0]
    outputs = []
    for level in range(3):
        bank = [LOW_TAPS] if level < 2 else [LOW_TAPS, HIGH_TAPS]
        first, last = LEVELS[level + 1]
        outputs = []
        for taps in bank:
            result = np.zeros((last - first + 1, CELLS))
            for k in range(first, last + 1):
                for j in range(8):
                    if low <= 2 * k + j <= high:
                        result[k - first] += taps[j] * values[2 * k + j - low]
            outputs.append(result)
        values, low, high = outputs[0], first, last
    return np.stack(outputs)


def bank_matrix():
    line = line_matrix()
    result = np.zeros((2, 2, 2, 64, 2, 2, 64))
    for group in range(2):
        for xband in range(2):
            for b in range(2):
                for part in range(2):
                    for yband in range(2):
                        for k in range(COARSE):
                            lane = ((xband * 2 + yband) * COARSE + k) * 2 + b
                            result[group, xband, b, :CELLS, part, group, lane] = line[yband, part * COARSE + k]
    return result.reshape(512, 256).astype(np.float32)


def split(values):
    high = values.astype(BF16)
    return high, (values - high.astype(F32)).astype(BF16)


def dot3(left, right, dims=((1,), (0,))):
    form = (dims, ((), ()))
    rows = left[0].shape[0]
    both = lax.dot_general(jnp.concatenate(left, axis=0), right[0], form, preferred_element_type=F32)
    return both[:rows] + both[rows:] + lax.dot_general(left[0], right[1], form, preferred_element_type=F32)


NT = ((1,), (1,))


class Analysis:
    def __init__(self, load):
        self.load = load
        self.memo = {}

    def get(self, level, k, taps=LOW_TAPS, band=0):
        if level == 0:
            if (0, k) not in self.memo:
                self.memo[0, k] = self.load(k)
            return self.memo[0, k]
        key = (level, k, band)
        if key not in self.memo:
            low, high = LEVELS[level - 1]
            total = None
            for j in range(8):
                if low <= 2 * k + j <= high:
                    term = self.get(level - 1, 2 * k + j) * F32(taps[j])
                    total = term if total is None else total + term
            self.memo[key] = total
        return self.memo[key]


class Synthesis:
    def __init__(self, load):
        self.load = load
        self.memo = {}

    def top(self, band, k):
        if (band, k) not in self.memo:
            self.memo[band, k] = self.load(band, k)
        return self.memo[band, k]

    def get(self, level, i):
        key = (level, i, "s")
        if key not in self.memo:
            low, high = LEVELS[level + 1]
            total = None
            for k in range(low, high + 1):
                j = i - 2 * k
                if 0 <= j < 8:
                    if level == 2:
                        term = self.top(0, k) * F32(LOW_TAPS[j]) + self.top(1, k) * F32(HIGH_TAPS[j])
                    else:
                        term = self.get(level + 1, k) * F32(LOW_TAPS[j])
                    total = term if total is None else total + term
            self.memo[key] = total
        return self.memo[key]


def synthesis_column(lines, rows):
    def load(band, k):
        part, group, row = (k + COARSE) // 6, (k + COARSE) % 6 // 3, (k + COARSE) % 3
        start = (part * 3 + row) * CH
        lanes = group * 256 + band * 128
        return lines[pl.ds(pl.multiple_of(start + rows, 8), 8), lanes : lanes + 128]

    return Synthesis(load)


def analyze_column(lines, rows, load):
    walk = Analysis(load)
    for k in range(-COARSE, COARSE):
        part, group, row = (k + COARSE) // 6, (k + COARSE) % 6 // 3, (k + COARSE) % 3
        start = (part * 3 + row) * CH
        for band, taps in enumerate((LOW_TAPS, HIGH_TAPS)):
            lanes = group * 256 + band * 128
            lines[pl.ds(pl.multiple_of(start + rows, 8), 8), lanes : lanes + 128] = walk.get(3, k, taps, band)


def side_by_side(values):
    return jnp.concatenate([values[k : k + CH] for k in range(0, values.shape[0], CH)], axis=1)


def in_coarse(values):
    return lax.rem(lax.broadcasted_iota(jnp.int32, values.shape, 1), 64) < 12


def mix(values, weights):
    count, width = values.shape[0] // CH, values.shape[1]
    both = dot3(weights, split(side_by_side(values)))
    chosen = jnp.where(in_coarse(both[:CH]), both[:CH], both[CH:])
    return jnp.concatenate([chosen[:, k * width : (k + 1) * width] for k in range(count)], axis=0)


def pack(source, target, half):
    for pair in range(2):
        values = source[2 * half + pair].reshape(CELLS * CH, CELLS)
        target[half, :, 64 * pair : 64 * pair + CELLS] = values


def kernel(
    nx, ny, field_hbm, cot_hbm, wc_hbm, wd_hbm, ws_hbm, bank_hbm, back_hbm, packed_hbm, sum_hbm,
    raw, raw_cot, field, cot, grad, skip, base, lines, kron, wc_ref, wd_ref, ws_ref, bank_ref, bank_parts, back_ref, back_parts,
    send_fwd, send_mix, recv_sum, recv_next, wide, packed, ar_pair, ar_in, ar_part, gsum, result,
    in_sems, out_sems, ex_send, ex_recv, ar_send, ar_recv, pair_send, pair_recv,
):
    gx = lax.axis_index("gx")
    gy = lax.axis_index("gy")
    right, left = lax.rem(gx + 1, nx), lax.rem(gx + nx - 1, nx)
    up, down = lax.rem(gy + 1, ny), lax.rem(gy + ny - 1, ny)

    halves = [pl.ds(0, 2), pl.ds(2, 2)]
    moves = [
        (field_hbm.at[halves[0]], raw.at[halves[0]]),
        (bank_hbm, bank_ref),
        (field_hbm.at[halves[1]], raw.at[halves[1]]),
        (wc_hbm, wc_ref),
        (wd_hbm, wd_ref),
        (ws_hbm, ws_ref),
        (back_hbm, back_ref),
        (cot_hbm.at[halves[0]], raw_cot.at[halves[0]]),
        (cot_hbm.at[halves[1]], raw_cot.at[halves[1]]),
    ]
    loads = [pltpu.make_async_copy(source, target, in_sems.at[i]) for i, (source, target) in enumerate(moves)]
    for load in loads:
        load.start()

    barrier = pltpu.get_barrier_semaphore()

    core, depth = lax.rem(gy, 2), ny // 2
    my_z = lax.div(gy, 2)
    partner = (gx, gy + 1 - 2 * core)

    def line(axis):
        if axis == 0:
            return nx, gx, lambda other: (other, gy)
        return depth, my_z, lambda other: (gx, other * 2 + core)

    def greet(device):
        pl.semaphore_signal(barrier, inc=1, device_id=device, device_id_type=MESH)

    def each(axis, action):
        size, me, device = line(axis)

        def step(r, carry):
            other = lax.rem(me + r, size)
            action(r, other, device(other))
            return carry

        lax.fori_loop(1, size, step, 0)

    for device in ((right, gy), (left, gy), (gx, up), (gx, down)):
        greet(device)
    for device in ((right, up), (left, down), (right, down), (left, up)):
        greet(device)
    greet(partner)
    for axis in range(2):
        each(axis, lambda r, other, device: greet(device))

    field[...] = jnp.zeros(field.shape, F32)
    cot[...] = jnp.zeros(cot.shape, F32)
    kron[...] = jnp.zeros(kron.shape, F32)

    def bank():
        return bank_parts[0], bank_parts[1]

    def bank_back():
        return back_parts[0], back_parts[1]

    def exchange(step, half, moves):
        copies = []
        for slot, (source, target, device) in enumerate(moves):
            copy = pltpu.make_async_remote_copy(
                src_ref=source,
                dst_ref=target,
                send_sem=ex_send.at[step, half, slot],
                recv_sem=ex_recv.at[step, half, slot],
                device_id=device,
                device_id_type=MESH,
            )
            copy.start()
            copies.append(copy)
        return copies

    def send_partials(step, half):
        parts = dot3(split(lines[half]), bank())
        before, own = send_fwd.at[step // 2, half, 0], send_fwd.at[step // 2, half, 1]
        before[...] = parts[:, :128]
        own[...] = parts[:, 128:]
        arrived = recv_sum.at[step // 2, half]
        first, second = pl.ds(0, ROWS), pl.ds(ROWS, ROWS)
        moves = [
            (before.at[first], arrived.at[pl.ds(0, ROWS)], (left, down)),
            (before.at[second], arrived.at[pl.ds(ROWS, ROWS)], (right, down)),
            (own.at[first], arrived.at[pl.ds(2 * ROWS, ROWS)], (left, gy)),
            (own.at[second], arrived.at[pl.ds(3 * ROWS, ROWS)], (right, gy)),
            (before, arrived.at[pl.ds(4 * ROWS, 2 * ROWS)], (gx, down)),
        ]
        return parts, exchange(step, half, moves)

    def gather_sum(step, half, parts, copies):
        for copy in copies:
            copy.wait_recv()
        arrived = recv_sum[step // 2, half]
        total = parts[:, 128:] + arrived[4 * ROWS :]
        above = arrived[ROWS : 2 * ROWS] + arrived[3 * ROWS : 4 * ROWS]
        below = arrived[:ROWS] + arrived[2 * ROWS : 3 * ROWS]
        return total + jnp.concatenate([above, below], axis=0)

    def send_next(step, half, values):
        send_mix[step // 2, half] = values
        return exchange(step, half, [(send_mix.at[step // 2, half], recv_next.at[step // 2, half], (gx, up))])

    def gather_wide(step, half, copies):
        for copy in copies:
            copy.wait_recv()
        return jnp.concatenate([recv_next[step // 2, half], send_mix[step // 2, half]], axis=1)

    def cells(x, rows):
        return pl.ds(pl.multiple_of(x * CH + rows, 8), 8)

    def first(half):
        pack(raw, field, half)

        def column(index, carry):
            rows = pl.multiple_of(index * 8, 8)
            analyze_column(lines.at[half], rows, lambda x: field[half, cells(x, rows), :])
            return carry

        lax.fori_loop(0, 4, column, 0)

    loads[1].wait()
    bank_parts[0], bank_parts[1] = split(bank_ref[...])
    loads[0].wait()
    first(0)
    pl.semaphore_wait(barrier, 8 + 1 + nx - 1 + depth - 1)
    parts0, copies1a = send_partials(0, 0)
    loads[2].wait()
    first(1)
    parts1, copies1b = send_partials(0, 1)

    eye = (
        lax.broadcasted_iota(jnp.int32, (CH, CH), 0) == lax.broadcasted_iota(jnp.int32, (CH, CH), 1)
    ).astype(BF16)

    def transposed(weight):
        form = (NT, ((), ()))
        return lax.dot_general(eye, weight, form, preferred_element_type=F32).astype(BF16)

    for load in loads[3:7]:
        load.wait()
    back_parts[0], back_parts[1] = split(back_ref[...])
    coarse_parts = split(wc_ref[...])
    detail_parts = split(wd_ref[...])
    skip_parts = split(ws_ref[...])
    weights_forward = tuple(
        jnp.concatenate([transposed(c), transposed(d)], axis=0) for c, d in zip(coarse_parts, detail_parts)
    )
    weights_back = tuple(jnp.concatenate([c, d], axis=0) for c, d in zip(coarse_parts, detail_parts))

    for which in range(2):
        forward = transposed(skip_parts[which]).astype(F32)
        backward = skip_parts[which].astype(F32)
        for i in range(8):
            block = slice(i * CH, (i + 1) * CH)
            kron[which, block, block] = forward
            kron[2 + which, block, block] = backward

    def skip_mix(source, target, kind, half):
        weights = (kron[kind].astype(BF16), kron[kind + 1].astype(BF16))
        for g in range(6):
            block = slice(256 * g, 256 * g + 256)
            target[half, block] = dot3(weights, split(source[half, block]))

    skip_mix(field, skip, 0, 0)
    loads[7].wait()
    pack(raw_cot, cot, 0)

    copies2a = send_next(1, 0, gather_sum(0, 0, parts0, copies1a))

    loads[8].wait()
    pack(raw_cot, cot, 1)

    copies2b = send_next(1, 1, gather_sum(0, 1, parts1, copies1b))

    skip_mix(field, skip, 0, 1)

    def middle(half, copies):
        values = gather_wide(1, half, copies)
        wide[half] = values
        lines[half] = dot3(split(mix(values, weights_forward)), bank_back())

        def column(index, carry):
            rows = pl.multiple_of(index * 8, 8)
            walk = synthesis_column(lines.at[half], rows)

            def load(x):
                here = cells(x, rows)
                pre = walk.get(0, x) + skip[half, here, :]
                cube = F32(GELU_B) * (pre * pre)
                tanh = jnp.tanh(pre * (F32(GELU_A) + cube))
                slope = pre * (F32(GELU_A) + F32(3.0) * cube)
                rise = (F32(0.5) + F32(0.5) * tanh) * (F32(1.0) + (slope - slope * tanh))
                value = cot[half, here, :] * rise
                grad[half, here, :] = value
                return value

            analyze_column(lines.at[half], rows, load)
            return carry

        lax.fori_loop(0, 4, column, 0)
        return send_partials(2, half)

    parts0, copies3a = middle(0, copies2a)
    parts1, copies3b = middle(1, copies2b)

    def share(half, parts):
        flat = side_by_side(parts)
        coarse = in_coarse(flat)
        masked = jnp.concatenate([jnp.where(coarse, flat, 0.0), jnp.where(coarse, 0.0, flat)], axis=0)
        both = dot3(split(side_by_side(wide[half])), split(masked), NT)
        pair = jnp.zeros((256, 256), F32)
        for g in range(6):
            block = slice(256 * g, 256 * g + 256)
            pair = pair + dot3(split(field[half, block]), split(grad[half, block]), NT)
        return both, pair

    both0, pair0 = share(0, parts0)
    both1, pair1 = share(1, parts1)

    pair = pair0 + pair1
    skip_sum = pair[:CH, :CH]
    for i in range(1, 8):
        block = slice(i * CH, (i + 1) * CH)
        skip_sum = skip_sum + pair[block, block]
    share_sum = jnp.concatenate([both0 + both1, skip_sum, jnp.zeros((CH, CH), F32)], axis=1)
    gsum[0] = share_sum[: CH // 2]
    gsum[1] = share_sum[CH // 2 :]

    def to_partner(phase, source, target):
        return pltpu.make_async_remote_copy(
            src_ref=source,
            dst_ref=target,
            send_sem=pair_send.at[phase],
            recv_sem=pair_recv.at[phase],
            device_id=partner,
            device_id_type=MESH,
        )

    def line_copy(axis, r, device):
        me = line(axis)[1]
        return pltpu.make_async_remote_copy(
            src_ref=ar_part.at[axis],
            dst_ref=ar_in.at[axis, me],
            send_sem=ar_send.at[axis, r],
            recv_sem=ar_recv.at[axis, me],
            device_id=device,
            device_id_type=MESH,
        )

    def line_start(axis, total):
        ar_part[axis] = total
        ar_in[axis, line(axis)[1]] = total
        each(axis, lambda r, other, device: line_copy(axis, r, device).start())

    def line_sum(axis):
        def arrive(r, other, device):
            arrived = ar_in.at[axis, other]
            pltpu.make_async_copy(arrived, arrived, ar_recv.at[axis, other]).wait()

        each(axis, arrive)
        total = ar_in[axis, 0]
        for i in range(1, line(axis)[0]):
            total = total + ar_in[axis, i]
        return total

    swap = to_partner(0, gsum.at[1 - core], ar_pair)
    swap.start()

    copies4a = send_next(3, 0, mix(gather_sum(2, 0, parts0, copies3a), weights_back))

    swap.wait_recv()
    line_start(0, gsum[core] + ar_pair[...])

    skip_mix(grad, base, 2, 0)
    copies4b = send_next(3, 1, mix(gather_sum(2, 1, parts1, copies3b), weights_back))

    skip_mix(grad, base, 2, 1)

    def last(half, copies):
        lines[half] = dot3(split(gather_wide(3, half, copies)), bank_back())

        def column(index, carry):
            rows = pl.multiple_of(index * 8, 8)
            walk = synthesis_column(lines.at[half], rows)
            for x in range(CELLS):
                packed[half, cells(x, rows), :] = walk.get(0, x) + base[half, cells(x, rows), :]
            return carry

        lax.fori_loop(0, 4, column, 0)
        store = pltpu.make_async_copy(packed.at[half], packed_hbm.at[half], out_sems.at[half])
        store.start()
        return store

    store0 = last(0, copies4a)
    line_start(1, line_sum(0))

    store1 = last(1, copies4b)

    scale = F32(1.0 / (BATCH * CELLS * CELLS * nx * ny))
    result[core] = line_sum(1) * scale
    swap_back = to_partner(1, result.at[core], result.at[core])
    swap_back.start()

    for copies in (copies1a, copies1b, copies2a, copies2b, copies3a, copies3b, copies4a, copies4b):
        for copy in copies:
            copy.wait_send()
    for axis in range(2):
        each(axis, lambda r, other, device: line_copy(axis, r, device).wait_send())
    swap.wait_send()
    store0.wait()
    store1.wait()

    swap_back.wait()
    store = pltpu.make_async_copy(result, sum_hbm, out_sems.at[2])
    store.start()
    store.wait()


def unpack_kernel(
    packed_hbm, sum_hbm, out_hbm, gc_hbm, gd_hbm, gs_hbm, packed, summed, grads, out, in_sems, out_sems
):
    cells = CELLS // 2
    rows = cells * CH
    loads = []
    for half in range(2):
        for part in range(2):
            here = pl.ds(part * rows, rows)
            loads.append(
                pltpu.make_async_copy(
                    packed_hbm.at[half, here], packed.at[half, here], in_sems.at[2 * half + part]
                )
            )
    loads.append(pltpu.make_async_copy(sum_hbm, summed, in_sems.at[4]))
    for load in loads[4:] + loads[:4]:
        load.start()
    stores = []
    loads[4].wait()
    for i, target in enumerate((gc_hbm, gd_hbm, gs_hbm)):
        for part in range(2):
            rows_here = slice(part * CH // 2, (part + 1) * CH // 2)
            grads[i, rows_here] = summed[part, :, i * CH : (i + 1) * CH]
        store = pltpu.make_async_copy(grads.at[i], target, out_sems.at[4 + i])
        store.start()
        stores.append(store)
    for half in range(2):
        for part in range(2):
            loads[2 * half + part].wait()
            values = packed[half, part * rows : (part + 1) * rows]
            there = slice(part * cells, (part + 1) * cells)
            for pair in range(2):
                lanes = slice(64 * pair, 64 * pair + CELLS)
                out[2 * half + pair, there] = values[:, lanes].reshape(cells, CH, CELLS)
            target = (pl.ds(2 * half, 2), pl.ds(part * cells, cells))
            store = pltpu.make_async_copy(out.at[target], out_hbm.at[target], out_sems.at[2 * half + part])
            store.start()
            stores.append(store)
    for store in stores:
        store.wait()


def shards(nx, ny, field, w_coarse, w_detail, w_skip, cotangent):
    block = (BATCH, CELLS, CH, CELLS)
    packed = pltpu.VMEM((2, CELLS * CH, 128), F32)
    hbm = pl.BlockSpec(memory_space=pl.ANY)
    weight = pltpu.VMEM((CH, CH), F32)
    small = jax.ShapeDtypeStruct((CH, CH), F32)
    peers = max(nx, ny // 2)
    half_sum = (CH // 2, 128)
    bank = bank_matrix()
    packed_field, summed = pl.pallas_call(
        functools.partial(kernel, nx, ny),
        out_shape=(
            jax.ShapeDtypeStruct((2, CELLS * CH, 128), F32),
            jax.ShapeDtypeStruct((2, *half_sum), F32),
        ),
        in_specs=[hbm] * 7,
        out_specs=(hbm, hbm),
        scratch_shapes=[
            pltpu.VMEM(block, F32),
            pltpu.VMEM(block, F32),
            packed,
            packed,
            packed,
            packed,
            packed,
            pltpu.VMEM((2, 2 * ROWS, 512), F32),
            pltpu.VMEM((4, 256, 256), F32),
            weight,
            weight,
            weight,
            pltpu.VMEM((512, 256), F32),
            pltpu.VMEM((2, 512, 256), BF16),
            pltpu.VMEM((256, 512), F32),
            pltpu.VMEM((2, 256, 512), BF16),
            pltpu.VMEM((2, 2, 2, 2 * ROWS, 128), F32),
            pltpu.VMEM((2, 2, 2 * ROWS, 128), F32),
            pltpu.VMEM((2, 2, 6 * ROWS, 128), F32),
            pltpu.VMEM((2, 2, 2 * ROWS, 128), F32),
            pltpu.VMEM((2, 2 * ROWS, 256), F32),
            packed,
            pltpu.VMEM(half_sum, F32),
            pltpu.VMEM((2, peers, *half_sum), F32),
            pltpu.VMEM((2, *half_sum), F32),
            pltpu.VMEM((2, *half_sum), F32),
            pltpu.VMEM((2, *half_sum), F32),
            pltpu.SemaphoreType.DMA((9,)),
            pltpu.SemaphoreType.DMA((3,)),
            pltpu.SemaphoreType.DMA((4, 2, 5)),
            pltpu.SemaphoreType.DMA((4, 2, 5)),
            pltpu.SemaphoreType.DMA((2, peers)),
            pltpu.SemaphoreType.DMA((2, peers)),
            pltpu.SemaphoreType.DMA((2,)),
            pltpu.SemaphoreType.DMA((2,)),
        ],
        compiler_params=pltpu.CompilerParams(
            collective_id=0, has_side_effects=True, vmem_limit_bytes=60 * 1024 * 1024
        ),
    )(
        jnp.transpose(field, (0, 1, 3, 2)),
        jnp.transpose(cotangent, (0, 1, 3, 2)),
        w_coarse,
        w_detail,
        w_skip,
        jnp.asarray(bank),
        jnp.asarray(np.ascontiguousarray(bank.T)),
    )
    grad_field, *grads = pl.pallas_call(
        unpack_kernel,
        out_shape=(jax.ShapeDtypeStruct(block, F32), small, small, small),
        in_specs=[hbm, hbm],
        out_specs=(hbm, hbm, hbm, hbm),
        scratch_shapes=[
            packed,
            pltpu.VMEM((2, *half_sum), F32),
            pltpu.VMEM((3, CH, CH), F32),
            pltpu.VMEM(block, F32),
            pltpu.SemaphoreType.DMA((5,)),
            pltpu.SemaphoreType.DMA((7,)),
        ],
        compiler_params=pltpu.CompilerParams(vmem_limit_bytes=60 * 1024 * 1024),
    )(packed_field, summed)
    return (jnp.transpose(grad_field, (0, 1, 3, 2)), *grads)


def solution(mesh):
    nx, ny = mesh.shape["gx"], mesh.shape["gy"]
    in_specs = (P(None, "gx", "gy", None), P(), P(), P(), P(None, "gx", "gy", None))
    out_specs = (P(None, "gx", "gy", None), P(), P(), P())

    def run(*args):
        return shards(nx, ny, *args)

    return jax.shard_map(run, mesh=mesh, in_specs=in_specs, out_specs=out_specs, check_vma=False)
```

```python
import functools

import jax
import jax.numpy as jnp
import numpy as np
from jax import lax
from jax.experimental import pallas as pl
from jax.experimental.pallas import tpu as pltpu
from jax.sharding import PartitionSpec as P

LOW_TAPS = [
    0.23037781330885523,
    0.7148465705525415,
    0.6308807679295904,
    -0.02798376941698385,
    -0.18703481171888114,
    0.030841381835986965,
    0.032883011666982945,
    -0.010597401784997278,
]
HIGH_TAPS = [(-1) ** offset * LOW_TAPS[7 - offset] for offset in range(8)]

F32 = jnp.float32
BF16 = jnp.bfloat16
MESH = pl.DeviceIdType.MESH
CH = 32
BATCH = 4
CELLS = 48
COARSE = 6
ROWS = COARSE * CH // 2
GELU_A = 0.7978845608028654
GELU_B = GELU_A * 0.044715


def bounds(low, high):
    return -((7 - low) // 2), high // 2


LEVELS = [(0, CELLS - 1)]
for _ in range(3):
    LEVELS.append(bounds(*LEVELS[-1]))


def line_matrix():
    values = np.eye(CELLS)
    low, high = LEVELS[0]
    outputs = []
    for level in range(3):
        bank = [LOW_TAPS] if level < 2 else [LOW_TAPS, HIGH_TAPS]
        first, last = LEVELS[level + 1]
        outputs = []
        for taps in bank:
            result = np.zeros((last - first + 1, CELLS))
            for k in range(first, last + 1):
                for j in range(8):
                    if low <= 2 * k + j <= high:
                        result[k - first] += taps[j] * values[2 * k + j - low]
            outputs.append(result)
        values, low, high = outputs[0], first, last
    return np.stack(outputs)


def bank_matrix():
    line = line_matrix()
    result = np.zeros((2, 2, 2, 64, 2, 2, 64))
    for group in range(2):
        for xband in range(2):
            for b in range(2):
                for part in range(2):
                    for yband in range(2):
                        for k in range(COARSE):
                            lane = ((xband * 2 + yband) * COARSE + k) * 2 + b
                            result[group, xband, b, :CELLS, part, group, lane] = line[yband, part * COARSE + k]
    return result.reshape(512, 256).astype(np.float32)


def split(values):
    high = values.astype(BF16)
    return high, (values - high.astype(F32)).astype(BF16)


def dot3(left, right, dims=((1,), (0,))):
    form = (dims, ((), ()))
    rows = left[0].shape[0]
    both = lax.dot_general(jnp.concatenate(left, axis=0), right[0], form, preferred_element_type=F32)
    return both[:rows] + both[rows:] + lax.dot_general(left[0], right[1], form, preferred_element_type=F32)


NT = ((1,), (1,))


class Analysis:
    def __init__(self, load):
        self.load = load
        self.memo = {}

    def get(self, level, k, taps=LOW_TAPS, band=0):
        if level == 0:
            if (0, k) not in self.memo:
                self.memo[0, k] = self.load(k)
            return self.memo[0, k]
        key = (level, k, band)
        if key not in self.memo:
            low, high = LEVELS[level - 1]
            total = None
            for j in range(8):
                if low <= 2 * k + j <= high:
                    term = self.get(level - 1, 2 * k + j) * F32(taps[j])
                    total = term if total is None else total + term
            self.memo[key] = total
        return self.memo[key]


class Synthesis:
    def __init__(self, load):
        self.load = load
        self.memo = {}

    def top(self, band, k):
        if (band, k) not in self.memo:
            self.memo[band, k] = self.load(band, k)
        return self.memo[band, k]

    def get(self, level, i):
        key = (level, i, "s")
        if key not in self.memo:
            low, high = LEVELS[level + 1]
            total = None
            for k in range(low, high + 1):
                j = i - 2 * k
                if 0 <= j < 8:
                    if level == 2:
                        term = self.top(0, k) * F32(LOW_TAPS[j]) + self.top(1, k) * F32(HIGH_TAPS[j])
                    else:
                        term = self.get(level + 1, k) * F32(LOW_TAPS[j])
                    total = term if total is None else total + term
            self.memo[key] = total
        return self.memo[key]


def synthesis_column(lines, rows):
    def load(band, k):
        part, group, row = (k + COARSE) // 6, (k + COARSE) % 6 // 3, (k + COARSE) % 3
        start = (part * 3 + row) * CH
        lanes = group * 256 + band * 128
        return lines[pl.ds(pl.multiple_of(start + rows, 8), 8), lanes : lanes + 128]

    return Synthesis(load)


def analyze_column(lines, rows, load):
    walk = Analysis(load)
    for k in range(-COARSE, COARSE):
        part, group, row = (k + COARSE) // 6, (k + COARSE) % 6 // 3, (k + COARSE) % 3
        start = (part * 3 + row) * CH
        for band, taps in enumerate((LOW_TAPS, HIGH_TAPS)):
            lanes = group * 256 + band * 128
            lines[pl.ds(pl.multiple_of(start + rows, 8), 8), lanes : lanes + 128] = walk.get(3, k, taps, band)


def side_by_side(values):
    return jnp.concatenate([values[k : k + CH] for k in range(0, values.shape[0], CH)], axis=1)


def in_coarse(values):
    return lax.rem(lax.broadcasted_iota(jnp.int32, values.shape, 1), 64) < 12


def mix(values, weights):
    count, width = values.shape[0] // CH, values.shape[1]
    both = dot3(weights, split(side_by_side(values)))
    chosen = jnp.where(in_coarse(both[:CH]), both[:CH], both[CH:])
    return jnp.concatenate([chosen[:, k * width : (k + 1) * width] for k in range(count)], axis=0)


def pack(source, target, half):
    for pair in range(2):
        values = source[2 * half + pair].reshape(CELLS * CH, CELLS)
        target[half, :, 64 * pair : 64 * pair + CELLS] = values


def kernel(
    nx, ny, field_hbm, cot_hbm, wc_hbm, wd_hbm, ws_hbm, bank_hbm, back_hbm, packed_hbm, sum_hbm,
    raw, raw_cot, field, cot, grad, skip, base, lines, kron, wc_ref, wd_ref, ws_ref, bank_ref, bank_parts, back_ref, back_parts,
    send_fwd, send_mix, recv_sum, recv_next, wide, packed, ar_pair, ar_in, ar_part, gsum, result,
    in_sems, out_sems, ex_send, ex_recv, ar_send, ar_recv, pair_send, pair_recv,
):
    gx = lax.axis_index("gx")
    gy = lax.axis_index("gy")
    right, left = lax.rem(gx + 1, nx), lax.rem(gx + nx - 1, nx)
    up, down = lax.rem(gy + 1, ny), lax.rem(gy + ny - 1, ny)

    def piece(source, target, b, part):
        here = (b, pl.ds(part * (CELLS // 2), CELLS // 2))
        return source.at[here], target.at[here]

    moves = [piece(field_hbm, raw, b, part) for b in range(2) for part in range(2)]
    moves += [(bank_hbm, bank_ref)]
    moves += [piece(field_hbm, raw, b, part) for b in range(2, 4) for part in range(2)]
    moves += [(wc_hbm, wc_ref), (wd_hbm, wd_ref), (ws_hbm, ws_ref), (back_hbm, back_ref)]
    moves += [(cot_hbm.at[pl.ds(2 * half, 2)], raw_cot.at[pl.ds(2 * half, 2)]) for half in range(2)]
    loads = [pltpu.make_async_copy(source, target, in_sems.at[i]) for i, (source, target) in enumerate(moves)]
    for load in loads:
        load.start()

    barrier = pltpu.get_barrier_semaphore()

    core, depth = lax.rem(gy, 2), ny // 2
    my_z = lax.div(gy, 2)
    partner = (gx, gy + 1 - 2 * core)

    def line(axis):
        if axis == 0:
            return nx, gx, lambda other: (other, gy)
        return depth, my_z, lambda other: (gx, other * 2 + core)

    def greet(device):
        pl.semaphore_signal(barrier, inc=1, device_id=device, device_id_type=MESH)

    def each(axis, action):
        size, me, device = line(axis)

        def step(r, carry):
            other = lax.rem(me + r, size)
            action(r, other, device(other))
            return carry

        lax.fori_loop(1, size, step, 0)

    for device in ((right, gy), (left, gy), (gx, up), (gx, down)):
        greet(device)
    for device in ((right, up), (left, down), (right, down), (left, up)):
        greet(device)
    greet(partner)
    for axis in range(2):
        each(axis, lambda r, other, device: greet(device))

    field[...] = jnp.zeros(field.shape, F32)

    def bank():
        return bank_parts[0], bank_parts[1]

    def bank_back():
        return back_parts[0], back_parts[1]

    def exchange(step, half, moves):
        copies = []
        for slot, (source, target, device) in enumerate(moves):
            copy = pltpu.make_async_remote_copy(
                src_ref=source,
                dst_ref=target,
                send_sem=ex_send.at[step, half, slot],
                recv_sem=ex_recv.at[step, half, slot],
                device_id=device,
                device_id_type=MESH,
            )
            copy.start()
            copies.append(copy)
        return copies

    def send_partials(step, half):
        parts = dot3(split(lines[half]), bank())
        before, own = send_fwd.at[step // 2, half, 0], send_fwd.at[step // 2, half, 1]
        before[...] = parts[:, :128]
        own[...] = parts[:, 128:]
        arrived = recv_sum.at[step // 2, half]
        first, second = pl.ds(0, ROWS), pl.ds(ROWS, ROWS)
        moves = [
            (before.at[first], arrived.at[pl.ds(0, ROWS)], (left, down)),
            (before.at[second], arrived.at[pl.ds(ROWS, ROWS)], (right, down)),
            (own.at[first], arrived.at[pl.ds(2 * ROWS, ROWS)], (left, gy)),
            (own.at[second], arrived.at[pl.ds(3 * ROWS, ROWS)], (right, gy)),
            (before, arrived.at[pl.ds(4 * ROWS, 2 * ROWS)], (gx, down)),
        ]
        return parts, exchange(step, half, moves)

    def gather_sum(step, half, parts, copies):
        for copy in copies:
            copy.wait_recv()
        arrived = recv_sum[step // 2, half]
        total = parts[:, 128:] + arrived[4 * ROWS :]
        above = arrived[ROWS : 2 * ROWS] + arrived[3 * ROWS : 4 * ROWS]
        below = arrived[:ROWS] + arrived[2 * ROWS : 3 * ROWS]
        return total + jnp.concatenate([above, below], axis=0)

    def send_next(step, half, values):
        send_mix[step // 2, half] = values
        return exchange(step, half, [(send_mix.at[step // 2, half], recv_next.at[step // 2, half], (gx, up))])

    def gather_wide(step, half, copies):
        for copy in copies:
            copy.wait_recv()
        return jnp.concatenate([recv_next[step // 2, half], send_mix[step // 2, half]], axis=1)

    def cells(x, rows):
        return pl.ds(pl.multiple_of(x * CH + rows, 8), 8)

    def first(half):
        for pair in range(2):
            for part in range(2):
                loads[5 * half + 2 * pair + part].wait()
                here = slice(part * (CELLS // 2), (part + 1) * (CELLS // 2))
                rows = slice(part * (CELLS // 2) * CH, (part + 1) * (CELLS // 2) * CH)
                values = raw[2 * half + pair, here].reshape(CELLS // 2 * CH, CELLS)
                field[half, rows, 64 * pair : 64 * pair + CELLS] = values

        def column(index, carry):
            rows = pl.multiple_of(index * 8, 8)
            analyze_column(lines.at[half], rows, lambda x: field[half, cells(x, rows), :])
            return carry

        lax.fori_loop(0, 4, column, 0)

    first(0)
    loads[4].wait()
    bank_parts[0], bank_parts[1] = split(bank_ref[...])
    pl.semaphore_wait(barrier, 8 + 1 + nx - 1 + depth - 1)
    parts0, copies1a = send_partials(0, 0)
    first(1)
    parts1, copies1b = send_partials(0, 1)

    eye = (
        lax.broadcasted_iota(jnp.int32, (CH, CH), 0) == lax.broadcasted_iota(jnp.int32, (CH, CH), 1)
    ).astype(BF16)

    def transposed(weight):
        form = (NT, ((), ()))
        return lax.dot_general(eye, weight, form, preferred_element_type=F32).astype(BF16)

    for load in loads[9:13]:
        load.wait()
    back_parts[0], back_parts[1] = split(back_ref[...])
    coarse_parts = split(wc_ref[...])
    detail_parts = split(wd_ref[...])
    skip_parts = split(ws_ref[...])
    weights_forward = tuple(
        jnp.concatenate([transposed(c), transposed(d)], axis=0) for c, d in zip(coarse_parts, detail_parts)
    )
    weights_back = tuple(jnp.concatenate([c, d], axis=0) for c, d in zip(coarse_parts, detail_parts))

    cot[...] = jnp.zeros(cot.shape, F32)
    kron[...] = jnp.zeros(kron.shape, F32)
    for which in range(2):
        forward = transposed(skip_parts[which]).astype(F32)
        backward = skip_parts[which].astype(F32)
        for i in range(8):
            block = slice(i * CH, (i + 1) * CH)
            kron[which, block, block] = forward
            kron[2 + which, block, block] = backward

    def skip_mix(source, target, kind, half):
        weights = (kron[kind].astype(BF16), kron[kind + 1].astype(BF16))
        for g in range(6):
            block = slice(256 * g, 256 * g + 256)
            target[half, block] = dot3(weights, split(source[half, block]))

    skip_mix(field, skip, 0, 0)
    loads[13].wait()
    pack(raw_cot, cot, 0)

    copies2a = send_next(1, 0, gather_sum(0, 0, parts0, copies1a))

    loads[14].wait()
    pack(raw_cot, cot, 1)

    copies2b = send_next(1, 1, gather_sum(0, 1, parts1, copies1b))

    skip_mix(field, skip, 0, 1)

    def middle(half, copies):
        values = gather_wide(1, half, copies)
        wide[half] = values
        lines[half] = dot3(split(mix(values, weights_forward)), bank_back())

        def column(index, carry):
            rows = pl.multiple_of(index * 8, 8)
            walk = synthesis_column(lines.at[half], rows)

            def load(x):
                here = cells(x, rows)
                pre = walk.get(0, x) + skip[half, here, :]
                cube = F32(GELU_B) * (pre * pre)
                tanh = jnp.tanh(pre * (F32(GELU_A) + cube))
                slope = pre * (F32(GELU_A) + F32(3.0) * cube)
                rise = (F32(0.5) + F32(0.5) * tanh) * (F32(1.0) + (slope - slope * tanh))
                value = cot[half, here, :] * rise
                grad[half, here, :] = value
                return value

            analyze_column(lines.at[half], rows, load)
            return carry

        lax.fori_loop(0, 4, column, 0)
        return send_partials(2, half)

    parts0, copies3a = middle(0, copies2a)
    parts1, copies3b = middle(1, copies2b)

    def share(half, parts):
        flat = side_by_side(parts)
        coarse = in_coarse(flat)
        masked = jnp.concatenate([jnp.where(coarse, flat, 0.0), jnp.where(coarse, 0.0, flat)], axis=0)
        both = dot3(split(side_by_side(wide[half])), split(masked), NT)
        return both, dot3(split(side_by_side(field[half])), split(side_by_side(grad[half])), NT)

    both0, skip0 = share(0, parts0)
    both1, skip1 = share(1, parts1)

    share_sum = jnp.concatenate([both0 + both1, skip0 + skip1, jnp.zeros((CH, CH), F32)], axis=1)
    gsum[0] = share_sum[: CH // 2]
    gsum[1] = share_sum[CH // 2 :]

    def to_partner(phase, source, target):
        return pltpu.make_async_remote_copy(
            src_ref=source,
            dst_ref=target,
            send_sem=pair_send.at[phase],
            recv_sem=pair_recv.at[phase],
            device_id=partner,
            device_id_type=MESH,
        )

    def line_copy(axis, r, device):
        me = line(axis)[1]
        return pltpu.make_async_remote_copy(
            src_ref=ar_part.at[axis],
            dst_ref=ar_in.at[axis, me],
            send_sem=ar_send.at[axis, r],
            recv_sem=ar_recv.at[axis, me],
            device_id=device,
            device_id_type=MESH,
        )

    def line_start(axis, total):
        ar_part[axis] = total
        ar_in[axis, line(axis)[1]] = total
        each(axis, lambda r, other, device: line_copy(axis, r, device).start())

    def line_sum(axis):
        def arrive(r, other, device):
            arrived = ar_in.at[axis, other]
            pltpu.make_async_copy(arrived, arrived, ar_recv.at[axis, other]).wait()

        each(axis, arrive)
        total = ar_in[axis, 0]
        for i in range(1, line(axis)[0]):
            total = total + ar_in[axis, i]
        return total

    swap = to_partner(0, gsum.at[1 - core], ar_pair)
    swap.start()

    copies4a = send_next(3, 0, mix(gather_sum(2, 0, parts0, copies3a), weights_back))

    swap.wait_recv()
    line_start(0, gsum[core] + ar_pair[...])

    skip_mix(grad, base, 2, 0)
    copies4b = send_next(3, 1, mix(gather_sum(2, 1, parts1, copies3b), weights_back))

    skip_mix(grad, base, 2, 1)

    def last(half, copies):
        lines[half] = dot3(split(gather_wide(3, half, copies)), bank_back())

        def column(index, carry):
            rows = pl.multiple_of(index * 8, 8)
            walk = synthesis_column(lines.at[half], rows)
            for x in range(CELLS):
                packed[half, cells(x, rows), :] = walk.get(0, x) + base[half, cells(x, rows), :]
            return carry

        lax.fori_loop(0, 4, column, 0)
        store = pltpu.make_async_copy(packed.at[half], packed_hbm.at[half], out_sems.at[half])
        store.start()
        return store

    line_start(1, line_sum(0))

    store0 = last(0, copies4a)
    store1 = last(1, copies4b)

    scale = F32(1.0 / (BATCH * CELLS * CELLS * nx * ny))
    result[core] = line_sum(1) * scale
    swap_back = to_partner(1, result.at[core], result.at[core])
    swap_back.start()

    for copies in (copies1a, copies1b, copies2a, copies2b, copies3a, copies3b, copies4a, copies4b):
        for copy in copies:
            copy.wait_send()
    for axis in range(2):
        each(axis, lambda r, other, device: line_copy(axis, r, device).wait_send())
    swap.wait_send()
    store0.wait()
    store1.wait()

    swap_back.wait()
    store = pltpu.make_async_copy(result, sum_hbm, out_sems.at[2])
    store.start()
    store.wait()


def unpack_kernel(
    packed_hbm, sum_hbm, out_hbm, gc_hbm, gd_hbm, gs_hbm, packed, summed, grads, out, in_sems, out_sems
):
    cells = CELLS // 2
    rows = cells * CH
    loads = []
    for half in range(2):
        for part in range(2):
            here = pl.ds(part * rows, rows)
            loads.append(
                pltpu.make_async_copy(
                    packed_hbm.at[half, here], packed.at[half, here], in_sems.at[2 * half + part]
                )
            )
    loads.append(pltpu.make_async_copy(sum_hbm, summed, in_sems.at[4]))
    for load in loads[4:] + loads[:4]:
        load.start()
    stores = []
    loads[4].wait()
    for i, target in enumerate((gc_hbm, gd_hbm, gs_hbm)):
        for part in range(2):
            rows_here = slice(part * CH // 2, (part + 1) * CH // 2)
            grads[i, rows_here] = summed[part, :, i * CH : (i + 1) * CH]
        store = pltpu.make_async_copy(grads.at[i], target, out_sems.at[4 + i])
        store.start()
        stores.append(store)
    for half in range(2):
        for part in range(2):
            loads[2 * half + part].wait()
            values = packed[half, part * rows : (part + 1) * rows]
            there = slice(part * cells, (part + 1) * cells)
            for pair in range(2):
                lanes = slice(64 * pair, 64 * pair + CELLS)
                out[2 * half + pair, there] = values[:, lanes].reshape(cells, CH, CELLS)
            target = (pl.ds(2 * half, 2), pl.ds(part * cells, cells))
            store = pltpu.make_async_copy(out.at[target], out_hbm.at[target], out_sems.at[2 * half + part])
            store.start()
            stores.append(store)
    for store in stores:
        store.wait()


def shards(nx, ny, field, w_coarse, w_detail, w_skip, cotangent):
    block = (BATCH, CELLS, CH, CELLS)
    packed = pltpu.VMEM((2, CELLS * CH, 128), F32)
    hbm = pl.BlockSpec(memory_space=pl.ANY)
    weight = pltpu.VMEM((CH, CH), F32)
    small = jax.ShapeDtypeStruct((CH, CH), F32)
    peers = max(nx, ny // 2)
    half_sum = (CH // 2, 128)
    bank = bank_matrix()
    packed_field, summed = pl.pallas_call(
        functools.partial(kernel, nx, ny),
        out_shape=(
            jax.ShapeDtypeStruct((2, CELLS * CH, 128), F32),
            jax.ShapeDtypeStruct((2, *half_sum), F32),
        ),
        in_specs=[hbm] * 7,
        out_specs=(hbm, hbm),
        scratch_shapes=[
            pltpu.VMEM(block, F32),
            pltpu.VMEM(block, F32),
            packed,
            packed,
            packed,
            packed,
            packed,
            pltpu.VMEM((2, 2 * ROWS, 512), F32),
            pltpu.VMEM((4, 256, 256), F32),
            weight,
            weight,
            weight,
            pltpu.VMEM((512, 256), F32),
            pltpu.VMEM((2, 512, 256), BF16),
            pltpu.VMEM((256, 512), F32),
            pltpu.VMEM((2, 256, 512), BF16),
            pltpu.VMEM((2, 2, 2, 2 * ROWS, 128), F32),
            pltpu.VMEM((2, 2, 2 * ROWS, 128), F32),
            pltpu.VMEM((2, 2, 6 * ROWS, 128), F32),
            pltpu.VMEM((2, 2, 2 * ROWS, 128), F32),
            pltpu.VMEM((2, 2 * ROWS, 256), F32),
            packed,
            pltpu.VMEM(half_sum, F32),
            pltpu.VMEM((2, peers, *half_sum), F32),
            pltpu.VMEM((2, *half_sum), F32),
            pltpu.VMEM((2, *half_sum), F32),
            pltpu.VMEM((2, *half_sum), F32),
            pltpu.SemaphoreType.DMA((15,)),
            pltpu.SemaphoreType.DMA((3,)),
            pltpu.SemaphoreType.DMA((4, 2, 5)),
            pltpu.SemaphoreType.DMA((4, 2, 5)),
            pltpu.SemaphoreType.DMA((2, peers)),
            pltpu.SemaphoreType.DMA((2, peers)),
            pltpu.SemaphoreType.DMA((2,)),
            pltpu.SemaphoreType.DMA((2,)),
        ],
        compiler_params=pltpu.CompilerParams(
            collective_id=0, has_side_effects=True, vmem_limit_bytes=60 * 1024 * 1024
        ),
    )(
        jnp.transpose(field, (0, 1, 3, 2)),
        jnp.transpose(cotangent, (0, 1, 3, 2)),
        w_coarse,
        w_detail,
        w_skip,
        jnp.asarray(bank),
        jnp.asarray(np.ascontiguousarray(bank.T)),
    )
    grad_field, *grads = pl.pallas_call(
        unpack_kernel,
        out_shape=(jax.ShapeDtypeStruct(block, F32), small, small, small),
        in_specs=[hbm, hbm],
        out_specs=(hbm, hbm, hbm, hbm),
        scratch_shapes=[
            packed,
            pltpu.VMEM((2, *half_sum), F32),
            pltpu.VMEM((3, CH, CH), F32),
            pltpu.VMEM(block, F32),
            pltpu.SemaphoreType.DMA((5,)),
            pltpu.SemaphoreType.DMA((7,)),
        ],
        compiler_params=pltpu.CompilerParams(vmem_limit_bytes=60 * 1024 * 1024),
    )(packed_field, summed)
    return (jnp.transpose(grad_field, (0, 1, 3, 2)), *grads)


def solution(mesh):
    nx, ny = mesh.shape["gx"], mesh.shape["gy"]
    in_specs = (P(None, "gx", "gy", None), P(), P(), P(), P(None, "gx", "gy", None))
    out_specs = (P(None, "gx", "gy", None), P(), P(), P())

    def run(*args):
        return shards(nx, ny, *args)

    return jax.shard_map(run, mesh=mesh, in_specs=in_specs, out_specs=out_specs, check_vma=False)
```

```python
import functools

import jax
import jax.numpy as jnp
import numpy as np
from jax import lax
from jax.experimental import pallas as pl
from jax.experimental.pallas import tpu as pltpu
from jax.sharding import PartitionSpec as P

LOW_TAPS = [
    0.23037781330885523,
    0.7148465705525415,
    0.6308807679295904,
    -0.02798376941698385,
    -0.18703481171888114,
    0.030841381835986965,
    0.032883011666982945,
    -0.010597401784997278,
]
HIGH_TAPS = [(-1) ** offset * LOW_TAPS[7 - offset] for offset in range(8)]

F32 = jnp.float32
BF16 = jnp.bfloat16
MESH = pl.DeviceIdType.MESH
CH = 32
BATCH = 4
CELLS = 48
COARSE = 6
ROWS = COARSE * CH // 2
GELU_A = 0.7978845608028654
GELU_B = GELU_A * 0.044715


def bounds(low, high):
    return -((7 - low) // 2), high // 2


LEVELS = [(0, CELLS - 1)]
for _ in range(3):
    LEVELS.append(bounds(*LEVELS[-1]))


def line_matrix():
    values = np.eye(CELLS)
    low, high = LEVELS[0]
    outputs = []
    for level in range(3):
        bank = [LOW_TAPS] if level < 2 else [LOW_TAPS, HIGH_TAPS]
        first, last = LEVELS[level + 1]
        outputs = []
        for taps in bank:
            result = np.zeros((last - first + 1, CELLS))
            for k in range(first, last + 1):
                for j in range(8):
                    if low <= 2 * k + j <= high:
                        result[k - first] += taps[j] * values[2 * k + j - low]
            outputs.append(result)
        values, low, high = outputs[0], first, last
    return np.stack(outputs)


def bank_matrix():
    line = line_matrix()
    result = np.zeros((2, 2, 2, 64, 2, 2, 64))
    for group in range(2):
        for xband in range(2):
            for b in range(2):
                for part in range(2):
                    for yband in range(2):
                        for k in range(COARSE):
                            lane = ((xband * 2 + yband) * COARSE + k) * 2 + b
                            result[group, xband, b, :CELLS, part, group, lane] = line[yband, part * COARSE + k]
    return result.reshape(512, 256).astype(np.float32)


def split(values):
    high = values.astype(BF16)
    return high, (values - high.astype(F32)).astype(BF16)


def dot3(left, right, dims=((1,), (0,))):
    form = (dims, ((), ()))
    rows = left[0].shape[0]
    both = lax.dot_general(jnp.concatenate(left, axis=0), right[0], form, preferred_element_type=F32)
    return both[:rows] + both[rows:] + lax.dot_general(left[0], right[1], form, preferred_element_type=F32)


NT = ((1,), (1,))


class Analysis:
    def __init__(self, load):
        self.load = load
        self.memo = {}

    def get(self, level, k, taps=LOW_TAPS, band=0):
        if level == 0:
            if (0, k) not in self.memo:
                self.memo[0, k] = self.load(k)
            return self.memo[0, k]
        key = (level, k, band)
        if key not in self.memo:
            low, high = LEVELS[level - 1]
            total = None
            for j in range(8):
                if low <= 2 * k + j <= high:
                    term = self.get(level - 1, 2 * k + j) * F32(taps[j])
                    total = term if total is None else total + term
            self.memo[key] = total
        return self.memo[key]


class Synthesis:
    def __init__(self, load):
        self.load = load
        self.memo = {}

    def top(self, band, k):
        if (band, k) not in self.memo:
            self.memo[band, k] = self.load(band, k)
        return self.memo[band, k]

    def get(self, level, i):
        key = (level, i, "s")
        if key not in self.memo:
            low, high = LEVELS[level + 1]
            total = None
            for k in range(low, high + 1):
                j = i - 2 * k
                if 0 <= j < 8:
                    if level == 2:
                        term = self.top(0, k) * F32(LOW_TAPS[j]) + self.top(1, k) * F32(HIGH_TAPS[j])
                    else:
                        term = self.get(level + 1, k) * F32(LOW_TAPS[j])
                    total = term if total is None else total + term
            self.memo[key] = total
        return self.memo[key]


def synthesis_column(lines, rows):
    def load(band, k):
        part, group, row = (k + COARSE) // 6, (k + COARSE) % 6 // 3, (k + COARSE) % 3
        start = (part * 3 + row) * CH
        lanes = group * 256 + band * 128
        return lines[pl.ds(pl.multiple_of(start + rows, 8), 8), lanes : lanes + 128]

    return Synthesis(load)


def analyze_column(lines, rows, load):
    walk = Analysis(load)
    for k in range(-COARSE, COARSE):
        part, group, row = (k + COARSE) // 6, (k + COARSE) % 6 // 3, (k + COARSE) % 3
        start = (part * 3 + row) * CH
        for band, taps in enumerate((LOW_TAPS, HIGH_TAPS)):
            lanes = group * 256 + band * 128
            lines[pl.ds(pl.multiple_of(start + rows, 8), 8), lanes : lanes + 128] = walk.get(3, k, taps, band)


def side_by_side(values):
    return jnp.concatenate([values[k : k + CH] for k in range(0, values.shape[0], CH)], axis=1)


def in_coarse(values):
    return lax.rem(lax.broadcasted_iota(jnp.int32, values.shape, 1), 64) < 12


def mix(values, weights):
    count, width = values.shape[0] // CH, values.shape[1]
    both = dot3(weights, split(side_by_side(values)))
    chosen = jnp.where(in_coarse(both[:CH]), both[:CH], both[CH:])
    return jnp.concatenate([chosen[:, k * width : (k + 1) * width] for k in range(count)], axis=0)


def pack(source, target, half):
    for pair in range(2):
        values = source[2 * half + pair].reshape(CELLS * CH, CELLS)
        target[half, :, 64 * pair : 64 * pair + CELLS] = values


def kernel(
    nx, ny, field_hbm, cot_hbm, wc_hbm, wd_hbm, ws_hbm, bank_hbm, back_hbm, packed_hbm, sum_hbm,
    raw, raw_cot, field, cot, grad, skip, base, lines, kron, wc_ref, wd_ref, ws_ref, bank_ref, bank_parts, back_ref, back_parts,
    send_fwd, send_mix, recv_sum, recv_next, wide, packed, ar_pair, ar_in, ar_part, gsum, result,
    in_sems, out_sems, ex_send, ex_recv, ar_send, ar_recv, pair_send, pair_recv,
):
    gx = lax.axis_index("gx")
    gy = lax.axis_index("gy")
    right, left = lax.rem(gx + 1, nx), lax.rem(gx + nx - 1, nx)
    up, down = lax.rem(gy + 1, ny), lax.rem(gy + ny - 1, ny)

    def piece(source, target, b, part):
        here = (b, pl.ds(part * (CELLS // 2), CELLS // 2))
        return source.at[here], target.at[here]

    moves = [piece(field_hbm, raw, b, part) for b in range(2) for part in range(2)]
    moves += [(bank_hbm, bank_ref)]
    moves += [piece(field_hbm, raw, b, part) for b in range(2, 4) for part in range(2)]
    moves += [(wc_hbm, wc_ref), (wd_hbm, wd_ref), (ws_hbm, ws_ref), (back_hbm, back_ref)]
    moves += [(cot_hbm.at[pl.ds(2 * half, 2)], raw_cot.at[pl.ds(2 * half, 2)]) for half in range(2)]
    loads = [pltpu.make_async_copy(source, target, in_sems.at[i]) for i, (source, target) in enumerate(moves)]
    for load in loads:
        load.start()

    barrier = pltpu.get_barrier_semaphore()

    core, depth = lax.rem(gy, 2), ny // 2
    my_z = lax.div(gy, 2)
    partner = (gx, gy + 1 - 2 * core)

    def line(axis):
        if axis == 0:
            return nx, gx, lambda other: (other, gy)
        return depth, my_z, lambda other: (gx, other * 2 + core)

    def greet(device):
        pl.semaphore_signal(barrier, inc=1, device_id=device, device_id_type=MESH)

    def each(axis, action):
        size, me, device = line(axis)

        for r in range(1, size):
            other = lax.rem(me + r, size)
            action(r, other, device(other))

    for device in ((right, gy), (left, gy), (gx, up), (gx, down)):
        greet(device)
    for device in ((right, up), (left, down), (right, down), (left, up)):
        greet(device)
    greet(partner)
    for axis in range(2):
        each(axis, lambda r, other, device: greet(device))

    field[...] = jnp.zeros(field.shape, F32)

    def bank():
        return bank_parts[0], bank_parts[1]

    def bank_back():
        return back_parts[0], back_parts[1]

    def exchange(step, half, moves):
        copies = []
        for slot, (source, target, device) in enumerate(moves):
            copy = pltpu.make_async_remote_copy(
                src_ref=source,
                dst_ref=target,
                send_sem=ex_send.at[step, half, slot],
                recv_sem=ex_recv.at[step, half, slot],
                device_id=device,
                device_id_type=MESH,
            )
            copy.start()
            copies.append(copy)
        return copies

    def send_partials(step, half):
        parts = dot3(split(lines[half]), bank())
        before, own = send_fwd.at[step // 2, half, 0], send_fwd.at[step // 2, half, 1]
        before[...] = parts[:, :128]
        own[...] = parts[:, 128:]
        arrived = recv_sum.at[step // 2, half]
        first, second = pl.ds(0, ROWS), pl.ds(ROWS, ROWS)
        moves = [
            (before.at[first], arrived.at[pl.ds(0, ROWS)], (left, down)),
            (before.at[second], arrived.at[pl.ds(ROWS, ROWS)], (right, down)),
            (own.at[first], arrived.at[pl.ds(2 * ROWS, ROWS)], (left, gy)),
            (own.at[second], arrived.at[pl.ds(3 * ROWS, ROWS)], (right, gy)),
            (before, arrived.at[pl.ds(4 * ROWS, 2 * ROWS)], (gx, down)),
        ]
        return parts, exchange(step, half, moves)

    def gather_sum(step, half, parts, copies):
        for copy in copies:
            copy.wait_recv()
        arrived = recv_sum[step // 2, half]
        total = parts[:, 128:] + arrived[4 * ROWS :]
        above = arrived[ROWS : 2 * ROWS] + arrived[3 * ROWS : 4 * ROWS]
        below = arrived[:ROWS] + arrived[2 * ROWS : 3 * ROWS]
        return total + jnp.concatenate([above, below], axis=0)

    def send_next(step, half, values):
        send_mix[step // 2, half] = values
        return exchange(step, half, [(send_mix.at[step // 2, half], recv_next.at[step // 2, half], (gx, up))])

    def gather_wide(step, half, copies):
        for copy in copies:
            copy.wait_recv()
        return jnp.concatenate([recv_next[step // 2, half], send_mix[step // 2, half]], axis=1)

    def cells(x, rows):
        return pl.ds(pl.multiple_of(x * CH + rows, 8), 8)

    def first(half):
        for pair in range(2):
            for part in range(2):
                loads[5 * half + 2 * pair + part].wait()
                here = slice(part * (CELLS // 2), (part + 1) * (CELLS // 2))
                rows = slice(part * (CELLS // 2) * CH, (part + 1) * (CELLS // 2) * CH)
                values = raw[2 * half + pair, here].reshape(CELLS // 2 * CH, CELLS)
                field[half, rows, 64 * pair : 64 * pair + CELLS] = values

        def column(index, carry):
            rows = pl.multiple_of(index * 8, 8)
            analyze_column(lines.at[half], rows, lambda x: field[half, cells(x, rows), :])
            return carry

        lax.fori_loop(0, 4, column, 0)

    first(0)
    loads[4].wait()
    bank_parts[0], bank_parts[1] = split(bank_ref[...])
    pl.semaphore_wait(barrier, 8 + 1 + nx - 1 + depth - 1)
    parts0, copies1a = send_partials(0, 0)
    first(1)
    parts1, copies1b = send_partials(0, 1)

    eye = (
        lax.broadcasted_iota(jnp.int32, (CH, CH), 0) == lax.broadcasted_iota(jnp.int32, (CH, CH), 1)
    ).astype(BF16)

    def transposed(weight):
        form = (NT, ((), ()))
        return lax.dot_general(eye, weight, form, preferred_element_type=F32).astype(BF16)

    for load in loads[9:13]:
        load.wait()
    back_parts[0], back_parts[1] = split(back_ref[...])
    coarse_parts = split(wc_ref[...])
    detail_parts = split(wd_ref[...])
    skip_parts = split(ws_ref[...])
    weights_forward = tuple(
        jnp.concatenate([transposed(c), transposed(d)], axis=0) for c, d in zip(coarse_parts, detail_parts)
    )
    weights_back = tuple(jnp.concatenate([c, d], axis=0) for c, d in zip(coarse_parts, detail_parts))

    cot[...] = jnp.zeros(cot.shape, F32)
    kron[...] = jnp.zeros(kron.shape, F32)
    for which in range(2):
        forward = transposed(skip_parts[which]).astype(F32)
        backward = skip_parts[which].astype(F32)
        for i in range(8):
            block = slice(i * CH, (i + 1) * CH)
            kron[which, block, block] = forward
            kron[2 + which, block, block] = backward

    def skip_mix(source, target, kind, half):
        weights = (kron[kind].astype(BF16), kron[kind + 1].astype(BF16))
        for g in range(6):
            block = slice(256 * g, 256 * g + 256)
            target[half, block] = dot3(weights, split(source[half, block]))

    skip_mix(field, skip, 0, 0)
    loads[13].wait()
    pack(raw_cot, cot, 0)

    copies2a = send_next(1, 0, gather_sum(0, 0, parts0, copies1a))

    loads[14].wait()
    pack(raw_cot, cot, 1)

    copies2b = send_next(1, 1, gather_sum(0, 1, parts1, copies1b))

    skip_mix(field, skip, 0, 1)

    def middle(half, copies):
        values = gather_wide(1, half, copies)
        wide[half] = values
        lines[half] = dot3(split(mix(values, weights_forward)), bank_back())

        def column(index, carry):
            rows = pl.multiple_of(index * 8, 8)
            walk = synthesis_column(lines.at[half], rows)

            def load(x):
                here = cells(x, rows)
                pre = walk.get(0, x) + skip[half, here, :]
                cube = F32(GELU_B) * (pre * pre)
                tanh = jnp.tanh(pre * (F32(GELU_A) + cube))
                slope = pre * (F32(GELU_A) + F32(3.0) * cube)
                rise = (F32(0.5) + F32(0.5) * tanh) * (F32(1.0) + (slope - slope * tanh))
                value = cot[half, here, :] * rise
                grad[half, here, :] = value
                return value

            analyze_column(lines.at[half], rows, load)
            return carry

        lax.fori_loop(0, 4, column, 0)
        return send_partials(2, half)

    parts0, copies3a = middle(0, copies2a)
    parts1, copies3b = middle(1, copies2b)

    def share(half, parts):
        flat = side_by_side(parts)
        coarse = in_coarse(flat)
        masked = jnp.concatenate([jnp.where(coarse, flat, 0.0), jnp.where(coarse, 0.0, flat)], axis=0)
        both = dot3(split(side_by_side(wide[half])), split(masked), NT)
        return both, dot3(split(side_by_side(field[half])), split(side_by_side(grad[half])), NT)

    both0, skip0 = share(0, parts0)
    both1, skip1 = share(1, parts1)

    def fold(values):
        return jnp.concatenate([values[8 * g : 8 * g + 8] for g in range(4)], axis=1)

    both = both0 + both1
    share_sum = jnp.concatenate([fold(both[:, :CH]), fold(both[:, CH:]), fold(skip0 + skip1)], axis=0)
    gsum[0] = share_sum[:12]
    gsum[1] = share_sum[12:]

    def to_partner(phase, source, target):
        return pltpu.make_async_remote_copy(
            src_ref=source,
            dst_ref=target,
            send_sem=pair_send.at[phase],
            recv_sem=pair_recv.at[phase],
            device_id=partner,
            device_id_type=MESH,
        )

    def line_copy(axis, r, device):
        me = line(axis)[1]
        return pltpu.make_async_remote_copy(
            src_ref=ar_part.at[axis],
            dst_ref=ar_in.at[axis, me],
            send_sem=ar_send.at[axis, r],
            recv_sem=ar_recv.at[axis, me],
            device_id=device,
            device_id_type=MESH,
        )

    def line_start(axis, total):
        ar_part[axis] = total
        ar_in[axis, line(axis)[1]] = total
        each(axis, lambda r, other, device: line_copy(axis, r, device).start())

    def line_sum(axis):
        def arrive(r, other, device):
            arrived = ar_in.at[axis, other]
            pltpu.make_async_copy(arrived, arrived, ar_recv.at[axis, other]).wait()

        each(axis, arrive)
        total = ar_in[axis, 0]
        for i in range(1, line(axis)[0]):
            total = total + ar_in[axis, i]
        return total

    swap = to_partner(0, gsum.at[1 - core], ar_pair)
    swap.start()

    copies4a = send_next(3, 0, mix(gather_sum(2, 0, parts0, copies3a), weights_back))

    swap.wait_recv()
    line_start(0, gsum[core] + ar_pair[...])

    skip_mix(grad, base, 2, 0)
    copies4b = send_next(3, 1, mix(gather_sum(2, 1, parts1, copies3b), weights_back))

    skip_mix(grad, base, 2, 1)

    def last(half, copies):
        lines[half] = dot3(split(gather_wide(3, half, copies)), bank_back())

        def column(index, carry):
            rows = pl.multiple_of(index * 8, 8)
            walk = synthesis_column(lines.at[half], rows)
            for x in range(CELLS):
                packed[half, cells(x, rows), :] = walk.get(0, x) + base[half, cells(x, rows), :]
            return carry

        lax.fori_loop(0, 4, column, 0)
        store = pltpu.make_async_copy(packed.at[half], packed_hbm.at[half], out_sems.at[half])
        store.start()
        return store

    line_start(1, line_sum(0))

    store0 = last(0, copies4a)
    store1 = last(1, copies4b)

    scale = F32(1.0 / (BATCH * CELLS * CELLS * nx * ny))
    result[core] = line_sum(1) * scale
    swap_back = to_partner(1, result.at[core], result.at[core])
    swap_back.start()

    for copies in (copies1a, copies1b, copies2a, copies2b, copies3a, copies3b, copies4a, copies4b):
        for copy in copies:
            copy.wait_send()
    for axis in range(2):
        each(axis, lambda r, other, device: line_copy(axis, r, device).wait_send())
    swap.wait_send()
    store0.wait()
    store1.wait()

    swap_back.wait()
    store = pltpu.make_async_copy(result, sum_hbm, out_sems.at[2])
    store.start()
    store.wait()


def unpack_kernel(
    packed_hbm, sum_hbm, out_hbm, gc_hbm, gd_hbm, gs_hbm, packed, summed, grads, out, in_sems, out_sems
):
    cells = CELLS // 2
    rows = cells * CH
    loads = []
    for half in range(2):
        for part in range(2):
            here = pl.ds(part * rows, rows)
            loads.append(
                pltpu.make_async_copy(
                    packed_hbm.at[half, here], packed.at[half, here], in_sems.at[2 * half + part]
                )
            )
    loads.append(pltpu.make_async_copy(sum_hbm, summed, in_sems.at[4]))
    for load in loads[4:] + loads[:4]:
        load.start()
    stores = []
    loads[4].wait()
    folded = jnp.concatenate([summed[0], summed[1]], axis=0)
    for i, target in enumerate((gc_hbm, gd_hbm, gs_hbm)):
        for g in range(4):
            grads[i, 8 * g : 8 * g + 8] = folded[8 * i : 8 * i + 8, CH * g : CH * g + CH]
        store = pltpu.make_async_copy(grads.at[i], target, out_sems.at[4 + i])
        store.start()
        stores.append(store)
    for half in range(2):
        for part in range(2):
            loads[2 * half + part].wait()
            values = packed[half, part * rows : (part + 1) * rows]
            there = slice(part * cells, (part + 1) * cells)
            for pair in range(2):
                lanes = slice(64 * pair, 64 * pair + CELLS)
                out[2 * half + pair, there] = values[:, lanes].reshape(cells, CH, CELLS)
            target = (pl.ds(2 * half, 2), pl.ds(part * cells, cells))
            store = pltpu.make_async_copy(out.at[target], out_hbm.at[target], out_sems.at[2 * half + part])
            store.start()
            stores.append(store)
    for store in stores:
        store.wait()


def shards(nx, ny, field, w_coarse, w_detail, w_skip, cotangent):
    block = (BATCH, CELLS, CH, CELLS)
    packed = pltpu.VMEM((2, CELLS * CH, 128), F32)
    hbm = pl.BlockSpec(memory_space=pl.ANY)
    weight = pltpu.VMEM((CH, CH), F32)
    small = jax.ShapeDtypeStruct((CH, CH), F32)
    peers = max(nx, ny // 2)
    half_sum = (12, 128)
    bank = bank_matrix()
    packed_field, summed = pl.pallas_call(
        functools.partial(kernel, nx, ny),
        out_shape=(
            jax.ShapeDtypeStruct((2, CELLS * CH, 128), F32),
            jax.ShapeDtypeStruct((2, *half_sum), F32),
        ),
        in_specs=[hbm] * 7,
        out_specs=(hbm, hbm),
        scratch_shapes=[
            pltpu.VMEM(block, F32),
            pltpu.VMEM(block, F32),
            packed,
            packed,
            packed,
            packed,
            packed,
            pltpu.VMEM((2, 2 * ROWS, 512), F32),
            pltpu.VMEM((4, 256, 256), F32),
            weight,
            weight,
            weight,
            pltpu.VMEM((512, 256), F32),
            pltpu.VMEM((2, 512, 256), BF16),
            pltpu.VMEM((256, 512), F32),
            pltpu.VMEM((2, 256, 512), BF16),
            pltpu.VMEM((2, 2, 2, 2 * ROWS, 128), F32),
            pltpu.VMEM((2, 2, 2 * ROWS, 128), F32),
            pltpu.VMEM((2, 2, 6 * ROWS, 128), F32),
            pltpu.VMEM((2, 2, 2 * ROWS, 128), F32),
            pltpu.VMEM((2, 2 * ROWS, 256), F32),
            packed,
            pltpu.VMEM(half_sum, F32),
            pltpu.VMEM((2, peers, *half_sum), F32),
            pltpu.VMEM((2, *half_sum), F32),
            pltpu.VMEM((2, *half_sum), F32),
            pltpu.VMEM((2, *half_sum), F32),
            pltpu.SemaphoreType.DMA((15,)),
            pltpu.SemaphoreType.DMA((3,)),
            pltpu.SemaphoreType.DMA((4, 2, 5)),
            pltpu.SemaphoreType.DMA((4, 2, 5)),
            pltpu.SemaphoreType.DMA((2, peers)),
            pltpu.SemaphoreType.DMA((2, peers)),
            pltpu.SemaphoreType.DMA((2,)),
            pltpu.SemaphoreType.DMA((2,)),
        ],
        compiler_params=pltpu.CompilerParams(
            collective_id=0, has_side_effects=True, vmem_limit_bytes=60 * 1024 * 1024
        ),
    )(
        jnp.transpose(field, (0, 1, 3, 2)),
        jnp.transpose(cotangent, (0, 1, 3, 2)),
        w_coarse,
        w_detail,
        w_skip,
        jnp.asarray(bank),
        jnp.asarray(np.ascontiguousarray(bank.T)),
    )
    grad_field, *grads = pl.pallas_call(
        unpack_kernel,
        out_shape=(jax.ShapeDtypeStruct(block, F32), small, small, small),
        in_specs=[hbm, hbm],
        out_specs=(hbm, hbm, hbm, hbm),
        scratch_shapes=[
            packed,
            pltpu.VMEM((2, *half_sum), F32),
            pltpu.VMEM((3, CH, CH), F32),
            pltpu.VMEM(block, F32),
            pltpu.SemaphoreType.DMA((5,)),
            pltpu.SemaphoreType.DMA((7,)),
        ],
        compiler_params=pltpu.CompilerParams(vmem_limit_bytes=60 * 1024 * 1024),
    )(packed_field, summed)
    return (jnp.transpose(grad_field, (0, 1, 3, 2)), *grads)


def solution(mesh):
    nx, ny = mesh.shape["gx"], mesh.shape["gy"]
    in_specs = (P(None, "gx", "gy", None), P(), P(), P(), P(None, "gx", "gy", None))
    out_specs = (P(None, "gx", "gy", None), P(), P(), P())

    def run(*args):
        return shards(nx, ny, *args)

    return jax.shard_map(run, mesh=mesh, in_specs=in_specs, out_specs=out_specs, check_vma=False)
```

```python
import functools

import jax
import jax.numpy as jnp
import numpy as np
from jax import lax
from jax.experimental import pallas as pl
from jax.experimental.pallas import tpu as pltpu
from jax.sharding import PartitionSpec as P

LOW_TAPS = [
    0.23037781330885523,
    0.7148465705525415,
    0.6308807679295904,
    -0.02798376941698385,
    -0.18703481171888114,
    0.030841381835986965,
    0.032883011666982945,
    -0.010597401784997278,
]
HIGH_TAPS = [(-1) ** offset * LOW_TAPS[7 - offset] for offset in range(8)]

UNIT_LOW = [tap / LOW_TAPS[1] for tap in LOW_TAPS]
UNIT_HIGH = [tap / LOW_TAPS[1] for tap in HIGH_TAPS]

F32 = jnp.float32
BF16 = jnp.bfloat16
MESH = pl.DeviceIdType.MESH
CH = 32
BATCH = 4
CELLS = 48
COARSE = 6
ROWS = COARSE * CH // 2
GELU_A = 0.7978845608028654
GELU_B = GELU_A * 0.044715


def bounds(low, high):
    return -((7 - low) // 2), high // 2


LEVELS = [(0, CELLS - 1)]
for _ in range(3):
    LEVELS.append(bounds(*LEVELS[-1]))


def line_matrix():
    values = np.eye(CELLS)
    low, high = LEVELS[0]
    outputs = []
    for level in range(3):
        bank = [LOW_TAPS] if level < 2 else [LOW_TAPS, HIGH_TAPS]
        first, last = LEVELS[level + 1]
        outputs = []
        for taps in bank:
            result = np.zeros((last - first + 1, CELLS))
            for k in range(first, last + 1):
                for j in range(8):
                    if low <= 2 * k + j <= high:
                        result[k - first] += taps[j] * values[2 * k + j - low]
            outputs.append(result)
        values, low, high = outputs[0], first, last
    return np.stack(outputs)


def bank_matrix():
    line = line_matrix()
    result = np.zeros((2, 2, 2, 64, 2, 2, 64))
    for group in range(2):
        for xband in range(2):
            for b in range(2):
                for part in range(2):
                    for yband in range(2):
                        for k in range(COARSE):
                            lane = ((xband * 2 + yband) * COARSE + k) * 2 + b
                            result[group, xband, b, :CELLS, part, group, lane] = line[yband, part * COARSE + k]
    return (LOW_TAPS[1] ** 3 * result).reshape(512, 256).astype(np.float32)


def split(values):
    high = values.astype(BF16)
    return high, (values - high.astype(F32)).astype(BF16)


def dot3(left, right, dims=((1,), (0,))):
    form = (dims, ((), ()))
    rows = left[0].shape[0]
    both = lax.dot_general(jnp.concatenate(left, axis=0), right[0], form, preferred_element_type=F32)
    return both[:rows] + both[rows:] + lax.dot_general(left[0], right[1], form, preferred_element_type=F32)


NT = ((1,), (1,))


def times(values, tap):
    return values if tap == 1.0 else values * F32(tap)


class Analysis:
    def __init__(self, load):
        self.load = load
        self.memo = {}

    def get(self, level, k, taps=UNIT_LOW, band=0):
        if level == 0:
            if (0, k) not in self.memo:
                self.memo[0, k] = self.load(k)
            return self.memo[0, k]
        key = (level, k, band)
        if key not in self.memo:
            low, high = LEVELS[level - 1]
            total = None
            for j in range(8):
                if low <= 2 * k + j <= high:
                    term = times(self.get(level - 1, 2 * k + j), taps[j])
                    total = term if total is None else total + term
            self.memo[key] = total
        return self.memo[key]


class Synthesis:
    def __init__(self, load):
        self.load = load
        self.memo = {}

    def top(self, band, k):
        if (band, k) not in self.memo:
            self.memo[band, k] = self.load(band, k)
        return self.memo[band, k]

    def get(self, level, i):
        key = (level, i, "s")
        if key not in self.memo:
            low, high = LEVELS[level + 1]
            total = None
            for k in range(low, high + 1):
                j = i - 2 * k
                if 0 <= j < 8:
                    if level == 2:
                        term = times(self.top(0, k), UNIT_LOW[j]) + times(self.top(1, k), UNIT_HIGH[j])
                    else:
                        term = times(self.get(level + 1, k), UNIT_LOW[j])
                    total = term if total is None else total + term
            self.memo[key] = total
        return self.memo[key]


def synthesis_column(lines, rows):
    def load(band, k):
        part, group, row = (k + COARSE) // 6, (k + COARSE) % 6 // 3, (k + COARSE) % 3
        start = (part * 3 + row) * CH
        lanes = group * 256 + band * 128
        return lines[pl.ds(pl.multiple_of(start + rows, 8), 8), lanes : lanes + 128]

    return Synthesis(load)


def analyze_column(lines, rows, load):
    walk = Analysis(load)
    for k in range(-COARSE, COARSE):
        part, group, row = (k + COARSE) // 6, (k + COARSE) % 6 // 3, (k + COARSE) % 3
        start = (part * 3 + row) * CH
        for band, taps in enumerate((UNIT_LOW, UNIT_HIGH)):
            lanes = group * 256 + band * 128
            lines[pl.ds(pl.multiple_of(start + rows, 8), 8), lanes : lanes + 128] = walk.get(3, k, taps, band)


def side_by_side(values):
    return jnp.concatenate([values[k : k + CH] for k in range(0, values.shape[0], CH)], axis=1)


def in_coarse(values):
    return lax.rem(lax.broadcasted_iota(jnp.int32, values.shape, 1), 64) < 12


def mix(values, weights):
    count, width = values.shape[0] // CH, values.shape[1]
    both = dot3(weights, split(side_by_side(values)))
    chosen = jnp.where(in_coarse(both[:CH]), both[:CH], both[CH:])
    return jnp.concatenate([chosen[:, k * width : (k + 1) * width] for k in range(count)], axis=0)


def pack(source, target, half):
    for pair in range(2):
        values = source[2 * half + pair].reshape(CELLS * CH, CELLS)
        target[half, :, 64 * pair : 64 * pair + CELLS] = values


def kernel(
    nx, ny, field_hbm, cot_hbm, wc_hbm, wd_hbm, ws_hbm, bank_hbm, back_hbm, packed_hbm, sum_hbm,
    raw, raw_cot, field, cot, grad, skip, base, lines, kron, wc_ref, wd_ref, ws_ref, bank_ref, bank_parts, back_ref, back_parts,
    send_fwd, send_mix, recv_sum, recv_next, wide, packed, ar_pair, ar_in, ar_part, gsum, result,
    in_sems, out_sems, ex_send, ex_recv, ar_send, ar_recv, pair_send, pair_recv,
):
    gx = lax.axis_index("gx")
    gy = lax.axis_index("gy")
    right, left = lax.rem(gx + 1, nx), lax.rem(gx + nx - 1, nx)
    up, down = lax.rem(gy + 1, ny), lax.rem(gy + ny - 1, ny)

    def piece(source, target, b, part):
        here = (b, pl.ds(part * (CELLS // 2), CELLS // 2))
        return source.at[here], target.at[here]

    moves = [piece(field_hbm, raw, b, part) for b in range(2) for part in range(2)]
    moves += [(bank_hbm, bank_ref)]
    moves += [piece(field_hbm, raw, b, part) for b in range(2, 4) for part in range(2)]
    moves += [(wc_hbm, wc_ref), (wd_hbm, wd_ref), (ws_hbm, ws_ref), (back_hbm, back_ref)]
    moves += [(cot_hbm.at[pl.ds(2 * half, 2)], raw_cot.at[pl.ds(2 * half, 2)]) for half in range(2)]
    loads = [pltpu.make_async_copy(source, target, in_sems.at[i]) for i, (source, target) in enumerate(moves)]
    for load in loads:
        load.start()

    barrier = pltpu.get_barrier_semaphore()

    core, depth = lax.rem(gy, 2), ny // 2
    my_z = lax.div(gy, 2)
    partner = (gx, gy + 1 - 2 * core)

    def line(axis):
        if axis == 0:
            return nx, gx, lambda other: (other, gy)
        return depth, my_z, lambda other: (gx, other * 2 + core)

    def greet(device):
        pl.semaphore_signal(barrier, inc=1, device_id=device, device_id_type=MESH)

    def each(axis, action):
        size, me, device = line(axis)

        for r in range(1, size):
            other = lax.rem(me + r, size)
            action(r, other, device(other))

    for device in ((right, gy), (left, gy), (gx, up), (gx, down)):
        greet(device)
    for device in ((right, up), (left, down), (right, down), (left, up)):
        greet(device)
    greet(partner)
    for axis in range(2):
        each(axis, lambda r, other, device: greet(device))

    field[...] = jnp.zeros(field.shape, F32)

    def bank():
        return bank_parts[0], bank_parts[1]

    def bank_back():
        return back_parts[0], back_parts[1]

    def exchange(step, half, moves):
        copies = []
        for slot, (source, target, device) in enumerate(moves):
            copy = pltpu.make_async_remote_copy(
                src_ref=source,
                dst_ref=target,
                send_sem=ex_send.at[step, half, slot],
                recv_sem=ex_recv.at[step, half, slot],
                device_id=device,
                device_id_type=MESH,
            )
            copy.start()
            copies.append(copy)
        return copies

    def send_partials(step, half):
        parts = dot3(split(lines[half]), bank())
        before, own = send_fwd.at[step // 2, half, 0], send_fwd.at[step // 2, half, 1]
        before[...] = parts[:, :128]
        own[...] = parts[:, 128:]
        arrived = recv_sum.at[step // 2, half]
        first, second = pl.ds(0, ROWS), pl.ds(ROWS, ROWS)
        moves = [
            (before.at[first], arrived.at[pl.ds(0, ROWS)], (left, down)),
            (before.at[second], arrived.at[pl.ds(ROWS, ROWS)], (right, down)),
            (own.at[first], arrived.at[pl.ds(2 * ROWS, ROWS)], (left, gy)),
            (own.at[second], arrived.at[pl.ds(3 * ROWS, ROWS)], (right, gy)),
            (before, arrived.at[pl.ds(4 * ROWS, 2 * ROWS)], (gx, down)),
        ]
        return parts, exchange(step, half, moves)

    def gather_sum(step, half, parts, copies):
        for copy in copies:
            copy.wait_recv()
        arrived = recv_sum[step // 2, half]
        total = parts[:, 128:] + arrived[4 * ROWS :]
        above = arrived[ROWS : 2 * ROWS] + arrived[3 * ROWS : 4 * ROWS]
        below = arrived[:ROWS] + arrived[2 * ROWS : 3 * ROWS]
        return total + jnp.concatenate([above, below], axis=0)

    def send_next(step, half, values):
        send_mix[step // 2, half] = values
        return exchange(step, half, [(send_mix.at[step // 2, half], recv_next.at[step // 2, half], (gx, up))])

    def gather_wide(step, half, copies):
        for copy in copies:
            copy.wait_recv()
        return jnp.concatenate([recv_next[step // 2, half], send_mix[step // 2, half]], axis=1)

    def cells(x, rows):
        return pl.ds(pl.multiple_of(x * CH + rows, 8), 8)

    def first(half):
        for pair in range(2):
            for part in range(2):
                loads[5 * half + 2 * pair + part].wait()
                here = slice(part * (CELLS // 2), (part + 1) * (CELLS // 2))
                rows = slice(part * (CELLS // 2) * CH, (part + 1) * (CELLS // 2) * CH)
                values = raw[2 * half + pair, here].reshape(CELLS // 2 * CH, CELLS)
                field[half, rows, 64 * pair : 64 * pair + CELLS] = values

        def column(index, carry):
            rows = pl.multiple_of(index * 8, 8)
            analyze_column(lines.at[half], rows, lambda x: field[half, cells(x, rows), :])
            return carry

        lax.fori_loop(0, 4, column, 0)

    first(0)
    loads[4].wait()
    bank_parts[0], bank_parts[1] = split(bank_ref[...])
    pl.semaphore_wait(barrier, 8 + 1 + nx - 1 + depth - 1)
    parts0, copies1a = send_partials(0, 0)
    first(1)
    parts1, copies1b = send_partials(0, 1)

    eye = (
        lax.broadcasted_iota(jnp.int32, (CH, CH), 0) == lax.broadcasted_iota(jnp.int32, (CH, CH), 1)
    ).astype(BF16)

    def transposed(weight):
        form = (NT, ((), ()))
        return lax.dot_general(eye, weight, form, preferred_element_type=F32).astype(BF16)

    for load in loads[9:13]:
        load.wait()
    back_parts[0], back_parts[1] = split(back_ref[...])
    coarse_parts = split(wc_ref[...])
    detail_parts = split(wd_ref[...])
    skip_parts = split(ws_ref[...])
    weights_forward = tuple(
        jnp.concatenate([transposed(c), transposed(d)], axis=0) for c, d in zip(coarse_parts, detail_parts)
    )
    weights_back = tuple(jnp.concatenate([c, d], axis=0) for c, d in zip(coarse_parts, detail_parts))

    cot[...] = jnp.zeros(cot.shape, F32)
    kron[...] = jnp.zeros(kron.shape, F32)
    for which in range(2):
        forward = transposed(skip_parts[which]).astype(F32)
        backward = skip_parts[which].astype(F32)
        for i in range(8):
            block = slice(i * CH, (i + 1) * CH)
            kron[which, block, block] = forward
            kron[2 + which, block, block] = backward

    def skip_mix(source, target, kind, half):
        weights = (kron[kind].astype(BF16), kron[kind + 1].astype(BF16))
        for g in range(6):
            block = slice(256 * g, 256 * g + 256)
            target[half, block] = dot3(weights, split(source[half, block]))

    skip_mix(field, skip, 0, 0)
    loads[13].wait()
    pack(raw_cot, cot, 0)

    copies2a = send_next(1, 0, gather_sum(0, 0, parts0, copies1a))

    loads[14].wait()
    pack(raw_cot, cot, 1)

    copies2b = send_next(1, 1, gather_sum(0, 1, parts1, copies1b))

    skip_mix(field, skip, 0, 1)

    def middle(half, copies):
        values = gather_wide(1, half, copies)
        wide[half] = values
        lines[half] = dot3(split(mix(values, weights_forward)), bank_back())

        def column(index, carry):
            rows = pl.multiple_of(index * 8, 8)
            walk = synthesis_column(lines.at[half], rows)

            def load(x):
                here = cells(x, rows)
                pre = walk.get(0, x) + skip[half, here, :]
                cube = F32(GELU_B) * (pre * pre)
                tanh = jnp.tanh(pre * (F32(GELU_A) + cube))
                slope = pre * (F32(GELU_A) + F32(3.0) * cube)
                rise = (F32(0.5) + F32(0.5) * tanh) * (F32(1.0) + (slope - slope * tanh))
                value = cot[half, here, :] * rise
                grad[half, here, :] = value
                return value

            analyze_column(lines.at[half], rows, load)
            return carry

        lax.fori_loop(0, 4, column, 0)
        return send_partials(2, half)

    parts0, copies3a = middle(0, copies2a)
    parts1, copies3b = middle(1, copies2b)

    def share(half, parts):
        flat = side_by_side(parts)
        coarse = in_coarse(flat)
        masked = jnp.concatenate([jnp.where(coarse, flat, 0.0), jnp.where(coarse, 0.0, flat)], axis=0)
        both = dot3(split(side_by_side(wide[half])), split(masked), NT)
        return both, dot3(split(side_by_side(field[half])), split(side_by_side(grad[half])), NT)

    both0, skip0 = share(0, parts0)
    both1, skip1 = share(1, parts1)

    def fold(values):
        return jnp.concatenate([values[8 * g : 8 * g + 8] for g in range(4)], axis=1)

    both = both0 + both1
    share_sum = jnp.concatenate([fold(both[:, :CH]), fold(both[:, CH:]), fold(skip0 + skip1)], axis=0)
    gsum[0] = share_sum[:12]
    gsum[1] = share_sum[12:]

    def to_partner(phase, source, target):
        return pltpu.make_async_remote_copy(
            src_ref=source,
            dst_ref=target,
            send_sem=pair_send.at[phase],
            recv_sem=pair_recv.at[phase],
            device_id=partner,
            device_id_type=MESH,
        )

    def line_copy(axis, r, device):
        me = line(axis)[1]
        return pltpu.make_async_remote_copy(
            src_ref=ar_part.at[axis],
            dst_ref=ar_in.at[axis, me],
            send_sem=ar_send.at[axis, r],
            recv_sem=ar_recv.at[axis, me],
            device_id=device,
            device_id_type=MESH,
        )

    def line_start(axis, total):
        ar_part[axis] = total
        ar_in[axis, line(axis)[1]] = total
        each(axis, lambda r, other, device: line_copy(axis, r, device).start())

    def line_sum(axis):
        def arrive(r, other, device):
            arrived = ar_in.at[axis, other]
            pltpu.make_async_copy(arrived, arrived, ar_recv.at[axis, other]).wait()

        each(axis, arrive)
        total = ar_in[axis, 0]
        for i in range(1, line(axis)[0]):
            total = total + ar_in[axis, i]
        return total

    swap = to_partner(0, gsum.at[1 - core], ar_pair)
    swap.start()

    copies4a = send_next(3, 0, mix(gather_sum(2, 0, parts0, copies3a), weights_back))

    swap.wait_recv()
    line_start(0, gsum[core] + ar_pair[...])

    skip_mix(grad, base, 2, 0)
    copies4b = send_next(3, 1, mix(gather_sum(2, 1, parts1, copies3b), weights_back))

    skip_mix(grad, base, 2, 1)

    def last(half, copies):
        lines[half] = dot3(split(gather_wide(3, half, copies)), bank_back())

        def column(index, carry):
            rows = pl.multiple_of(index * 8, 8)
            walk = synthesis_column(lines.at[half], rows)
            for x in range(CELLS):
                packed[half, cells(x, rows), :] = walk.get(0, x) + base[half, cells(x, rows), :]
            return carry

        lax.fori_loop(0, 4, column, 0)
        store = pltpu.make_async_copy(packed.at[half], packed_hbm.at[half], out_sems.at[half])
        store.start()
        return store

    line_start(1, line_sum(0))

    store0 = last(0, copies4a)
    store1 = last(1, copies4b)

    scale = F32(1.0 / (BATCH * CELLS * CELLS * nx * ny))
    result[core] = line_sum(1) * scale
    swap_back = to_partner(1, result.at[core], result.at[core])
    swap_back.start()

    for copies in (copies1a, copies1b, copies2a, copies2b, copies3a, copies3b, copies4a, copies4b):
        for copy in copies:
            copy.wait_send()
    for axis in range(2):
        each(axis, lambda r, other, device: line_copy(axis, r, device).wait_send())
    swap.wait_send()
    store0.wait()
    store1.wait()

    swap_back.wait()
    store = pltpu.make_async_copy(result, sum_hbm, out_sems.at[2])
    store.start()
    store.wait()


def unpack_kernel(
    packed_hbm, sum_hbm, out_hbm, gc_hbm, gd_hbm, gs_hbm, packed, summed, grads, out, in_sems, out_sems
):
    cells = CELLS // 2
    rows = cells * CH
    loads = []
    for half in range(2):
        for part in range(2):
            here = pl.ds(part * rows, rows)
            loads.append(
                pltpu.make_async_copy(
                    packed_hbm.at[half, here], packed.at[half, here], in_sems.at[2 * half + part]
                )
            )
    loads.append(pltpu.make_async_copy(sum_hbm, summed, in_sems.at[4]))
    for load in loads[4:] + loads[:4]:
        load.start()
    stores = []
    loads[4].wait()
    folded = jnp.concatenate([summed[0], summed[1]], axis=0)
    for i, target in enumerate((gc_hbm, gd_hbm, gs_hbm)):
        for g in range(4):
            grads[i, 8 * g : 8 * g + 8] = folded[8 * i : 8 * i + 8, CH * g : CH * g + CH]
        store = pltpu.make_async_copy(grads.at[i], target, out_sems.at[4 + i])
        store.start()
        stores.append(store)
    for half in range(2):
        for part in range(2):
            loads[2 * half + part].wait()
            values = packed[half, part * rows : (part + 1) * rows]
            there = slice(part * cells, (part + 1) * cells)
            for pair in range(2):
                lanes = slice(64 * pair, 64 * pair + CELLS)
                out[2 * half + pair, there] = values[:, lanes].reshape(cells, CH, CELLS)
            target = (pl.ds(2 * half, 2), pl.ds(part * cells, cells))
            store = pltpu.make_async_copy(out.at[target], out_hbm.at[target], out_sems.at[2 * half + part])
            store.start()
            stores.append(store)
    for store in stores:
        store.wait()


def shards(nx, ny, field, w_coarse, w_detail, w_skip, cotangent):
    block = (BATCH, CELLS, CH, CELLS)
    packed = pltpu.VMEM((2, CELLS * CH, 128), F32)
    hbm = pl.BlockSpec(memory_space=pl.ANY)
    weight = pltpu.VMEM((CH, CH), F32)
    small = jax.ShapeDtypeStruct((CH, CH), F32)
    peers = max(nx, ny // 2)
    half_sum = (12, 128)
    bank = bank_matrix()
    packed_field, summed = pl.pallas_call(
        functools.partial(kernel, nx, ny),
        out_shape=(
            jax.ShapeDtypeStruct((2, CELLS * CH, 128), F32),
            jax.ShapeDtypeStruct((2, *half_sum), F32),
        ),
        in_specs=[hbm] * 7,
        out_specs=(hbm, hbm),
        scratch_shapes=[
            pltpu.VMEM(block, F32),
            pltpu.VMEM(block, F32),
            packed,
            packed,
            packed,
            packed,
            packed,
            pltpu.VMEM((2, 2 * ROWS, 512), F32),
            pltpu.VMEM((4, 256, 256), F32),
            weight,
            weight,
            weight,
            pltpu.VMEM((512, 256), F32),
            pltpu.VMEM((2, 512, 256), BF16),
            pltpu.VMEM((256, 512), F32),
            pltpu.VMEM((2, 256, 512), BF16),
            pltpu.VMEM((2, 2, 2, 2 * ROWS, 128), F32),
            pltpu.VMEM((2, 2, 2 * ROWS, 128), F32),
            pltpu.VMEM((2, 2, 6 * ROWS, 128), F32),
            pltpu.VMEM((2, 2, 2 * ROWS, 128), F32),
            pltpu.VMEM((2, 2 * ROWS, 256), F32),
            packed,
            pltpu.VMEM(half_sum, F32),
            pltpu.VMEM((2, peers, *half_sum), F32),
            pltpu.VMEM((2, *half_sum), F32),
            pltpu.VMEM((2, *half_sum), F32),
            pltpu.VMEM((2, *half_sum), F32),
            pltpu.SemaphoreType.DMA((15,)),
            pltpu.SemaphoreType.DMA((3,)),
            pltpu.SemaphoreType.DMA((4, 2, 5)),
            pltpu.SemaphoreType.DMA((4, 2, 5)),
            pltpu.SemaphoreType.DMA((2, peers)),
            pltpu.SemaphoreType.DMA((2, peers)),
            pltpu.SemaphoreType.DMA((2,)),
            pltpu.SemaphoreType.DMA((2,)),
        ],
        compiler_params=pltpu.CompilerParams(
            collective_id=0, has_side_effects=True, vmem_limit_bytes=60 * 1024 * 1024
        ),
    )(
        jnp.transpose(field, (0, 1, 3, 2)),
        jnp.transpose(cotangent, (0, 1, 3, 2)),
        w_coarse,
        w_detail,
        w_skip,
        jnp.asarray(bank),
        jnp.asarray(np.ascontiguousarray(bank.T)),
    )
    grad_field, *grads = pl.pallas_call(
        unpack_kernel,
        out_shape=(jax.ShapeDtypeStruct(block, F32), small, small, small),
        in_specs=[hbm, hbm],
        out_specs=(hbm, hbm, hbm, hbm),
        scratch_shapes=[
            packed,
            pltpu.VMEM((2, *half_sum), F32),
            pltpu.VMEM((3, CH, CH), F32),
            pltpu.VMEM(block, F32),
            pltpu.SemaphoreType.DMA((5,)),
            pltpu.SemaphoreType.DMA((7,)),
        ],
        compiler_params=pltpu.CompilerParams(vmem_limit_bytes=60 * 1024 * 1024),
    )(packed_field, summed)
    return (jnp.transpose(grad_field, (0, 1, 3, 2)), *grads)


def solution(mesh):
    nx, ny = mesh.shape["gx"], mesh.shape["gy"]
    in_specs = (P(None, "gx", "gy", None), P(), P(), P(), P(None, "gx", "gy", None))
    out_specs = (P(None, "gx", "gy", None), P(), P(), P())

    def run(*args):
        return shards(nx, ny, *args)

    return jax.shard_map(run, mesh=mesh, in_specs=in_specs, out_specs=out_specs, check_vma=False)
```
